32 devices in a mesh: seq: 8 (over z, y), mp: 4 (over x, core).
Axes of the slice: x: 2, y: 2, z: 4, core: 2. Of those that a mesh axis runs over, the one named last changes fastest.
Arguments:
- queries: bfloat16 [4096, 8192], P('seq', 'mp'), may hold values from -6 to 6
- keys_in: bfloat16 [4096, 8192], P('seq', 'mp'), may hold values from -6 to 6
- values_in: bfloat16 [4096, 8192], P('seq', 'mp'), may hold values from -6 to 6
- residual: bfloat16 [4096, 8192], P('seq', 'mp')
- short_taps: bfloat16 [3, 7, 8192], P(None, None, 'mp'), may hold values from -2 to 2
- mr_filter: bfloat16 [128, 512], P('seq', 'mp'), may hold values from -0.5 to 0.5
- norm_gain: bfloat16 [8192], P('mp'), may hold values from 0.5 to 1.5
- predecessor: int32 [8], replicated, may hold values from -1 to 7, as said below
- stretch_lengths: int32 [8], replicated, may hold values from 1 to 512, as said below
Outputs:
- mixed: bfloat16 [4096, 8192], P('seq', 'mp')
- normed: bfloat16 [4096, 8192], P('seq', 'mp')
The draws below stay inside these ranges and needn't reach their ends.
Inputs may be any that keep to these rules, and one draw needn't show every extreme that they name: predecessor[j] is the stretch holding the preceding 512 tokens of stretch j's genome, or -1 for a genome's first stretch; each stretch precedes at most one stretch, and the chains have no cycles. `stretch_lengths`: every stretch that precedes another stretch is full (512 valid tokens); valid tokens come first.
All inputs are finite; a program needn't handle non-finite values.
Results may differ from the reference program's by a relative error of at most 0.0049.
Values may be sent and summed in bfloat16 or wider, within the bound.
No kernel may reach another device: no remote copies, remote signals or barrier semaphores. Data moves between devices by JAX's collectives and lax.ppermute only.
A program may use at most 64 MiB of HBM per device.

```python
import jax
import jax.numpy as jnp
from jax import lax

D = 8192
GSIZE = 16
GROUPS = 512
TAPS = 128
SHORT = 7
TOK_DEV = 512
STRETCHES = 8
TOKENS = 4096


def draw_residual(key, part):
    first, second = jax.random.split(jax.random.fold_in(key, 11), 2)
    column_scale = 10.0 ** (jnp.arange(D, dtype=jnp.float32) / D)
    row_scale = 10.0 ** jax.random.uniform(second, (TOKENS, 1), jnp.float32)
    base = jax.random.normal(first, (TOKENS, D), jnp.float32)
    return (0.3 * base * row_scale * column_scale[None, :]).astype(jnp.bfloat16)


def chain_layout(key):
    base = jax.random.fold_in(key, 7)
    first, second, third = jax.random.split(base, 3)
    rest = jax.random.permutation(first, STRETCHES - 1).astype(jnp.int32)
    target = STRETCHES // 2 - 1
    head_value = rest[0]
    rest = jnp.where(rest == target, head_value, rest)
    rest = rest.at[0].set(target).astype(jnp.int32)
    order = jnp.concatenate([jnp.full((1,), STRETCHES - 1, jnp.int32), rest])
    position = jnp.arange(STRETCHES, dtype=jnp.int32)
    coins = jax.random.randint(second, (STRETCHES,), 0, 4) == 0
    starts = (position == 0) | coins & (position != 1)
    before = jnp.concatenate([jnp.zeros((1,), jnp.int32), order[:-1]])
    pred_pos = jnp.where(starts, -1, before).astype(jnp.int32)
    last = jnp.concatenate([starts[1:], jnp.ones((1,), bool)])
    ragged = jax.random.randint(third, (STRETCHES,), 1, TOK_DEV + 1)
    length_pos = jnp.where(last, ragged, TOK_DEV).astype(jnp.int32)
    pred_out = jnp.zeros((STRETCHES,), jnp.int32).at[order].set(pred_pos)
    length_out = jnp.zeros((STRETCHES,), jnp.int32).at[order].set(length_pos)
    return (pred_out, length_out)


def draw_predecessor(key, part):
    return chain_layout(key)[0]


def draw_stretch_lengths(key, part):
    return chain_layout(key)[1]


def shard_levels(rng, extent, shards, low, top_value):
    level, own = 1.0, jax.random.fold_in(rng, 6)
    for dim, parts in shards:
        steps = jnp.exp(jax.random.uniform(jax.random.fold_in(own, dim), (parts,), jnp.float32, low / len(shards), top_value / len(shards)))
        level = level * jnp.repeat(steps, extent[dim] // parts).reshape([-1 if axis == dim else 1 for axis in range(len(extent))])
    return level


def noise(stream_key, shape, scale, reach, cuts=(), kind=jnp.bfloat16):
    array = jax.random.normal(stream_key, shape, jnp.float32) * scale
    if len(cuts) > 0:
        array = shard_levels(stream_key, shape, cuts, -0.22, 0.18) * array
    return jnp.clip(array, min=-reach, max=reach).astype(kind)


def setup_inputs(seed: int = 0) -> dict:
    seeds = jax.random.split(jax.random.key(seed), 10)
    queries = noise(seeds[0], (TOKENS, D), 1.0, 6.0, ((0, 8), (1, 4)))
    keys_in = noise(seeds[1], (TOKENS, D), 1.0, 6.0, ((0, 8), (1, 4)))
    values_in = noise(seeds[2], (TOKENS, D), 1.0, 6.0, ((0, 8), (1, 4)))
    residual = draw_residual(jax.random.fold_in(seeds[9], 71), 0)
    short_taps = noise(seeds[4], (3, SHORT, D), SHORT ** -0.5, 2.0, ((2, 4),))
    mr_filter = noise(seeds[5], (TAPS, GROUPS), TAPS ** -0.5, 0.5, ((0, 8), (1, 4)))
    norm_gain = jnp.clip(1.0 + 0.1 * jax.random.normal(seeds[6], (D,), jnp.float32), 0.5, 1.5).astype(jnp.bfloat16)
    predecessor = draw_predecessor(jax.random.fold_in(seeds[9], 71), 0)
    stretch_lengths = draw_stretch_lengths(jax.random.fold_in(seeds[9], 71), 0)
    return dict(queries=queries, keys_in=keys_in, values_in=values_in, residual=residual, short_taps=short_taps, mr_filter=mr_filter, norm_gain=norm_gain, predecessor=predecessor, stretch_lengths=stretch_lengths)


EPSILON = 1e-06

def featurize(extended, taps):
    length = extended.shape[0] - 8
    total = jnp.zeros((length, extended.shape[1]), jnp.float32)
    for offset in range(taps.shape[0]):
        total = total + taps[offset].astype(jnp.float32) * extended[8 - offset:8 - offset + length].astype(jnp.float32)
    return total

def toeplitz_blocks(filter_rows):
    tap_count = filter_rows.shape[0]
    group_count = filter_rows.shape[1]
    flipped = filter_rows[::-1].T
    pattern = jnp.concatenate([jnp.zeros((group_count, 1), filter_rows.dtype), flipped, jnp.zeros((group_count, tap_count), filter_rows.dtype)], axis=1)
    tiled = jnp.tile(pattern, (1, tap_count))[:, :2 * tap_count * tap_count]
    return tiled.reshape(group_count, tap_count, 2 * tap_count)

def long_conv(extended, filter_rows, group_size):
    tap_count = filter_rows.shape[0]
    length = extended.shape[0] - tap_count
    blocks = length // tap_count
    channels = extended.shape[1]
    pieces = extended.reshape(blocks + 1, tap_count, channels)
    windows = jnp.concatenate([pieces[:-1], pieces[1:]], axis=1).reshape(blocks, 2 * tap_count, channels // group_size, group_size)
    matrices = toeplitz_blocks(filter_rows)
    result = jnp.einsum('gij,bjgc->bigc', matrices.astype(jnp.float32), windows.astype(jnp.float32))
    return result.reshape(length, channels)

def tail_of(stretched, source, count):
    present = source >= 0
    clipped = jnp.clip(source, 0, STRETCHES - 1).astype(jnp.int32)
    whole = lax.dynamic_index_in_dim(stretched, clipped, 0, keepdims=False)
    tail = whole[whole.shape[0] - count:]
    return jnp.where(present, tail, jnp.zeros_like(tail))

def reference(queries, keys_in, values_in, residual, short_taps, mr_filter, norm_gain, predecessor, stretch_lengths):
    stretch_query = queries.reshape(STRETCHES, TOK_DEV, D)
    stretch_key = keys_in.reshape(STRETCHES, TOK_DEV, D)
    stretch_value = values_in.reshape(STRETCHES, TOK_DEV, D)
    stretch_resid = residual.reshape(STRETCHES, TOK_DEV, D)

    def first_pass(index):
        source = predecessor[index]
        key_ext = jnp.concatenate([tail_of(stretch_key, source, 8), lax.dynamic_index_in_dim(stretch_key, index, 0, keepdims=False)])
        value_ext = jnp.concatenate([tail_of(stretch_value, source, 8), lax.dynamic_index_in_dim(stretch_value, index, 0, keepdims=False)])
        return (featurize(key_ext, short_taps[1]) * featurize(value_ext, short_taps[2])).astype(jnp.bfloat16)
    indices = jnp.arange(STRETCHES, dtype=jnp.int32)
    mixed_all = lax.map(first_pass, indices)

    def second_pass(index):
        source = predecessor[index]
        query_ext = jnp.concatenate([tail_of(stretch_query, source, 8), lax.dynamic_index_in_dim(stretch_query, index, 0, keepdims=False)])
        query_feat = featurize(query_ext, short_taps[0])
        extended = jnp.concatenate([tail_of(mixed_all, source, TAPS), lax.dynamic_index_in_dim(mixed_all, index, 0, keepdims=False)])
        filtered = long_conv(extended, mr_filter, GSIZE)
        valid = (jnp.arange(TOK_DEV, dtype=jnp.int32) < stretch_lengths[index])[:, None]
        mixed = jnp.where(valid, query_feat * filtered, 0.0).astype(jnp.bfloat16)
        summed = lax.dynamic_index_in_dim(stretch_resid, index, 0, keepdims=False).astype(jnp.float32) + mixed.astype(jnp.float32)
        total = lax.optimization_barrier(jnp.sum(summed * summed, axis=1))
        scale_rows = lax.rsqrt(total / D + EPSILON)
        normed = jnp.where(valid, summed * scale_rows[:, None] * norm_gain.astype(jnp.float32), 0.0).astype(jnp.bfloat16)
        return (mixed, normed)
    mixed_out, normed_out = lax.map(second_pass, indices)
    return (mixed_out.reshape(TOKENS, D), normed_out.reshape(TOKENS, D))
```

```python
import functools

import jax
import jax.numpy as jnp
from jax import lax
from jax.experimental import pallas as pl
from jax.experimental.pallas import tpu as pltpu
from jax.sharding import PartitionSpec as P

EPSILON = 1e-06
F32 = jnp.float32
BF16 = jnp.bfloat16
LANES = 128
STEP = 256
BLOCK = 64
WINDOW = 256
PACKED = 160
OPENING = 144
VMEM_LIMIT = 48 * 1024 * 1024


def params():
    return pltpu.CompilerParams(vmem_limit_bytes=VMEM_LIMIT)


def cost(flops, bytes_accessed):
    return pl.CostEstimate(flops=flops, bytes_accessed=bytes_accessed, transcendentals=0)


def short_conv(scratch, taps, start, rows):
    total = None
    for offset in range(taps.shape[0]):
        term = taps[offset : offset + 1] * scratch[pl.ds(start + 8 - offset, rows), :]
        total = term if total is None else total + term
    return total


def tail_kernel(width_taps, q_ref, k_ref, v_ref, kb_ref, vb_ref, taps_ref, filt_ref, out_ref, ks, vs):
    taps = taps_ref[...].astype(F32)
    pieces = []
    for lane in range(0, STEP, LANES):
        cols = slice(lane, lane + LANES)
        ks[0:16, :] = kb_ref[:, cols].astype(F32)
        vs[0:16, :] = vb_ref[:, cols].astype(F32)
        ks[16:144, :] = k_ref[:, cols].astype(F32)
        vs[16:144, :] = v_ref[:, cols].astype(F32)
        for row in range(0, 128, 64):
            key = short_conv(ks, taps[1, :, cols], row + 8, 64)
            value = short_conv(vs, taps[2, :, cols], row + 8, 64)
            out_ref[0, row : row + 64, cols] = (key * value).astype(BF16)
        last = [q_ref[:, cols].astype(F32)[8:], ks[136:144, :], vs[136:144, :]]
        if filt_ref is None:
            last.append(jnp.zeros((8, LANES), F32))
        else:
            first = lane // LANES * 8
            last.append(filt_ref[...].astype(F32)[first : first + 8])
        pieces.append(jnp.concatenate(last))
    out_ref[0, 128:160, :] = jnp.concatenate(pieces, axis=1).astype(BF16)


def tail_call(queries, keys_in, values_in, short_taps, mr_filter):
    rows, width = queries.shape
    steps = width // STEP
    packed = mr_filter is not None
    in_specs = [
        pl.BlockSpec((16, STEP), lambda p: (rows // 16 - 1, p)),
        pl.BlockSpec((128, STEP), lambda p: (rows // 128 - 1, p)),
        pl.BlockSpec((128, STEP), lambda p: (rows // 128 - 1, p)),
        pl.BlockSpec((16, STEP), lambda p: (rows // 16 - 9, p)),
        pl.BlockSpec((16, STEP), lambda p: (rows // 16 - 9, p)),
        pl.BlockSpec((3, 7, STEP), lambda p: (0, 0, p)),
    ]
    operands = [queries, keys_in, values_in, keys_in, values_in, short_taps]
    body = functools.partial(tail_kernel, 7)
    if packed:
        in_specs.append(pl.BlockSpec((16, LANES), lambda p: (0, 0)))
        operands.append(mr_filter)
    else:
        body = lambda *refs: tail_kernel(7, *refs[:6], None, *refs[6:])
    return pl.pallas_call(
        body,
        grid=(steps,),
        in_specs=in_specs,
        out_specs=pl.BlockSpec((1, PACKED, STEP), lambda p: (p, 0, 0)),
        out_shape=jax.ShapeDtypeStruct((steps, PACKED, STEP), BF16),
        scratch_shapes=[pltpu.VMEM((144, LANES), F32), pltpu.VMEM((144, LANES), F32)],
        compiler_params=params(),
        cost_estimate=cost(128 * width * 30, 128 * width * 6),
        name="tail",
    )(*operands)


def feature_kernel(k_ref, v_ref, taps_ref, out_ref, ks, vs):
    rows = k_ref.shape[0]
    taps = taps_ref[...].astype(F32)
    for lane in range(0, STEP, LANES):
        cols = slice(lane, lane + LANES)
        ks[0:8, :] = jnp.zeros((8, LANES), F32)
        vs[0:8, :] = jnp.zeros((8, LANES), F32)
        ks[8 : rows + 8, :] = k_ref[:, cols].astype(F32)
        vs[8 : rows + 8, :] = v_ref[:, cols].astype(F32)
        for row in range(0, rows, 64):
            key = short_conv(ks, taps[1, :, cols], row, 64)
            value = short_conv(vs, taps[2, :, cols], row, 64)
            out_ref[row : row + 64, cols] = (key * value).astype(BF16)


def feature_call(keys_in, values_in, short_taps):
    rows, width = keys_in.shape
    block = pl.BlockSpec((rows, STEP), lambda p: (0, p))
    return pl.pallas_call(
        feature_kernel,
        grid=(width // STEP,),
        in_specs=[block, block, pl.BlockSpec((3, 7, STEP), lambda p: (0, 0, p))],
        out_specs=block,
        out_shape=jax.ShapeDtypeStruct((rows, width), BF16),
        scratch_shapes=[pltpu.VMEM((rows + 8, LANES), F32), pltpu.VMEM((rows + 8, LANES), F32)],
        compiler_params=params(),
        cost_estimate=cost(rows * width * 30, rows * width * 6),
        name="features",
    )(keys_in, values_in, short_taps)


def route_kernel(pred_ref, in_ref, out_ref, filt_ref):
    for j in range(in_ref.shape[0]):
        out_ref[j] = in_ref[jnp.maximum(pred_ref[j], 0)]
        last = in_ref[j, 144:160, :].astype(F32)[8:]
        filt_ref[16 * j : 16 * j + 16, :] = jnp.concatenate([last[:, :LANES], last[:, LANES:]]).astype(BF16)


def route_call(predecessor, received):
    count = received.shape[0]
    return pl.pallas_call(
        route_kernel,
        in_specs=[pl.BlockSpec(memory_space=pltpu.SMEM), pl.BlockSpec(memory_space=pltpu.VMEM)],
        out_specs=[pl.BlockSpec(memory_space=pltpu.VMEM)] * 2,
        out_shape=[
            jax.ShapeDtypeStruct(received.shape, BF16),
            jax.ShapeDtypeStruct((16 * count, LANES), BF16),
        ],
        compiler_params=params(),
        name="route",
    )(predecessor, received)


def pick_groups(result, group_size, rows=BLOCK):
    shape = (rows, result.shape[1])
    group = (lax.broadcasted_iota(jnp.int32, shape, 1) & (LANES - 1)) // group_size
    picked = result[:rows]
    for g in range(1, LANES // group_size):
        picked = jnp.where(group == g, result[g * rows : (g + 1) * rows], picked)
    return picked


def main_kernel(group_size, len_ref, q_ref, u_ref, res_ref, taps_ref, filt_ref, mixed_ref, toep_ref, sum_ref, qs, spread, acc):
    step = pl.program_id(0)
    rows = q_ref.shape[0]
    per_lane = LANES // group_size
    per_step = STEP // group_size
    length = len_ref[lax.axis_index("seq")]

    @pl.when(step == 0)
    def _():
        tap_count = filt_ref.shape[0]
        tap = lax.broadcasted_iota(jnp.int32, (tap_count, WINDOW), 0)
        place = lax.broadcasted_iota(jnp.int32, (tap_count, WINDOW), 1)
        onehot = (place == WINDOW - BLOCK - tap).astype(BF16)
        spread[...] = lax.dot_general(
            filt_ref[...], onehot, (((0,), (0,)), ((), ())), preferred_element_type=F32
        )
        acc[...] = jnp.zeros_like(acc)

    taps = taps_ref[...].astype(F32)
    mixed_ref[0:128, :] = jnp.zeros((128, STEP), BF16)
    base = pl.multiple_of(step * per_step, per_step)
    line_block = spread[pl.ds(base, per_step), :]
    for g in range(per_step):
        line = jnp.broadcast_to(line_block[g : g + 1], (BLOCK, WINDOW))
        toep_ref[g * BLOCK : (g + 1) * BLOCK, :] = pltpu.roll(line, 0, 1, stride=1, stride_axis=0).astype(BF16)
    for tile in range(STEP // LANES):
        cols = slice(tile * LANES, (tile + 1) * LANES)
        qs[0:8, :] = jnp.zeros((8, LANES), F32)
        qs[8 : rows + 8, :] = q_ref[:, cols].astype(F32)
        matrix = toep_ref[tile * per_lane * BLOCK : (tile + 1) * per_lane * BLOCK, :]
        for start in range(128, rows, 2 * BLOCK):
            windows = []
            for first in (start, start + BLOCK):
                low = first + BLOCK - WINDOW
                if low < 0:
                    windows.append(
                        jnp.concatenate([jnp.zeros((-low, LANES), BF16), u_ref[0 : first + BLOCK, cols]])
                    )
                else:
                    windows.append(u_ref[low : first + BLOCK, cols])
            result = jnp.dot(matrix, jnp.concatenate(windows, axis=1), preferred_element_type=F32)
            picked = pick_groups(result, group_size)
            for half in range(2):
                first = start + half * BLOCK
                filtered = picked[:, half * LANES : (half + 1) * LANES]
                query = short_conv(qs, taps[0, :, cols], first, BLOCK)
                row = lax.broadcasted_iota(jnp.int32, (BLOCK, LANES), 0) + first
                mixed = jnp.where(row < length, query * filtered, 0.0).astype(BF16)
                mixed_ref[first : first + BLOCK, cols] = mixed
                summed = res_ref[first : first + BLOCK, cols].astype(F32) + mixed.astype(F32)
                acc[first - 128 : first - 128 + BLOCK, :] += summed * summed

    @pl.when(step == pl.num_programs(0) - 1)
    def _():
        sum_ref[...] = jnp.sum(acc[...].T, axis=0, keepdims=True)


def main_call(group_size, stretch_lengths, queries, mixed_in, residual, short_taps, filter_rows):
    rows, width = queries.shape
    per_step = STEP // group_size
    groups = filter_rows.shape[1]
    block = pl.BlockSpec((rows, STEP), lambda p, *_: (0, p))
    return pl.pallas_call(
        functools.partial(main_kernel, group_size),
        grid_spec=pltpu.PrefetchScalarGridSpec(
            num_scalar_prefetch=1,
            grid=(width // STEP,),
            in_specs=[
                block,
                block,
                block,
                pl.BlockSpec((3, 7, STEP), lambda p, *_: (0, 0, p)),
                pl.BlockSpec(filter_rows.shape, lambda p, *_: (0, 0)),
            ],
            out_specs=[
                block,
                pl.BlockSpec((per_step * BLOCK, WINDOW), lambda p, *_: (p, 0)),
                pl.BlockSpec((1, rows - 128), lambda p, *_: (0, 0)),
            ],
            scratch_shapes=[
                pltpu.VMEM((rows + 8, LANES), F32),
                pltpu.VMEM((groups, WINDOW), F32),
                pltpu.VMEM((rows - 128, LANES), F32),
            ],
        ),
        out_shape=[
            jax.ShapeDtypeStruct((rows, width), BF16),
            jax.ShapeDtypeStruct((groups * BLOCK, WINDOW), BF16),
            jax.ShapeDtypeStruct((1, rows - 128), F32),
        ],
        compiler_params=params(),
        cost_estimate=cost(rows * width * 2 * WINDOW * 8, rows * width * 12),
        name="conv",
    )(stretch_lengths, queries, mixed_in, residual, short_taps, filter_rows)


def head_kernel(group_size, pred_ref, len_ref, prev_ref, q_ref, k_ref, v_ref, u_ref, res_ref, taps_ref, toep_ref, part_ref, kept_ref, mixed_ref, sum_ref, qs, ks, vs, acc):
    del kept_ref
    step = pl.program_id(0)
    per_lane = LANES // group_size
    device = lax.axis_index("seq")
    length = len_ref[device]
    follows = pred_ref[device] >= 0

    @pl.when(step == 0)
    def _():
        acc[...] = jnp.zeros_like(acc)

    taps = taps_ref[...].astype(F32)
    for tile in range(STEP // LANES):
        cols = slice(tile * LANES, (tile + 1) * LANES)
        prev = jnp.where(follows, prev_ref[0, 128:160, cols].astype(F32), 0.0)
        qs[0:8, :] = prev[0:8]
        ks[0:8, :] = prev[8:16]
        vs[0:8, :] = prev[16:24]
        qs[8 : OPENING + 8, :] = q_ref[:, cols].astype(F32)
        ks[8:24, :] = k_ref[:, cols].astype(F32)
        vs[8:24, :] = v_ref[:, cols].astype(F32)
        key = short_conv(ks, taps[1, :, cols], 0, 16)
        value = short_conv(vs, taps[2, :, cols], 0, 16)
        opening = (key * value).astype(BF16)
        state = prev_ref[0, 0:128, cols]
        state = jnp.where(follows, state, jnp.zeros_like(state))
        extended = jnp.concatenate([jnp.zeros((64, LANES), BF16), state, opening, u_ref[16:192, cols]])
        windows = jnp.concatenate([extended[0:WINDOW], extended[BLOCK : BLOCK + WINDOW]], axis=1)
        matrix = toep_ref[tile * per_lane * BLOCK : (tile + 1) * per_lane * BLOCK, :]
        result = jnp.dot(matrix, windows, preferred_element_type=F32)
        picked = pick_groups(result, group_size)
        edge = OPENING - 2 * BLOCK
        edge_matrix = jnp.concatenate([matrix[g * BLOCK : g * BLOCK + edge] for g in range(per_lane)])
        edge_result = jnp.dot(edge_matrix, extended[2 * BLOCK : 2 * BLOCK + WINDOW], preferred_element_type=F32)
        parts = [
            (0, BLOCK, picked[:, :LANES]),
            (BLOCK, BLOCK, picked[:, LANES:]),
            (2 * BLOCK, edge, pick_groups(edge_result, group_size, edge)),
        ]
        for first, rows, filtered in parts:
            query = short_conv(qs, taps[0, :, cols], first, rows)
            row = lax.broadcasted_iota(jnp.int32, (rows, LANES), 0) + first
            mixed = jnp.where(row < length, query * filtered, 0.0).astype(BF16)
            mixed_ref[first : first + rows, cols] = mixed
            summed = res_ref[first : first + rows, cols].astype(F32) + mixed.astype(F32)
            acc[first : first + rows, :] += summed * summed

    @pl.when(step == pl.num_programs(0) - 1)
    def _():
        opening_sum = jnp.sum(acc[...].T, axis=0, keepdims=True)
        lane = lax.broadcasted_iota(jnp.int32, (1, LANES), 1)
        edge_sum = jnp.where(lane < OPENING - LANES, opening_sum[:, LANES:], part_ref[:, :LANES])
        sum_ref[...] = jnp.concatenate([opening_sum[:, :LANES], edge_sum, part_ref[:, LANES:]], axis=1)


def head_call(group_size, predecessor, stretch_lengths, previous, queries, keys_in, values_in, mixed_in, residual, short_taps, toeplitz, partial_sum, mixed):
    rows, width = queries.shape
    per_step = STEP // group_size
    block = pl.BlockSpec((OPENING, STEP), lambda p, *_: (0, p))
    small = pl.BlockSpec((16, STEP), lambda p, *_: (0, p))
    return pl.pallas_call(
        functools.partial(head_kernel, group_size),
        grid_spec=pltpu.PrefetchScalarGridSpec(
            num_scalar_prefetch=2,
            grid=(width // STEP,),
            in_specs=[
                pl.BlockSpec((1, PACKED, STEP), lambda p, *_: (p, 0, 0)),
                block,
                small,
                small,
                pl.BlockSpec((192, STEP), lambda p, *_: (0, p)),
                block,
                pl.BlockSpec((3, 7, STEP), lambda p, *_: (0, 0, p)),
                pl.BlockSpec((per_step * BLOCK, WINDOW), lambda p, *_: (p, 0)),
                pl.BlockSpec(partial_sum.shape, lambda p, *_: (0, 0)),
                pl.BlockSpec(memory_space=pl.ANY),
            ],
            out_specs=[block, pl.BlockSpec((1, rows), lambda p, *_: (0, 0))],
            scratch_shapes=[
                pltpu.VMEM((OPENING + 8, LANES), F32),
                pltpu.VMEM((24, LANES), F32),
                pltpu.VMEM((24, LANES), F32),
                pltpu.VMEM((256, LANES), F32),
            ],
        ),
        out_shape=[
            jax.ShapeDtypeStruct((rows, width), BF16),
            jax.ShapeDtypeStruct((1, rows), F32),
        ],
        input_output_aliases={11: 0},
        compiler_params=params(),
        cost_estimate=cost(128 * width * 2 * WINDOW * 8, 128 * width * 12),
        name="head",
    )(predecessor, stretch_lengths, previous, queries, keys_in, values_in, mixed_in, residual, short_taps, toeplitz, partial_sum, mixed)


def norm_kernel(channels, rows, len_ref, sum_ref, mixed_ref, res_ref, gain_ref, out_ref):
    first = pl.program_id(0) * rows
    length = len_ref[lax.axis_index("seq")]
    scale_line = lax.rsqrt(sum_ref[...] / channels + EPSILON)
    scale = jnp.broadcast_to(scale_line, (LANES, rows)).T
    row = lax.broadcasted_iota(jnp.int32, (rows, LANES), 0) + first
    scale = jnp.where(row < length, scale, 0.0)
    valid = row < length
    for lane in range(0, mixed_ref.shape[1], LANES):
        cols = slice(lane, lane + LANES)
        gain = gain_ref[:, cols].astype(F32)
        summed = res_ref[:, cols].astype(F32) + mixed_ref[:, cols].astype(F32)
        out_ref[:, cols] = jnp.where(valid, summed * scale * gain, 0.0).astype(BF16)


def norm_call(channels, stretch_lengths, total, mixed, residual, norm_gain):
    rows, width = mixed.shape
    block = pl.BlockSpec((128, width), lambda p, *_: (p, 0))
    return pl.pallas_call(
        functools.partial(norm_kernel, channels, 128),
        grid_spec=pltpu.PrefetchScalarGridSpec(
            num_scalar_prefetch=1,
            grid=(rows // 128,),
            in_specs=[
                pl.BlockSpec((1, 128), lambda p, *_: (0, p)),
                block,
                block,
                pl.BlockSpec((1, width), lambda p, *_: (0, 0)),
            ],
            out_specs=block,
        ),
        out_shape=jax.ShapeDtypeStruct((rows, width), BF16),
        compiler_params=params(),
        cost_estimate=cost(rows * width * 6, rows * width * 6),
        name="norm",
    )(stretch_lengths, total, mixed, residual, norm_gain.reshape(1, width))


def exchange(pieces):
    return lax.all_to_all(pieces, "seq", split_axis=0, concat_axis=0, tiled=True)


def body(queries, keys_in, values_in, residual, short_taps, mr_filter, norm_gain, predecessor, stretch_lengths):
    rows, width = queries.shape
    count = lax.axis_size("seq")
    parts = lax.axis_size("mp")
    group_size = width // mr_filter.shape[1]
    two_phase = width // STEP == count and mr_filter.shape == (16, LANES)
    if two_phase:
        packed = tail_call(queries, keys_in, values_in, short_taps, mr_filter)
        received = exchange(packed)
        mixed_in = feature_call(keys_in, values_in, short_taps)
        routed, filter_rows = route_call(predecessor, received)
        previous = exchange(routed)
    else:
        packed = tail_call(queries, keys_in, values_in, short_taps, None)
        gathered = lax.all_gather(packed[None], "seq", axis=0, tiled=True)
        source = jnp.clip(predecessor[lax.axis_index("seq")], 0, count - 1)
        previous = lax.dynamic_index_in_dim(gathered, source, 0, keepdims=False)
        filter_rows = lax.all_gather(mr_filter, "seq", axis=0, tiled=True)
        mixed_in = feature_call(keys_in, values_in, short_taps)
    mixed, toeplitz, partial_sum = main_call(
        group_size, stretch_lengths, queries, mixed_in, residual, short_taps, filter_rows
    )
    mixed, squares = head_call(
        group_size, predecessor, stretch_lengths, previous, queries, keys_in, values_in, mixed_in,
        residual, short_taps, toeplitz, partial_sum, mixed,
    )
    total = lax.psum(squares, "mp")
    normed = norm_call(width * parts, stretch_lengths, total, mixed, residual, norm_gain)
    return (mixed, normed)


def solution(mesh):
    in_specs = (
        P("seq", "mp"),
        P("seq", "mp"),
        P("seq", "mp"),
        P("seq", "mp"),
        P(None, None, "mp"),
        P("seq", "mp"),
        P("mp"),
        P(),
        P(),
    )
    out_specs = (P("seq", "mp"), P("seq", "mp"))
    return jax.shard_map(body, mesh=mesh, in_specs=in_specs, out_specs=out_specs, check_vma=False)
```

```python
import functools

import jax
import jax.numpy as jnp
from jax import lax
from jax.experimental import pallas as pl
from jax.experimental.pallas import tpu as pltpu
from jax.sharding import PartitionSpec as P

EPSILON = 1e-06
F32 = jnp.float32
BF16 = jnp.bfloat16
LANES = 128
STEP = 256
WIDE = 512
BLOCK = 64
WINDOW = 256
PACKED = 160
OPENING = 144
VMEM_LIMIT = 60 * 1024 * 1024


def params():
    return pltpu.CompilerParams(vmem_limit_bytes=VMEM_LIMIT)


def cost(flops, bytes_accessed):
    return pl.CostEstimate(flops=flops, bytes_accessed=bytes_accessed, transcendentals=0)


def short_conv(scratch, taps, start, rows):
    total = None
    for offset in range(taps.shape[0]):
        term = taps[offset : offset + 1] * scratch[pl.ds(start + 8 - offset, rows), :]
        total = term if total is None else total + term
    return total


def tail_kernel(slots, swapped, packed, q_ref, k_ref, v_ref, kb_ref, vb_ref, taps_ref, filt_ref, *rest):
    outs, (held, ks, vs) = rest[:slots], rest[slots:]
    device = lax.axis_index("seq")

    def piece(slot, carry):
        first = (jnp.bitwise_xor(slot, device) if swapped else slot) * STEP
        lasts = []
        for tile in range(STEP // LANES):
            cols = pl.ds(pl.multiple_of(first + tile * LANES, LANES), LANES)
            here = slice(tile * LANES, (tile + 1) * LANES)
            kt, vt = ks.at[tile], vs.at[tile]
            kt[0:16, :] = kb_ref[:, cols].astype(F32)
            vt[0:16, :] = vb_ref[:, cols].astype(F32)
            kt[16:144, :] = k_ref[:, cols].astype(F32)
            vt[16:144, :] = v_ref[:, cols].astype(F32)
            key_taps = taps_ref[1, :, cols].astype(F32)
            value_taps = taps_ref[2, :, cols].astype(F32)
            for row in range(0, 128, 64):
                key = short_conv(kt, key_taps, row + 8, 64)
                value = short_conv(vt, value_taps, row + 8, 64)
                held[slot, row : row + 64, here] = (key * value).astype(BF16)
            last = [q_ref[:, cols].astype(F32)[8:], kt[136:144, :], vt[136:144, :]]
            if packed:
                last.append(filt_ref[...].astype(F32)[8 * tile : 8 * tile + 8])
            else:
                last.append(jnp.zeros((8, LANES), F32))
            lasts.append(jnp.concatenate(last))
        held[slot, 128:PACKED, :] = jnp.concatenate(lasts, axis=1).astype(BF16)
        return carry

    lax.fori_loop(0, slots, piece, 0)
    for slot in range(slots):
        outs[slot][...] = held[slot]


def tail_call(swapped, packed, queries, keys_in, values_in, short_taps, mr_filter):
    rows, width = queries.shape
    slots = width // STEP
    return pl.pallas_call(
        functools.partial(tail_kernel, slots, swapped, packed),
        grid=(1,),
        in_specs=[
            pl.BlockSpec((16, width), lambda p: (rows // 16 - 1, 0)),
            pl.BlockSpec((128, width), lambda p: (rows // 128 - 1, 0)),
            pl.BlockSpec((128, width), lambda p: (rows // 128 - 1, 0)),
            pl.BlockSpec((16, width), lambda p: (rows // 16 - 9, 0)),
            pl.BlockSpec((16, width), lambda p: (rows // 16 - 9, 0)),
            pl.BlockSpec(short_taps.shape, lambda p: (0, 0, 0)),
            pl.BlockSpec(mr_filter.shape, lambda p: (0, 0)),
        ],
        out_specs=[pl.BlockSpec((PACKED, STEP), lambda p: (0, 0))] * slots,
        out_shape=[jax.ShapeDtypeStruct((PACKED, STEP), BF16)] * slots,
        scratch_shapes=[
            pltpu.VMEM((slots, PACKED, STEP), BF16),
            pltpu.VMEM((2, 144, LANES), F32),
            pltpu.VMEM((2, 144, LANES), F32),
        ],
        compiler_params=params(),
        cost_estimate=cost(128 * width * 30, 128 * width * 6),
        name="tail",
    )(queries, keys_in, values_in, keys_in, values_in, short_taps, mr_filter)


def feature_kernel(k_ref, v_ref, taps_ref, out_ref, ks, vs):
    rows = k_ref.shape[0]

    def pair(index, carry):
        for tile in range(2):
            cols = pl.ds(pl.multiple_of(index * 2 * LANES + tile * LANES, LANES), LANES)
            kt, vt = ks.at[tile], vs.at[tile]
            kt[0:8, :] = jnp.zeros((8, LANES), F32)
            vt[0:8, :] = jnp.zeros((8, LANES), F32)
            kt[8 : rows + 8, :] = k_ref[:, cols].astype(F32)
            vt[8 : rows + 8, :] = v_ref[:, cols].astype(F32)
            key_taps = taps_ref[1, :, cols].astype(F32)
            value_taps = taps_ref[2, :, cols].astype(F32)
            for row in range(0, rows, 64):
                key = short_conv(kt, key_taps, row, 64)
                value = short_conv(vt, value_taps, row, 64)
                out_ref[row : row + 64, cols] = (key * value).astype(BF16)
        return carry

    lax.fori_loop(0, k_ref.shape[1] // (2 * LANES), pair, 0)


def feature_call(keys_in, values_in, short_taps):
    rows, width = keys_in.shape
    block = pl.BlockSpec((rows, WIDE), lambda p: (0, p))
    return pl.pallas_call(
        feature_kernel,
        grid=(width // WIDE,),
        in_specs=[block, block, pl.BlockSpec((3, 7, WIDE), lambda p: (0, 0, p))],
        out_specs=block,
        out_shape=jax.ShapeDtypeStruct((rows, width), BF16),
        scratch_shapes=[pltpu.VMEM((2, rows + 8, LANES), F32), pltpu.VMEM((2, rows + 8, LANES), F32)],
        compiler_params=params(),
        cost_estimate=cost(rows * width * 30, rows * width * 6),
        name="features",
    )(keys_in, values_in, short_taps)


def route_kernel(count, pred_ref, *refs):
    ins, outs, (filt_ref, held) = refs[:count], refs[count : 2 * count], refs[2 * count :]
    device = lax.axis_index("seq")
    for slot in range(count):
        held[slot] = ins[slot][...]
    for slot in range(count):
        source = jnp.maximum(pred_ref[jnp.bitwise_xor(device, slot)], 0)
        outs[slot][...] = held[jnp.bitwise_xor(source, device)]
    for j in range(count):
        last = held[jnp.bitwise_xor(device, j), 144:160, :].astype(F32)[8:]
        filt_ref[16 * j : 16 * j + 16, :] = jnp.concatenate([last[:, :LANES], last[:, LANES:]]).astype(BF16)


def route_call(predecessor, received):
    count = len(received)
    piece = jax.ShapeDtypeStruct((PACKED, STEP), BF16)
    results = pl.pallas_call(
        functools.partial(route_kernel, count),
        in_specs=[pl.BlockSpec(memory_space=pltpu.SMEM)] + [pl.BlockSpec(memory_space=pltpu.VMEM)] * count,
        out_specs=[pl.BlockSpec(memory_space=pltpu.VMEM)] * (count + 1),
        out_shape=[piece] * count + [jax.ShapeDtypeStruct((16 * count, LANES), BF16)],
        scratch_shapes=[pltpu.VMEM((count, PACKED, STEP), BF16)],
        compiler_params=params(),
        name="route",
    )(predecessor, *received)
    return results[:count], results[count]


def pick_groups(result, group_size, rows=BLOCK):
    shape = (rows, result.shape[1])
    group = (lax.broadcasted_iota(jnp.int32, shape, 1) & (LANES - 1)) // group_size
    picked = result[:rows]
    for g in range(1, LANES // group_size):
        picked = jnp.where(group == g, result[g * rows : (g + 1) * rows], picked)
    return picked


def main_kernel(group_size, len_ref, q_ref, u_ref, res_ref, taps_ref, filt_ref, mixed_ref, toep_ref, sum_ref, qs, spread, acc):
    step = pl.program_id(0)
    rows = q_ref.shape[0]
    per_lane = LANES // group_size
    length = len_ref[lax.axis_index("seq")]

    @pl.when(step == 0)
    def _():
        tap_count = filt_ref.shape[0]
        tap = lax.broadcasted_iota(jnp.int32, (tap_count, WINDOW), 0)
        place = lax.broadcasted_iota(jnp.int32, (tap_count, WINDOW), 1)
        onehot = (place == WINDOW - BLOCK - tap).astype(BF16)
        spread[...] = lax.dot_general(
            filt_ref[...], onehot, (((0,), (0,)), ((), ())), preferred_element_type=F32
        )
        acc[...] = jnp.zeros_like(acc)

    mixed_ref[0:128, :] = jnp.zeros((128, WIDE), BF16)

    def pair(index, carry):
        for tile in range(2):
            number = index * 2 + tile
            cols = pl.ds(pl.multiple_of(number * LANES, LANES), LANES)
            qt = qs.at[tile]
            qt[0:8, :] = jnp.zeros((8, LANES), F32)
            qt[8 : rows + 8, :] = q_ref[:, cols].astype(F32)
            query_taps = taps_ref[0, :, cols].astype(F32)
            base = pl.multiple_of((step * (WIDE // LANES) + number) * per_lane, per_lane)
            lines = spread[pl.ds(base, per_lane), :]
            blocks = []
            for g in range(per_lane):
                line = jnp.broadcast_to(lines[g : g + 1], (BLOCK, WINDOW))
                blocks.append(pltpu.roll(line, 0, 1, stride=1, stride_axis=0).astype(BF16))
            matrix = jnp.concatenate(blocks)
            toep_ref[pl.ds(pl.multiple_of(number * per_lane * BLOCK, 16), per_lane * BLOCK), :] = matrix
            for start in range(128, rows, 2 * BLOCK):
                windows = []
                for first in (start, start + BLOCK):
                    low = first + BLOCK - WINDOW
                    if low < 0:
                        windows.append(
                            jnp.concatenate([jnp.zeros((-low, LANES), BF16), u_ref[0 : first + BLOCK, cols]])
                        )
                    else:
                        windows.append(u_ref[low : first + BLOCK, cols])
                result = jnp.dot(matrix, jnp.concatenate(windows, axis=1), preferred_element_type=F32)
                picked = pick_groups(result, group_size)
                for half in range(2):
                    first = start + half * BLOCK
                    filtered = picked[:, half * LANES : (half + 1) * LANES]
                    query = short_conv(qt, query_taps, first, BLOCK)
                    row = lax.broadcasted_iota(jnp.int32, (BLOCK, LANES), 0) + first
                    mixed = jnp.where(row < length, query * filtered, 0.0).astype(BF16)
                    mixed_ref[first : first + BLOCK, cols] = mixed
                    summed = res_ref[first : first + BLOCK, cols].astype(F32) + mixed.astype(F32)
                    acc[first - 128 : first - 128 + BLOCK, :] += summed * summed
        return carry

    lax.fori_loop(0, WIDE // (2 * LANES), pair, 0)

    @pl.when(step == pl.num_programs(0) - 1)
    def _():
        sum_ref[...] = jnp.sum(acc[...].T, axis=0, keepdims=True)


def main_call(group_size, stretch_lengths, queries, mixed_in, residual, short_taps, filter_rows):
    rows, width = queries.shape
    per_step = WIDE // group_size
    groups = filter_rows.shape[1]
    block = pl.BlockSpec((rows, WIDE), lambda p, *_: (0, p))
    return pl.pallas_call(
        functools.partial(main_kernel, group_size),
        grid_spec=pltpu.PrefetchScalarGridSpec(
            num_scalar_prefetch=1,
            grid=(width // WIDE,),
            in_specs=[
                block,
                block,
                block,
                pl.BlockSpec((3, 7, WIDE), lambda p, *_: (0, 0, p)),
                pl.BlockSpec(filter_rows.shape, lambda p, *_: (0, 0)),
            ],
            out_specs=[
                block,
                pl.BlockSpec((per_step * BLOCK, WINDOW), lambda p, *_: (p, 0)),
                pl.BlockSpec((1, rows - 128), lambda p, *_: (0, 0)),
            ],
            scratch_shapes=[
                pltpu.VMEM((2, rows + 8, LANES), F32),
                pltpu.VMEM((groups, WINDOW), F32),
                pltpu.VMEM((rows - 128, LANES), F32),
            ],
        ),
        out_shape=[
            jax.ShapeDtypeStruct((rows, width), BF16),
            jax.ShapeDtypeStruct((groups * BLOCK, WINDOW), BF16),
            jax.ShapeDtypeStruct((1, rows - 128), F32),
        ],
        compiler_params=params(),
        cost_estimate=cost(rows * width * 2 * WINDOW * 8, rows * width * 12),
        name="conv",
    )(stretch_lengths, queries, mixed_in, residual, short_taps, filter_rows)


def head_kernel(group_size, slots, swapped, pred_ref, len_ref, *refs):
    prevs, refs = refs[:slots], refs[slots:]
    q_ref, k_ref, v_ref, u_ref, res_ref, taps_ref, toep_ref, kept_ref, mixed_ref, sum_ref, held, qs, ks, vs, acc = refs
    del kept_ref
    step = pl.program_id(0)
    per_lane = LANES // group_size
    device = lax.axis_index("seq")
    length = len_ref[device]
    follows = pred_ref[device] >= 0

    @pl.when(step == 0)
    def _():
        acc[...] = jnp.zeros_like(acc)
        for slot in range(slots):
            held[slot] = prevs[slot][...]

    def pair(index, carry):
        piece = step * (WIDE // STEP) + index
        slot = jnp.bitwise_xor(piece, device) if swapped else piece
        for tile in range(2):
            number = index * 2 + tile
            cols = pl.ds(pl.multiple_of(number * LANES, LANES), LANES)
            here = slice(tile * LANES, (tile + 1) * LANES)
            qt, kt, vt = qs.at[tile], ks.at[tile], vs.at[tile]
            prev = jnp.where(follows, held[slot, 128:PACKED, here].astype(F32), 0.0)
            qt[0:8, :] = prev[0:8]
            kt[0:8, :] = prev[8:16]
            vt[0:8, :] = prev[16:24]
            qt[8 : OPENING + 8, :] = q_ref[:, cols].astype(F32)
            kt[8:24, :] = k_ref[:, cols].astype(F32)
            vt[8:24, :] = v_ref[:, cols].astype(F32)
            query_taps = taps_ref[0, :, cols].astype(F32)
            key = short_conv(kt, taps_ref[1, :, cols].astype(F32), 0, 16)
            value = short_conv(vt, taps_ref[2, :, cols].astype(F32), 0, 16)
            opening = (key * value).astype(BF16)
            state = held[slot, 0:128, here]
            state = jnp.where(follows, state, jnp.zeros_like(state))
            extended = jnp.concatenate([jnp.zeros((64, LANES), BF16), state, opening, u_ref[16:192, cols]])
            windows = jnp.concatenate([extended[0:WINDOW], extended[BLOCK : BLOCK + WINDOW]], axis=1)
            matrix = toep_ref[pl.ds(pl.multiple_of(number * per_lane * BLOCK, 16), per_lane * BLOCK), :]
            result = jnp.dot(matrix, windows, preferred_element_type=F32)
            picked = pick_groups(result, group_size)
            edge = OPENING - 2 * BLOCK
            edge_matrix = jnp.concatenate([matrix[g * BLOCK : g * BLOCK + edge] for g in range(per_lane)])
            edge_result = jnp.dot(edge_matrix, extended[2 * BLOCK : 2 * BLOCK + WINDOW], preferred_element_type=F32)
            parts = [
                (0, BLOCK, picked[:, :LANES]),
                (BLOCK, BLOCK, picked[:, LANES:]),
                (2 * BLOCK, edge, pick_groups(edge_result, group_size, edge)),
            ]
            for first, rows, filtered in parts:
                query = short_conv(qt, query_taps, first, rows)
                row = lax.broadcasted_iota(jnp.int32, (rows, LANES), 0) + first
                mixed = jnp.where(row < length, query * filtered, 0.0).astype(BF16)
                mixed_ref[first : first + rows, cols] = mixed
                summed = res_ref[first : first + rows, cols].astype(F32) + mixed.astype(F32)
                acc[first : first + rows, :] += summed * summed
        return carry

    lax.fori_loop(0, WIDE // STEP, pair, 0)

    @pl.when(step == pl.num_programs(0) - 1)
    def _():
        sum_ref[...] = jnp.sum(acc[...].T, axis=0, keepdims=True)


def head_call(group_size, swapped, predecessor, stretch_lengths, previous, queries, keys_in, values_in, mixed_in, residual, short_taps, toeplitz, mixed):
    rows, width = queries.shape
    slots = len(previous)
    per_step = WIDE // group_size
    block = pl.BlockSpec((OPENING, WIDE), lambda p, *_: (0, p))
    small = pl.BlockSpec((16, WIDE), lambda p, *_: (0, p))
    return pl.pallas_call(
        functools.partial(head_kernel, group_size, slots, swapped),
        grid_spec=pltpu.PrefetchScalarGridSpec(
            num_scalar_prefetch=2,
            grid=(width // WIDE,),
            in_specs=[pl.BlockSpec((PACKED, STEP), lambda p, *_: (0, 0))] * slots
            + [
                block,
                small,
                small,
                pl.BlockSpec((192, WIDE), lambda p, *_: (0, p)),
                block,
                pl.BlockSpec((3, 7, WIDE), lambda p, *_: (0, 0, p)),
                pl.BlockSpec((per_step * BLOCK, WINDOW), lambda p, *_: (p, 0)),
                pl.BlockSpec(memory_space=pl.ANY),
            ],
            out_specs=[block, pl.BlockSpec((1, 256), lambda p, *_: (0, 0))],
            scratch_shapes=[
                pltpu.VMEM((slots, PACKED, STEP), BF16),
                pltpu.VMEM((2, OPENING + 8, LANES), F32),
                pltpu.VMEM((2, 24, LANES), F32),
                pltpu.VMEM((2, 24, LANES), F32),
                pltpu.VMEM((256, LANES), F32),
            ],
        ),
        out_shape=[
            jax.ShapeDtypeStruct((rows, width), BF16),
            jax.ShapeDtypeStruct((1, 256), F32),
        ],
        input_output_aliases={slots + 9: 0},
        compiler_params=params(),
        cost_estimate=cost(128 * width * 2 * WINDOW * 8, 128 * width * 12),
        name="head",
    )(predecessor, stretch_lengths, *previous, queries, keys_in, values_in, mixed_in, residual, short_taps, toeplitz, mixed)


def norm_kernel(channels, first_block, sums, len_ref, *refs):
    sum_refs, (mixed_ref, res_ref, gain_ref), out_ref = refs[:sums], refs[sums : sums + 3], refs[-1]
    rows = mixed_ref.shape[0]
    first = (pl.program_id(0) + first_block) * rows
    length = len_ref[lax.axis_index("seq")]
    total = sum_refs[0][...]
    for ref in sum_refs[1:]:
        total = total + ref[...]
    scale = jnp.broadcast_to(lax.rsqrt(total / channels + EPSILON), (LANES, total.shape[1])).T[:rows]
    valid = lax.broadcasted_iota(jnp.int32, (rows, LANES), 0) + first < length
    for lane in range(0, mixed_ref.shape[1], LANES):
        cols = slice(lane, lane + LANES)
        gain = gain_ref[:, cols].astype(F32)
        summed = res_ref[:, cols].astype(F32) + mixed_ref[:, cols].astype(F32)
        out_ref[:, cols] = jnp.where(valid, summed * scale * gain, 0.0).astype(BF16)


def norm_call(channels, opening, stretch_lengths, totals, mixed, residual, norm_gain, normed=None):
    rows, width = mixed.shape
    size, first_block, steps, lanes = (OPENING, 0, 1, 256) if opening else (128, 1, rows // 128 - 1, 128)
    block = pl.BlockSpec((size, width), lambda p, *_: (p + first_block, 0))
    operands = [*totals, mixed, residual, norm_gain.reshape(1, width)]
    in_specs = [pl.BlockSpec((1, lanes), lambda p, *_: (0, p))] * len(totals)
    in_specs += [block, block, pl.BlockSpec((1, width), lambda p, *_: (0, 0))]
    aliases = {}
    if normed is not None:
        aliases = {len(operands) + 1: 0}
        operands.append(normed)
        in_specs.append(pl.BlockSpec(memory_space=pl.ANY))
    return pl.pallas_call(
        functools.partial(norm_kernel, channels, first_block, len(totals)),
        grid_spec=pltpu.PrefetchScalarGridSpec(
            num_scalar_prefetch=1, grid=(steps,), in_specs=in_specs, out_specs=block
        ),
        out_shape=jax.ShapeDtypeStruct((rows, width), BF16),
        input_output_aliases=aliases,
        compiler_params=params(),
        cost_estimate=cost(steps * size * width * 6, steps * size * width * 6),
        name="norm_opening" if opening else "norm",
    )(stretch_lengths, *operands)


def swap(array, axis, distance):
    size = lax.axis_size(axis)
    return lax.ppermute(array, axis, [(i, i ^ distance) for i in range(size)])


def shares(squares):
    parts = lax.axis_size("mp")
    if parts != 4:
        return [lax.psum(squares, "mp")]
    return [squares] + [swap(squares, "mp", k) for k in range(1, parts)]


def body(queries, keys_in, values_in, residual, short_taps, mr_filter, norm_gain, predecessor, stretch_lengths):
    rows, width = queries.shape
    count = lax.axis_size("seq")
    channels = width * lax.axis_size("mp")
    group_size = width // mr_filter.shape[1]
    two_phase = width // STEP == count == 8 and mr_filter.shape == (16, LANES)
    packed = tail_call(two_phase, two_phase, queries, keys_in, values_in, short_taps, mr_filter)
    if two_phase:
        received = [packed[0]] + [swap(packed[k], "seq", k) for k in range(1, count)]
        mixed_in = feature_call(keys_in, values_in, short_taps)
        routed, filter_rows = route_call(predecessor, received)
        previous = [routed[0]] + [swap(routed[k], "seq", k) for k in range(1, count)]
    else:
        gathered = lax.all_gather(jnp.stack(packed)[None], "seq", axis=0, tiled=True)
        source = jnp.clip(predecessor[lax.axis_index("seq")], 0, count - 1)
        chosen = lax.dynamic_index_in_dim(gathered, source, 0, keepdims=False)
        previous = [chosen[k] for k in range(len(packed))]
        filter_rows = lax.all_gather(mr_filter, "seq", axis=0, tiled=True)
        mixed_in = feature_call(keys_in, values_in, short_taps)
    mixed, toeplitz, squares = main_call(
        group_size, stretch_lengths, queries, mixed_in, residual, short_taps, filter_rows
    )
    normed = norm_call(channels, False, stretch_lengths, shares(squares), mixed, residual, norm_gain)
    mixed, squares = head_call(
        group_size, two_phase, predecessor, stretch_lengths, previous, queries, keys_in, values_in,
        mixed_in, residual, short_taps, toeplitz, mixed,
    )
    normed = norm_call(channels, True, stretch_lengths, shares(squares), mixed, residual, norm_gain, normed)
    return (mixed, normed)


def solution(mesh):
    in_specs = (
        P("seq", "mp"),
        P("seq", "mp"),
        P("seq", "mp"),
        P("seq", "mp"),
        P(None, None, "mp"),
        P("seq", "mp"),
        P("mp"),
        P(),
        P(),
    )
    out_specs = (P("seq", "mp"), P("seq", "mp"))
    return jax.shard_map(body, mesh=mesh, in_specs=in_specs, out_specs=out_specs, check_vma=False)
```

```python
import functools

import jax
import jax.numpy as jnp
from jax import lax
from jax.experimental import pallas as pl
from jax.experimental.pallas import tpu as pltpu
from jax.sharding import PartitionSpec as P

EPSILON = 1e-06
F32 = jnp.float32
BF16 = jnp.bfloat16
LANES = 128
STEP = 256
WIDE = 512
BLOCK = 64
WINDOW = 256
PACKED = 160
OPENING = 144
VMEM_LIMIT = 60 * 1024 * 1024


def params():
    return pltpu.CompilerParams(vmem_limit_bytes=VMEM_LIMIT)


def cost(flops, bytes_accessed):
    return pl.CostEstimate(flops=flops, bytes_accessed=bytes_accessed, transcendentals=0)


def short_conv(scratch, taps, start, rows):
    total = None
    for offset in range(taps.shape[0]):
        term = taps[offset : offset + 1] * scratch[pl.ds(start + 8 - offset, rows), :]
        total = term if total is None else total + term
    return total


def tail_kernel(packed, q_ref, k_ref, v_ref, kb_ref, vb_ref, taps_ref, filt_ref, out_ref, ks, vs):
    def piece(slot, carry):
        lasts = []
        for tile in range(STEP // LANES):
            cols = pl.ds(pl.multiple_of(slot * STEP + tile * LANES, LANES), LANES)
            here = slice(tile * LANES, (tile + 1) * LANES)
            kt, vt = ks.at[tile], vs.at[tile]
            kt[0:16, :] = kb_ref[:, cols].astype(F32)
            vt[0:16, :] = vb_ref[:, cols].astype(F32)
            kt[16:144, :] = k_ref[:, cols].astype(F32)
            vt[16:144, :] = v_ref[:, cols].astype(F32)
            key_taps = taps_ref[1, :, cols].astype(F32)
            value_taps = taps_ref[2, :, cols].astype(F32)
            for row in range(0, 128, 64):
                key = short_conv(kt, key_taps, row + 8, 64)
                value = short_conv(vt, value_taps, row + 8, 64)
                out_ref[slot, row : row + 64, here] = (key * value).astype(BF16)
            last = [q_ref[:, cols].astype(F32)[8:], kt[136:144, :], vt[136:144, :]]
            if packed:
                last.append(filt_ref[...].astype(F32)[8 * tile : 8 * tile + 8])
            else:
                last.append(jnp.zeros((8, LANES), F32))
            lasts.append(jnp.concatenate(last))
        out_ref[slot, 128:PACKED, :] = jnp.concatenate(lasts, axis=1).astype(BF16)
        return carry

    lax.fori_loop(0, out_ref.shape[0], piece, 0)


def tail_call(packed, queries, keys_in, values_in, short_taps, mr_filter):
    rows, width = queries.shape
    slots = width // STEP
    return pl.pallas_call(
        functools.partial(tail_kernel, packed),
        grid=(1,),
        in_specs=[
            pl.BlockSpec((16, width), lambda p: (rows // 16 - 1, 0)),
            pl.BlockSpec((128, width), lambda p: (rows // 128 - 1, 0)),
            pl.BlockSpec((128, width), lambda p: (rows // 128 - 1, 0)),
            pl.BlockSpec((16, width), lambda p: (rows // 16 - 9, 0)),
            pl.BlockSpec((16, width), lambda p: (rows // 16 - 9, 0)),
            pl.BlockSpec(short_taps.shape, lambda p: (0, 0, 0)),
            pl.BlockSpec(mr_filter.shape, lambda p: (0, 0)),
        ],
        out_specs=pl.BlockSpec((slots, PACKED, STEP), lambda p: (0, 0, 0)),
        out_shape=jax.ShapeDtypeStruct((slots, PACKED, STEP), BF16),
        scratch_shapes=[pltpu.VMEM((2, 144, LANES), F32), pltpu.VMEM((2, 144, LANES), F32)],
        compiler_params=params(),
        cost_estimate=cost(128 * width * 30, 128 * width * 6),
        name="tail",
    )(queries, keys_in, values_in, keys_in, values_in, short_taps, mr_filter)


def feature_kernel(k_ref, v_ref, taps_ref, out_ref, ks, vs):
    rows = k_ref.shape[0]

    def pair(index, carry):
        for tile in range(2):
            cols = pl.ds(pl.multiple_of(index * 2 * LANES + tile * LANES, LANES), LANES)
            kt, vt = ks.at[tile], vs.at[tile]
            kt[0:8, :] = jnp.zeros((8, LANES), F32)
            vt[0:8, :] = jnp.zeros((8, LANES), F32)
            kt[8 : rows + 8, :] = k_ref[:, cols].astype(F32)
            vt[8 : rows + 8, :] = v_ref[:, cols].astype(F32)
            key_taps = taps_ref[1, :, cols].astype(F32)
            value_taps = taps_ref[2, :, cols].astype(F32)
            for row in range(0, rows, 64):
                key = short_conv(kt, key_taps, row, 64)
                value = short_conv(vt, value_taps, row, 64)
                out_ref[row : row + 64, cols] = (key * value).astype(BF16)
        return carry

    lax.fori_loop(0, k_ref.shape[1] // (2 * LANES), pair, 0)


def feature_call(keys_in, values_in, short_taps):
    rows, width = keys_in.shape
    block = pl.BlockSpec((rows, WIDE), lambda p: (0, p))
    return pl.pallas_call(
        feature_kernel,
        grid=(width // WIDE,),
        in_specs=[block, block, pl.BlockSpec((3, 7, WIDE), lambda p: (0, 0, p))],
        out_specs=block,
        out_shape=jax.ShapeDtypeStruct((rows, width), BF16),
        scratch_shapes=[pltpu.VMEM((2, rows + 8, LANES), F32), pltpu.VMEM((2, rows + 8, LANES), F32)],
        compiler_params=params(),
        cost_estimate=cost(rows * width * 30, rows * width * 6),
        name="features",
    )(keys_in, values_in, short_taps)


def route_kernel(pred_ref, in_ref, out_ref, filt_ref):
    for j in range(in_ref.shape[0]):
        out_ref[j] = in_ref[jnp.maximum(pred_ref[j], 0)]
        last = in_ref[j, 144:160, :].astype(F32)[8:]
        filt_ref[16 * j : 16 * j + 16, :] = jnp.concatenate([last[:, :LANES], last[:, LANES:]]).astype(BF16)


def route_call(predecessor, received):
    count = received.shape[0]
    return pl.pallas_call(
        route_kernel,
        in_specs=[pl.BlockSpec(memory_space=pltpu.SMEM), pl.BlockSpec(memory_space=pltpu.VMEM)],
        out_specs=[pl.BlockSpec(memory_space=pltpu.VMEM)] * 2,
        out_shape=[
            jax.ShapeDtypeStruct(received.shape, BF16),
            jax.ShapeDtypeStruct((16 * count, LANES), BF16),
        ],
        compiler_params=params(),
        cost_estimate=cost(0, received.size * 4),
        name="route",
    )(predecessor, received)


def spread_taps(filter_rows):
    shape = (filter_rows.shape[0], WINDOW)
    tap = lax.broadcasted_iota(jnp.int32, shape, 0)
    place = lax.broadcasted_iota(jnp.int32, shape, 1)
    onehot = (place == WINDOW - BLOCK - tap).astype(BF16)
    return lax.dot_general(filter_rows, onehot, (((0,), (0,)), ((), ())), preferred_element_type=F32)


def toeplitz(lines):
    blocks = []
    for g in range(lines.shape[0]):
        line = jnp.broadcast_to(lines[g : g + 1], (BLOCK, WINDOW))
        blocks.append(pltpu.roll(line, 0, 1, stride=1, stride_axis=0).astype(BF16))
    return jnp.concatenate(blocks)


def pick_groups(result, group_size, rows=BLOCK):
    shape = (rows, result.shape[1])
    group = (lax.broadcasted_iota(jnp.int32, shape, 1) & (LANES - 1)) // group_size
    picked = result[:rows]
    for g in range(1, LANES // group_size):
        picked = jnp.where(group == g, result[g * rows : (g + 1) * rows], picked)
    return picked


def main_kernel(group_size, len_ref, q_ref, u_ref, res_ref, taps_ref, filt_ref, mixed_ref, sum_ref, lines_ref, qs, acc):
    step = pl.program_id(0)
    rows = q_ref.shape[0]
    per_lane = LANES // group_size
    length = len_ref[lax.axis_index("seq")]

    @pl.when(step == 0)
    def _():
        lines_ref[...] = spread_taps(filt_ref[...])
        acc[...] = jnp.zeros_like(acc)

    mixed_ref[0:128, :] = jnp.zeros((128, WIDE), BF16)

    def pair(index, carry):
        for tile in range(2):
            number = index * 2 + tile
            cols = pl.ds(pl.multiple_of(number * LANES, LANES), LANES)
            qt = qs.at[tile]
            qt[0:8, :] = jnp.zeros((8, LANES), F32)
            qt[8 : rows + 8, :] = q_ref[:, cols].astype(F32)
            query_taps = taps_ref[0, :, cols].astype(F32)
            base = pl.multiple_of((step * (WIDE // LANES) + number) * per_lane, per_lane)
            matrix = toeplitz(lines_ref[pl.ds(base, per_lane), :])
            for start in range(128, rows, 2 * BLOCK):
                windows = []
                for first in (start, start + BLOCK):
                    low = first + BLOCK - WINDOW
                    if low < 0:
                        windows.append(
                            jnp.concatenate([jnp.zeros((-low, LANES), BF16), u_ref[0 : first + BLOCK, cols]])
                        )
                    else:
                        windows.append(u_ref[low : first + BLOCK, cols])
                result = jnp.dot(matrix, jnp.concatenate(windows, axis=1), preferred_element_type=F32)
                picked = pick_groups(result, group_size)
                for half in range(2):
                    first = start + half * BLOCK
                    filtered = picked[:, half * LANES : (half + 1) * LANES]
                    query = short_conv(qt, query_taps, first, BLOCK)
                    row = lax.broadcasted_iota(jnp.int32, (BLOCK, LANES), 0) + first
                    mixed = jnp.where(row < length, query * filtered, 0.0).astype(BF16)
                    mixed_ref[first : first + BLOCK, cols] = mixed
                    summed = res_ref[first : first + BLOCK, cols].astype(F32) + mixed.astype(F32)
                    acc[first - 128 : first - 128 + BLOCK, :] += summed * summed
        return carry

    lax.fori_loop(0, WIDE // (2 * LANES), pair, 0)

    @pl.when(step == pl.num_programs(0) - 1)
    def _():
        sum_ref[...] = jnp.sum(acc[...].T, axis=0, keepdims=True)


def main_call(group_size, stretch_lengths, queries, mixed_in, residual, short_taps, filter_rows):
    rows, width = queries.shape
    groups = filter_rows.shape[1]
    block = pl.BlockSpec((rows, WIDE), lambda p, *_: (0, p))
    return pl.pallas_call(
        functools.partial(main_kernel, group_size),
        grid_spec=pltpu.PrefetchScalarGridSpec(
            num_scalar_prefetch=1,
            grid=(width // WIDE,),
            in_specs=[
                block,
                block,
                block,
                pl.BlockSpec((3, 7, WIDE), lambda p, *_: (0, 0, p)),
                pl.BlockSpec(filter_rows.shape, lambda p, *_: (0, 0)),
            ],
            out_specs=[
                block,
                pl.BlockSpec((1, rows - 128), lambda p, *_: (0, 0)),
                pl.BlockSpec((groups, WINDOW), lambda p, *_: (0, 0)),
            ],
            scratch_shapes=[
                pltpu.VMEM((2, rows + 8, LANES), F32),
                pltpu.VMEM((rows - 128, LANES), F32),
            ],
        ),
        out_shape=[
            jax.ShapeDtypeStruct((rows, width), BF16),
            jax.ShapeDtypeStruct((1, rows - 128), F32),
            jax.ShapeDtypeStruct((groups, WINDOW), F32),
        ],
        compiler_params=params(),
        cost_estimate=cost(rows * width * 2 * WINDOW * 8, rows * width * 12),
        name="conv",
    )(stretch_lengths, queries, mixed_in, residual, short_taps, filter_rows)


def head_kernel(group_size, pred_ref, len_ref, held, q_ref, k_ref, v_ref, u_ref, res_ref, taps_ref, lines_ref, kept_ref, mixed_ref, sum_ref, qs, ks, vs, acc):
    del kept_ref
    step = pl.program_id(0)
    per_lane = LANES // group_size
    device = lax.axis_index("seq")
    length = len_ref[device]
    follows = pred_ref[device] >= 0

    @pl.when(step == 0)
    def _():
        acc[...] = jnp.zeros_like(acc)

    def pair(index, carry):
        for tile in range(2):
            number = index * 2 + tile
            cols = pl.ds(pl.multiple_of(number * LANES, LANES), LANES)
            here = slice(tile * LANES, (tile + 1) * LANES)
            qt, kt, vt = qs.at[tile], ks.at[tile], vs.at[tile]
            prev = jnp.where(follows, held[index, 128:PACKED, here].astype(F32), 0.0)
            qt[0:8, :] = prev[0:8]
            kt[0:8, :] = prev[8:16]
            vt[0:8, :] = prev[16:24]
            qt[8 : OPENING + 8, :] = q_ref[:, cols].astype(F32)
            kt[8:24, :] = k_ref[:, cols].astype(F32)
            vt[8:24, :] = v_ref[:, cols].astype(F32)
            query_taps = taps_ref[0, :, cols].astype(F32)
            key = short_conv(kt, taps_ref[1, :, cols].astype(F32), 0, 16)
            value = short_conv(vt, taps_ref[2, :, cols].astype(F32), 0, 16)
            opening = (key * value).astype(BF16)
            state = held[index, 0:128, here]
            state = jnp.where(follows, state, jnp.zeros_like(state))
            extended = jnp.concatenate([jnp.zeros((64, LANES), BF16), state, opening, u_ref[16:192, cols]])
            windows = jnp.concatenate([extended[0:WINDOW], extended[BLOCK : BLOCK + WINDOW]], axis=1)
            base = pl.multiple_of(number * per_lane, per_lane)
            matrix = toeplitz(lines_ref[pl.ds(base, per_lane), :])
            result = jnp.dot(matrix, windows, preferred_element_type=F32)
            picked = pick_groups(result, group_size)
            edge = OPENING - 2 * BLOCK
            edge_matrix = jnp.concatenate([matrix[g * BLOCK : g * BLOCK + edge] for g in range(per_lane)])
            edge_result = jnp.dot(edge_matrix, extended[2 * BLOCK : 2 * BLOCK + WINDOW], preferred_element_type=F32)
            parts = [
                (0, BLOCK, picked[:, :LANES]),
                (BLOCK, BLOCK, picked[:, LANES:]),
                (2 * BLOCK, edge, pick_groups(edge_result, group_size, edge)),
            ]
            for first, rows, filtered in parts:
                query = short_conv(qt, query_taps, first, rows)
                row = lax.broadcasted_iota(jnp.int32, (rows, LANES), 0) + first
                mixed = jnp.where(row < length, query * filtered, 0.0).astype(BF16)
                mixed_ref[first : first + rows, cols] = mixed
                summed = res_ref[first : first + rows, cols].astype(F32) + mixed.astype(F32)
                acc[first : first + rows, :] += summed * summed
        return carry

    lax.fori_loop(0, WIDE // STEP, pair, 0)

    @pl.when(step == pl.num_programs(0) - 1)
    def _():
        sum_ref[...] = jnp.sum(acc[...].T, axis=0, keepdims=True)


def head_call(group_size, predecessor, stretch_lengths, previous, queries, keys_in, values_in, mixed_in, residual, short_taps, lines, mixed):
    rows, width = queries.shape
    per_step = WIDE // group_size
    block = pl.BlockSpec((OPENING, WIDE), lambda p, *_: (0, p))
    small = pl.BlockSpec((16, WIDE), lambda p, *_: (0, p))
    return pl.pallas_call(
        functools.partial(head_kernel, group_size),
        grid_spec=pltpu.PrefetchScalarGridSpec(
            num_scalar_prefetch=2,
            grid=(width // WIDE,),
            in_specs=[
                pl.BlockSpec((WIDE // STEP, PACKED, STEP), lambda p, *_: (p, 0, 0)),
                block,
                small,
                small,
                pl.BlockSpec((192, WIDE), lambda p, *_: (0, p)),
                block,
                pl.BlockSpec((3, 7, WIDE), lambda p, *_: (0, 0, p)),
                pl.BlockSpec((per_step, WINDOW), lambda p, *_: (p, 0)),
                pl.BlockSpec(memory_space=pl.ANY),
            ],
            out_specs=[block, pl.BlockSpec((1, 256), lambda p, *_: (0, 0))],
            scratch_shapes=[
                pltpu.VMEM((2, OPENING + 8, LANES), F32),
                pltpu.VMEM((2, 24, LANES), F32),
                pltpu.VMEM((2, 24, LANES), F32),
                pltpu.VMEM((256, LANES), F32),
            ],
        ),
        out_shape=[
            jax.ShapeDtypeStruct((rows, width), BF16),
            jax.ShapeDtypeStruct((1, 256), F32),
        ],
        input_output_aliases={10: 0},
        compiler_params=params(),
        cost_estimate=cost(128 * width * 2 * WINDOW * 8, 128 * width * 12),
        name="head",
    )(predecessor, stretch_lengths, previous, queries, keys_in, values_in, mixed_in, residual, short_taps, lines, mixed)


def norm_kernel(channels, first_block, sums, len_ref, *refs):
    sum_refs, (mixed_ref, res_ref, gain_ref), out_ref = refs[:sums], refs[sums : sums + 3], refs[-1]
    rows = mixed_ref.shape[0]
    first = (pl.program_id(0) + first_block) * rows
    length = len_ref[lax.axis_index("seq")]
    total = sum_refs[0][...]
    for ref in sum_refs[1:]:
        total = total + ref[...]
    scale = jnp.broadcast_to(lax.rsqrt(total / channels + EPSILON), (LANES, total.shape[1])).T[:rows]
    scale = jnp.where(lax.broadcasted_iota(jnp.int32, (rows, LANES), 0) + first < length, scale, 0.0)
    for lane in range(0, mixed_ref.shape[1], LANES):
        cols = slice(lane, lane + LANES)
        gain = gain_ref[:, cols].astype(F32)
        summed = res_ref[:, cols].astype(F32) + mixed_ref[:, cols].astype(F32)
        out_ref[:, cols] = (summed * scale * gain).astype(BF16)


def norm_call(channels, opening, stretch_lengths, totals, mixed, residual, norm_gain, normed=None):
    rows, width = mixed.shape
    size, first_block, steps, lanes = (OPENING, 0, 1, 256) if opening else (128, 1, rows // 128 - 1, 128)
    block = pl.BlockSpec((size, width), lambda p, *_: (p + first_block, 0))
    operands = [*totals, mixed, residual, norm_gain.reshape(1, width)]
    in_specs = [pl.BlockSpec((1, lanes), lambda p, *_: (0, p))] * len(totals)
    in_specs += [block, block, pl.BlockSpec((1, width), lambda p, *_: (0, 0))]
    aliases = {}
    if normed is not None:
        aliases = {len(operands) + 1: 0}
        operands.append(normed)
        in_specs.append(pl.BlockSpec(memory_space=pl.ANY))
    return pl.pallas_call(
        functools.partial(norm_kernel, channels, first_block, len(totals)),
        grid_spec=pltpu.PrefetchScalarGridSpec(
            num_scalar_prefetch=1, grid=(steps,), in_specs=in_specs, out_specs=block
        ),
        out_shape=jax.ShapeDtypeStruct((rows, width), BF16),
        input_output_aliases=aliases,
        compiler_params=params(),
        cost_estimate=cost(steps * size * width * 6, steps * size * width * 6),
        name="norm_opening" if opening else "norm",
    )(stretch_lengths, *operands)


def swap(array, axis, distance):
    size = lax.axis_size(axis)
    return lax.ppermute(array, axis, [(i, i ^ distance) for i in range(size)])


def exchange(pieces):
    return lax.all_to_all(pieces, "seq", split_axis=0, concat_axis=0, tiled=True)


def shares(squares):
    parts = lax.axis_size("mp")
    if parts != 4:
        return [lax.psum(squares, "mp")]
    return [squares] + [swap(squares, "mp", k) for k in range(1, parts)]


def body(queries, keys_in, values_in, residual, short_taps, mr_filter, norm_gain, predecessor, stretch_lengths):
    rows, width = queries.shape
    count = lax.axis_size("seq")
    channels = width * lax.axis_size("mp")
    group_size = width // mr_filter.shape[1]
    two_phase = width // STEP == count == 8 and mr_filter.shape == (16, LANES)
    packed = tail_call(two_phase, queries, keys_in, values_in, short_taps, mr_filter)
    mixed_in = feature_call(keys_in, values_in, short_taps)
    if two_phase:
        received = exchange(packed)
        received, mixed_in = lax.optimization_barrier((received, mixed_in))
        routed, filter_rows = route_call(predecessor, received)
        previous = exchange(routed)
    else:
        gathered = lax.all_gather(packed[None], "seq", axis=0, tiled=True)
        source = jnp.clip(predecessor[lax.axis_index("seq")], 0, count - 1)
        previous = lax.dynamic_index_in_dim(gathered, source, 0, keepdims=False)
        filter_rows = lax.all_gather(mr_filter, "seq", axis=0, tiled=True)
    mixed, squares, lines = main_call(
        group_size, stretch_lengths, queries, mixed_in, residual, short_taps, filter_rows
    )
    totals = shares(squares)
    mixed, squares = head_call(
        group_size, predecessor, stretch_lengths, previous, queries, keys_in, values_in,
        mixed_in, residual, short_taps, lines, mixed,
    )
    normed = norm_call(channels, False, stretch_lengths, totals, mixed, residual, norm_gain)
    normed = norm_call(channels, True, stretch_lengths, shares(squares), mixed, residual, norm_gain, normed)
    return (mixed, normed)


def solution(mesh):
    in_specs = (
        P("seq", "mp"),
        P("seq", "mp"),
        P("seq", "mp"),
        P("seq", "mp"),
        P(None, None, "mp"),
        P("seq", "mp"),
        P("mp"),
        P(),
        P(),
    )
    out_specs = (P("seq", "mp"), P("seq", "mp"))
    return jax.shard_map(body, mesh=mesh, in_specs=in_specs, out_specs=out_specs, check_vma=False)
```

```python
import functools

import jax
import jax.numpy as jnp
from jax import lax
from jax.experimental import pallas as pl
from jax.experimental.pallas import tpu as pltpu
from jax.sharding import PartitionSpec as P

EPSILON = 1e-06
F32 = jnp.float32
BF16 = jnp.bfloat16
LANES = 128
WIDE = 512
HALVES = 2
BLOCK = 64
WINDOW = 256
PACKED = 160
OPENING = 144
VMEM_LIMIT = 60 * 1024 * 1024


def params(limit=VMEM_LIMIT):
    return pltpu.CompilerParams(vmem_limit_bytes=limit)


def cost(flops, bytes_accessed):
    return pl.CostEstimate(flops=flops, bytes_accessed=bytes_accessed, transcendentals=0)


def short_conv(scratch, taps, start, rows):
    total = None
    for offset in range(taps.shape[0]):
        term = taps[offset : offset + 1] * scratch[pl.ds(start + 8 - offset, rows), :]
        total = term if total is None else total + term
    return total


def tail_kernel(filter_row, q_ref, k_ref, v_ref, kb_ref, vb_ref, taps_ref, filt_ref, out_ref, ks, vs):
    def pair(index, carry):
        for tile in range(2):
            slot = index * 2 + tile
            cols = pl.ds(pl.multiple_of(slot * LANES, LANES), LANES)
            kt, vt = ks.at[tile], vs.at[tile]
            kt[0:16, :] = kb_ref[:, cols].astype(F32)
            vt[0:16, :] = vb_ref[:, cols].astype(F32)
            kt[16:144, :] = k_ref[:, cols].astype(F32)
            vt[16:144, :] = v_ref[:, cols].astype(F32)
            key_taps = taps_ref[1, :, cols].astype(F32)
            value_taps = taps_ref[2, :, cols].astype(F32)
            for row in range(0, 128, 64):
                key = short_conv(kt, key_taps, row + 8, 64)
                value = short_conv(vt, value_taps, row + 8, 64)
                out_ref[slot, row : row + 64, :] = (key * value).astype(BF16)
            last = [q_ref[:, cols].astype(F32)[8:], kt[136:144, :], vt[136:144, :]]
            if filter_row is None:
                last.append(jnp.zeros((8, LANES), F32))
            else:
                last.append(filt_ref[...].astype(F32)[filter_row : filter_row + 8])
            out_ref[slot, 128:PACKED, :] = jnp.concatenate(last).astype(BF16)
        return carry

    lax.fori_loop(0, out_ref.shape[0] // 2, pair, 0)


def tail_call(half, packed, queries, keys_in, values_in, short_taps, mr_filter):
    rows, width = queries.shape
    part = width // HALVES
    slots = part // LANES
    return pl.pallas_call(
        functools.partial(tail_kernel, half * 8 if packed else None),
        grid=(1,),
        in_specs=[
            pl.BlockSpec((16, part), lambda p: (rows // 16 - 1, half)),
            pl.BlockSpec((128, part), lambda p: (rows // 128 - 1, half)),
            pl.BlockSpec((128, part), lambda p: (rows // 128 - 1, half)),
            pl.BlockSpec((16, part), lambda p: (rows // 16 - 9, half)),
            pl.BlockSpec((16, part), lambda p: (rows // 16 - 9, half)),
            pl.BlockSpec((3, 7, part), lambda p: (0, 0, half)),
            pl.BlockSpec(mr_filter.shape, lambda p: (0, 0)),
        ],
        out_specs=pl.BlockSpec((slots, PACKED, LANES), lambda p: (0, 0, 0)),
        out_shape=jax.ShapeDtypeStruct((slots, PACKED, LANES), BF16),
        scratch_shapes=[pltpu.VMEM((2, 144, LANES), F32), pltpu.VMEM((2, 144, LANES), F32)],
        compiler_params=params(),
        cost_estimate=cost(128 * part * 30, 128 * part * 6),
        name="tail%d" % half,
    )(queries, keys_in, values_in, keys_in, values_in, short_taps, mr_filter)


def feature_kernel(k_ref, v_ref, taps_ref, out_ref, ks, vs):
    rows = k_ref.shape[0]

    def pair(index, carry):
        for tile in range(2):
            cols = pl.ds(pl.multiple_of(index * 2 * LANES + tile * LANES, LANES), LANES)
            kt, vt = ks.at[tile], vs.at[tile]
            kt[0:8, :] = jnp.zeros((8, LANES), F32)
            vt[0:8, :] = jnp.zeros((8, LANES), F32)
            kt[8 : rows + 8, :] = k_ref[:, cols].astype(F32)
            vt[8 : rows + 8, :] = v_ref[:, cols].astype(F32)
            key_taps = taps_ref[1, :, cols].astype(F32)
            value_taps = taps_ref[2, :, cols].astype(F32)
            for row in range(0, rows, 64):
                key = short_conv(kt, key_taps, row, 64)
                value = short_conv(vt, value_taps, row, 64)
                out_ref[row : row + 64, cols] = (key * value).astype(BF16)
        return carry

    lax.fori_loop(0, k_ref.shape[1] // (2 * LANES), pair, 0)


def feature_call(keys_in, values_in, short_taps):
    rows, width = keys_in.shape
    rows = rows - 128
    block = pl.BlockSpec((rows, WIDE), lambda p: (0, p))
    return pl.pallas_call(
        feature_kernel,
        grid=(width // WIDE,),
        in_specs=[block, block, pl.BlockSpec((3, 7, WIDE), lambda p: (0, 0, p))],
        out_specs=block,
        out_shape=jax.ShapeDtypeStruct((rows, width), BF16),
        scratch_shapes=[pltpu.VMEM((2, rows + 8, LANES), F32), pltpu.VMEM((2, rows + 8, LANES), F32)],
        compiler_params=params(),
        cost_estimate=cost(rows * width * 30, rows * width * 6),
        name="features",
    )(keys_in, values_in, short_taps)


def route_kernel(pred_ref, in_ref, out_ref, filt_ref):
    for j in range(in_ref.shape[0]):
        out_ref[j] = in_ref[jnp.maximum(pred_ref[j], 0)]
    for j in range(0, in_ref.shape[0], 2):
        lasts = [in_ref[i, 144:160, :].astype(F32)[8:] for i in (j, j + 1)]
        filt_ref[8 * j : 8 * j + 16, :] = jnp.concatenate(lasts).astype(BF16)


def route_call(predecessor, received):
    count = received.shape[0]
    return pl.pallas_call(
        route_kernel,
        in_specs=[pl.BlockSpec(memory_space=pltpu.SMEM), pl.BlockSpec(memory_space=pltpu.VMEM)],
        out_specs=[pl.BlockSpec(memory_space=pltpu.VMEM)] * 2,
        out_shape=[
            jax.ShapeDtypeStruct(received.shape, BF16),
            jax.ShapeDtypeStruct((8 * count, LANES), BF16),
        ],
        compiler_params=params(),
        cost_estimate=cost(0, received.size * 4),
        name="route",
    )(predecessor, received)


def spread_taps(filter_half, half):
    shape = (filter_half.shape[0], WINDOW)
    row = lax.broadcasted_iota(jnp.int32, shape, 0)
    tap = row + (row & ~7) + 8 * half
    place = lax.broadcasted_iota(jnp.int32, shape, 1)
    onehot = (place == WINDOW - BLOCK - tap).astype(BF16)
    return lax.dot_general(filter_half, onehot, (((0,), (0,)), ((), ())), preferred_element_type=F32)


def toeplitz(lines):
    blocks = []
    for g in range(lines.shape[0]):
        line = jnp.broadcast_to(lines[g : g + 1], (BLOCK, WINDOW))
        blocks.append(pltpu.roll(line, 0, 1, stride=1, stride_axis=0).astype(BF16))
    return jnp.concatenate(blocks)


def pick_groups(result, group_size, rows=BLOCK):
    shape = (rows, result.shape[1])
    group = (lax.broadcasted_iota(jnp.int32, shape, 1) & (LANES - 1)) // group_size
    picked = result[:rows]
    for g in range(1, LANES // group_size):
        picked = jnp.where(group == g, result[g * rows : (g + 1) * rows], picked)
    return picked


def main_kernel(group_size, len_ref, q_ref, u_ref, tail0_ref, tail1_ref, res_ref, taps_ref, filt0_ref, filt1_ref, mixed_ref, sum_ref, lines_ref, qs, acc):
    step, steps = pl.program_id(0), pl.num_programs(0)
    rows, inner = q_ref.shape[0], u_ref.shape[0]
    per_lane = LANES // group_size
    length = len_ref[lax.axis_index("seq")]

    @pl.when(step == 0)
    def _():
        lines_ref[...] = spread_taps(filt0_ref[...], 0) + spread_taps(filt1_ref[...], 1)
        acc[...] = jnp.zeros_like(acc)

    mixed_ref[0:128, :] = jnp.zeros((128, WIDE), BF16)

    def pair(index, carry):
        for tile in range(2):
            number = index * 2 + tile
            cols = pl.ds(pl.multiple_of(number * LANES, LANES), LANES)
            qt = qs.at[tile]
            qt[0:8, :] = jnp.zeros((8, LANES), F32)
            qt[8 : rows + 8, :] = q_ref[:, cols].astype(F32)
            query_taps = taps_ref[0, :, cols].astype(F32)
            last = jnp.where(step < steps // HALVES, tail0_ref[number, 0:128, :], tail1_ref[number, 0:128, :])
            base = pl.multiple_of((step * (WIDE // LANES) + number) * per_lane, per_lane)
            matrix = toeplitz(lines_ref[pl.ds(base, per_lane), :])
            for start in range(128, rows, 2 * BLOCK):
                windows = []
                for first in (start, start + BLOCK):
                    low, high = first + BLOCK - WINDOW, first + BLOCK
                    if low < 0:
                        windows.append(jnp.concatenate([jnp.zeros((-low, LANES), BF16), u_ref[0:high, cols]]))
                    elif high > inner:
                        windows.append(jnp.concatenate([u_ref[low:inner, cols], last[: high - inner]]))
                    else:
                        windows.append(u_ref[low:high, cols])
                result = jnp.dot(matrix, jnp.concatenate(windows, axis=1), preferred_element_type=F32)
                picked = pick_groups(result, group_size)
                for half in range(2):
                    first = start + half * BLOCK
                    filtered = picked[:, half * LANES : (half + 1) * LANES]
                    query = short_conv(qt, query_taps, first, BLOCK)
                    row = lax.broadcasted_iota(jnp.int32, (BLOCK, LANES), 0) + first
                    mixed = jnp.where(row < length, query * filtered, 0.0).astype(BF16)
                    mixed_ref[first : first + BLOCK, cols] = mixed
                    summed = res_ref[first : first + BLOCK, cols].astype(F32) + mixed.astype(F32)
                    acc[first - 128 : first - 128 + BLOCK, :] += summed * summed
        return carry

    lax.fori_loop(0, WIDE // (2 * LANES), pair, 0)

    @pl.when(step == pl.num_programs(0) - 1)
    def _():
        sum_ref[...] = jnp.sum(acc[...].T, axis=0, keepdims=True)


def main_call(group_size, stretch_lengths, queries, mixed_in, tails, residual, short_taps, filters):
    rows, width = queries.shape
    groups = filters[0].shape[1]
    last = width // WIDE // HALVES - 1
    tail_block = (WIDE // LANES, PACKED, LANES)
    block = pl.BlockSpec((rows, WIDE), lambda p, *_: (0, p))
    return pl.pallas_call(
        functools.partial(main_kernel, group_size),
        grid_spec=pltpu.PrefetchScalarGridSpec(
            num_scalar_prefetch=1,
            grid=(width // WIDE,),
            in_specs=[
                block,
                pl.BlockSpec((mixed_in.shape[0], WIDE), lambda p, *_: (0, p)),
                pl.BlockSpec(tail_block, lambda p, *_: (jnp.minimum(p, last), 0, 0)),
                pl.BlockSpec(tail_block, lambda p, *_: (jnp.maximum(p - last - 1, 0), 0, 0)),
                block,
                pl.BlockSpec((3, 7, WIDE), lambda p, *_: (0, 0, p)),
                pl.BlockSpec(filters[0].shape, lambda p, *_: (0, 0)),
                pl.BlockSpec(filters[1].shape, lambda p, *_: (0, 0)),
            ],
            out_specs=[
                block,
                pl.BlockSpec((1, rows - 128), lambda p, *_: (0, 0)),
                pl.BlockSpec((groups, WINDOW), lambda p, *_: (0, 0)),
            ],
            scratch_shapes=[
                pltpu.VMEM((2, rows + 8, LANES), F32),
                pltpu.VMEM((rows - 128, LANES), F32),
            ],
        ),
        out_shape=[
            jax.ShapeDtypeStruct((rows, width), BF16),
            jax.ShapeDtypeStruct((1, rows - 128), F32),
            jax.ShapeDtypeStruct((groups, WINDOW), F32),
        ],
        compiler_params=params(),
        cost_estimate=cost(rows * width * 2 * WINDOW * 8, rows * width * 12),
        name="conv",
    )(stretch_lengths, queries, mixed_in, *tails, residual, short_taps, *filters)


def head_kernel(group_size, pred_ref, len_ref, held, q_ref, k_ref, v_ref, u_ref, res_ref, taps_ref, lines_ref, part_ref, kept_ref, mixed_ref, sum_ref, qs, ks, vs, acc):
    del kept_ref
    step = pl.program_id(0)
    per_lane = LANES // group_size
    device = lax.axis_index("seq")
    length = len_ref[device]
    follows = pred_ref[device] >= 0

    @pl.when(step == 0)
    def _():
        acc[...] = jnp.zeros_like(acc)

    def pair(index, carry):
        for tile in range(2):
            number = index * 2 + tile
            cols = pl.ds(pl.multiple_of(number * LANES, LANES), LANES)
            qt, kt, vt = qs.at[tile], ks.at[tile], vs.at[tile]
            prev = jnp.where(follows, held[number, 128:PACKED, :].astype(F32), 0.0)
            qt[0:8, :] = prev[0:8]
            kt[0:8, :] = prev[8:16]
            vt[0:8, :] = prev[16:24]
            qt[8 : OPENING + 8, :] = q_ref[:, cols].astype(F32)
            kt[8:24, :] = k_ref[:, cols].astype(F32)
            vt[8:24, :] = v_ref[:, cols].astype(F32)
            query_taps = taps_ref[0, :, cols].astype(F32)
            key = short_conv(kt, taps_ref[1, :, cols].astype(F32), 0, 16)
            value = short_conv(vt, taps_ref[2, :, cols].astype(F32), 0, 16)
            opening = (key * value).astype(BF16)
            state = held[number, 0:128, :]
            state = jnp.where(follows, state, jnp.zeros_like(state))
            extended = jnp.concatenate([jnp.zeros((64, LANES), BF16), state, opening, u_ref[16:192, cols]])
            windows = jnp.concatenate([extended[0:WINDOW], extended[BLOCK : BLOCK + WINDOW]], axis=1)
            base = pl.multiple_of(number * per_lane, per_lane)
            matrix = toeplitz(lines_ref[pl.ds(base, per_lane), :])
            result = jnp.dot(matrix, windows, preferred_element_type=F32)
            picked = pick_groups(result, group_size)
            edge = OPENING - 2 * BLOCK
            edge_matrix = jnp.concatenate([matrix[g * BLOCK : g * BLOCK + edge] for g in range(per_lane)])
            edge_result = jnp.dot(edge_matrix, extended[2 * BLOCK : 2 * BLOCK + WINDOW], preferred_element_type=F32)
            parts = [
                (0, BLOCK, picked[:, :LANES]),
                (BLOCK, BLOCK, picked[:, LANES:]),
                (2 * BLOCK, edge, pick_groups(edge_result, group_size, edge)),
            ]
            for first, rows, filtered in parts:
                query = short_conv(qt, query_taps, first, rows)
                row = lax.broadcasted_iota(jnp.int32, (rows, LANES), 0) + first
                mixed = jnp.where(row < length, query * filtered, 0.0).astype(BF16)
                mixed_ref[first : first + rows, cols] = mixed
                summed = res_ref[first : first + rows, cols].astype(F32) + mixed.astype(F32)
                acc[first : first + rows, :] += summed * summed
        return carry

    lax.fori_loop(0, WIDE // (2 * LANES), pair, 0)

    @pl.when(step == pl.num_programs(0) - 1)
    def _():
        sum_ref[...] = part_ref[...] + jnp.sum(acc[...].T, axis=0, keepdims=True)


def head_call(half, group_size, predecessor, stretch_lengths, previous, queries, keys_in, values_in, mixed_in, residual, short_taps, lines, squares, mixed):
    rows, width = queries.shape
    per_step = WIDE // group_size
    steps = width // WIDE // HALVES
    skip = half * steps
    block = pl.BlockSpec((OPENING, WIDE), lambda p, *_: (0, p + skip))
    small = pl.BlockSpec((16, WIDE), lambda p, *_: (0, p + skip))
    return pl.pallas_call(
        functools.partial(head_kernel, group_size),
        grid_spec=pltpu.PrefetchScalarGridSpec(
            num_scalar_prefetch=2,
            grid=(steps,),
            in_specs=[
                pl.BlockSpec((WIDE // LANES, PACKED, LANES), lambda p, *_: (p, 0, 0)),
                block,
                small,
                small,
                pl.BlockSpec((192, WIDE), lambda p, *_: (0, p + skip)),
                block,
                pl.BlockSpec((3, 7, WIDE), lambda p, *_: (0, 0, p + skip)),
                pl.BlockSpec((per_step, WINDOW), lambda p, *_: (p + skip, 0)),
                pl.BlockSpec((1, 256), lambda p, *_: (0, 0)),
                pl.BlockSpec(memory_space=pl.ANY),
            ],
            out_specs=[block, pl.BlockSpec((1, 256), lambda p, *_: (0, 0))],
            scratch_shapes=[
                pltpu.VMEM((2, OPENING + 8, LANES), F32),
                pltpu.VMEM((2, 24, LANES), F32),
                pltpu.VMEM((2, 24, LANES), F32),
                pltpu.VMEM((256, LANES), F32),
            ],
        ),
        out_shape=[
            jax.ShapeDtypeStruct((rows, width), BF16),
            jax.ShapeDtypeStruct((1, 256), F32),
        ],
        input_output_aliases={11: 0},
        compiler_params=params(),
        cost_estimate=cost(64 * width * 2 * WINDOW * 8, 64 * width * 12),
        name="head%d" % half,
    )(predecessor, stretch_lengths, previous, queries, keys_in, values_in, mixed_in, residual, short_taps, lines, squares, mixed)


def norm_kernel(channels, first_block, sums, len_ref, *refs):
    sum_refs, (mixed_ref, res_ref, gain_ref), out_ref = refs[:sums], refs[sums : sums + 3], refs[-1]
    rows = mixed_ref.shape[0]
    first = (pl.program_id(0) + first_block) * rows
    length = len_ref[lax.axis_index("seq")]
    total = sum_refs[0][...]
    for ref in sum_refs[1:]:
        total = total + ref[...]
    scale = jnp.broadcast_to(lax.rsqrt(total / channels + EPSILON), (LANES, total.shape[1])).T[:rows]
    scale = jnp.where(lax.broadcasted_iota(jnp.int32, (rows, LANES), 0) + first < length, scale, 0.0)
    for lane in range(0, mixed_ref.shape[1], LANES):
        cols = slice(lane, lane + LANES)
        gain = gain_ref[:, cols].astype(F32)
        summed = res_ref[:, cols].astype(F32) + mixed_ref[:, cols].astype(F32)
        out_ref[:, cols] = (summed * scale * gain).astype(BF16)


def norm_call(channels, opening, stretch_lengths, totals, mixed, residual, norm_gain, normed=None):
    rows, width = mixed.shape
    size, first_block, steps, lanes = (OPENING, 0, 1, 256) if opening else (128, 1, rows // 128 - 1, 128)
    block = pl.BlockSpec((size, width), lambda p, *_: (p + first_block, 0))
    operands = [*totals, mixed, residual, norm_gain.reshape(1, width)]
    in_specs = [pl.BlockSpec((1, lanes), lambda p, *_: (0, p))] * len(totals)
    in_specs += [block, block, pl.BlockSpec((1, width), lambda p, *_: (0, 0))]
    aliases = {}
    if normed is not None:
        aliases = {len(operands) + 1: 0}
        operands.append(normed)
        in_specs.append(pl.BlockSpec(memory_space=pl.ANY))
    return pl.pallas_call(
        functools.partial(norm_kernel, channels, first_block, len(totals)),
        grid_spec=pltpu.PrefetchScalarGridSpec(
            num_scalar_prefetch=1, grid=(steps,), in_specs=in_specs, out_specs=block
        ),
        out_shape=jax.ShapeDtypeStruct((rows, width), BF16),
        input_output_aliases=aliases,
        compiler_params=params(),
        cost_estimate=cost(steps * size * width * 6, steps * size * width * 6),
        name="norm_opening" if opening else "norm",
    )(stretch_lengths, *operands)


def swap(array, axis, distance):
    size = lax.axis_size(axis)
    return lax.ppermute(array, axis, [(i, i ^ distance) for i in range(size)])


def exchange(pieces):
    return lax.all_to_all(pieces, "seq", split_axis=0, concat_axis=0, tiled=True)


def shares(squares):
    parts = lax.axis_size("mp")
    if parts != 4:
        return [lax.psum(squares, "mp")]
    return [squares] + [swap(squares, "mp", k) for k in range(1, parts)]


def body(queries, keys_in, values_in, residual, short_taps, mr_filter, norm_gain, predecessor, stretch_lengths):
    rows, width = queries.shape
    count = lax.axis_size("seq")
    channels = width * lax.axis_size("mp")
    group_size = width // mr_filter.shape[1]
    halves = range(HALVES)
    two_phase = width == HALVES * LANES * count and count == 8 and mr_filter.shape == (16, LANES)
    packed = [tail_call(h, two_phase, queries, keys_in, values_in, short_taps, mr_filter) for h in halves]
    mixed_in = feature_call(keys_in, values_in, short_taps)
    if two_phase:
        received = [exchange(pieces) for pieces in packed]
        received[0], mixed_in = lax.optimization_barrier((received[0], mixed_in))
        routed = [route_call(predecessor, pieces) for pieces in received]
        previous = [exchange(pieces) for pieces, _ in routed]
        filters = [rows_of_half for _, rows_of_half in routed]
    else:
        source = jnp.clip(predecessor[lax.axis_index("seq")], 0, count - 1)
        gathered = [lax.all_gather(pieces[None], "seq", axis=0, tiled=True) for pieces in packed]
        previous = [lax.dynamic_index_in_dim(pieces, source, 0, keepdims=False) for pieces in gathered]
        filter_rows = lax.all_gather(mr_filter, "seq", axis=0, tiled=True)
        split = filter_rows.reshape(-1, 2, 8, filter_rows.shape[1])
        filters = [split[:, h].reshape(-1, filter_rows.shape[1]) for h in halves]
    mixed, squares, lines = main_call(
        group_size, stretch_lengths, queries, mixed_in, packed, residual, short_taps, filters
    )
    totals = shares(squares)
    squares = jnp.zeros((1, 256), F32)
    for h in halves:
        mixed, squares = head_call(
            h, group_size, predecessor, stretch_lengths, previous[h], queries, keys_in, values_in,
            mixed_in, residual, short_taps, lines, squares, mixed,
        )
    normed = norm_call(channels, False, stretch_lengths, totals, mixed, residual, norm_gain)
    normed = norm_call(channels, True, stretch_lengths, shares(squares), mixed, residual, norm_gain, normed)
    return (mixed, normed)


def solution(mesh):
    in_specs = (
        P("seq", "mp"),
        P("seq", "mp"),
        P("seq", "mp"),
        P("seq", "mp"),
        P(None, None, "mp"),
        P("seq", "mp"),
        P("mp"),
        P(),
        P(),
    )
    out_specs = (P("seq", "mp"), P("seq", "mp"))
    return jax.shard_map(body, mesh=mesh, in_specs=in_specs, out_specs=out_specs, check_vma=False)
```

```python
import functools

import jax
import jax.numpy as jnp
from jax import lax
from jax.experimental import pallas as pl
from jax.experimental.pallas import tpu as pltpu
from jax.sharding import PartitionSpec as P

EPSILON = 1e-06
F32 = jnp.float32
BF16 = jnp.bfloat16
LANES = 128
STEP = 256
WIDE = 512
BLOCK = 64
WINDOW = 256
PACKED = 160
OPENING = 144
VMEM_LIMIT = 64 * 1024 * 1024


def params():
    return pltpu.CompilerParams(vmem_limit_bytes=VMEM_LIMIT)


def cost(flops, bytes_accessed):
    return pl.CostEstimate(flops=flops, bytes_accessed=bytes_accessed, transcendentals=0)


def short_conv(scratch, taps, start, rows):
    total = None
    for offset in range(taps.shape[0]):
        term = taps[offset : offset + 1] * scratch[pl.ds(start + 8 - offset, rows), :]
        total = term if total is None else total + term
    return total


def tail_kernel(packed, q_ref, k_ref, v_ref, kb_ref, vb_ref, taps_ref, filt_ref, out_ref, ks, vs):
    def piece(slot, carry):
        lasts = []
        for tile in range(STEP // LANES):
            cols = pl.ds(pl.multiple_of(slot * STEP + tile * LANES, LANES), LANES)
            here = slice(tile * LANES, (tile + 1) * LANES)
            kt, vt = ks.at[tile], vs.at[tile]
            kt[0:16, :] = kb_ref[:, cols].astype(F32)
            vt[0:16, :] = vb_ref[:, cols].astype(F32)
            kt[16:144, :] = k_ref[:, cols].astype(F32)
            vt[16:144, :] = v_ref[:, cols].astype(F32)
            key_taps = taps_ref[1, :, cols].astype(F32)
            value_taps = taps_ref[2, :, cols].astype(F32)
            for row in range(0, 128, 64):
                key = short_conv(kt, key_taps, row + 8, 64)
                value = short_conv(vt, value_taps, row + 8, 64)
                out_ref[slot, row : row + 64, here] = (key * value).astype(BF16)
            last = [q_ref[:, cols].astype(F32)[8:], kt[136:144, :], vt[136:144, :]]
            if packed:
                last.append(filt_ref[...].astype(F32)[8 * tile : 8 * tile + 8])
            else:
                last.append(jnp.zeros((8, LANES), F32))
            lasts.append(jnp.concatenate(last))
        out_ref[slot, 128:PACKED, :] = jnp.concatenate(lasts, axis=1).astype(BF16)
        return carry

    lax.fori_loop(0, out_ref.shape[0], piece, 0)


def tail_call(packed, queries, keys_in, values_in, short_taps, mr_filter):
    rows, width = queries.shape
    slots = width // STEP
    return pl.pallas_call(
        functools.partial(tail_kernel, packed),
        grid=(1,),
        in_specs=[
            pl.BlockSpec((16, width), lambda p: (rows // 16 - 1, 0)),
            pl.BlockSpec((128, width), lambda p: (rows // 128 - 1, 0)),
            pl.BlockSpec((128, width), lambda p: (rows // 128 - 1, 0)),
            pl.BlockSpec((16, width), lambda p: (rows // 16 - 9, 0)),
            pl.BlockSpec((16, width), lambda p: (rows // 16 - 9, 0)),
            pl.BlockSpec(short_taps.shape, lambda p: (0, 0, 0)),
            pl.BlockSpec(mr_filter.shape, lambda p: (0, 0)),
        ],
        out_specs=pl.BlockSpec((slots, PACKED, STEP), lambda p: (0, 0, 0)),
        out_shape=jax.ShapeDtypeStruct((slots, PACKED, STEP), BF16),
        scratch_shapes=[pltpu.VMEM((2, 144, LANES), F32), pltpu.VMEM((2, 144, LANES), F32)],
        compiler_params=params(),
        cost_estimate=cost(128 * width * 30, 128 * width * 6),
        name="tail",
    )(queries, keys_in, values_in, keys_in, values_in, short_taps, mr_filter)


def feature_kernel(k_ref, v_ref, taps_ref, out_ref, ks, vs):
    rows = k_ref.shape[0]

    def pair(index, carry):
        for tile in range(2):
            cols = pl.ds(pl.multiple_of(index * 2 * LANES + tile * LANES, LANES), LANES)
            kt, vt = ks.at[tile], vs.at[tile]
            kt[0:8, :] = jnp.zeros((8, LANES), F32)
            vt[0:8, :] = jnp.zeros((8, LANES), F32)
            kt[8 : rows + 8, :] = k_ref[:, cols].astype(F32)
            vt[8 : rows + 8, :] = v_ref[:, cols].astype(F32)
            key_taps = taps_ref[1, :, cols].astype(F32)
            value_taps = taps_ref[2, :, cols].astype(F32)
            for row in range(0, rows, 64):
                key = short_conv(kt, key_taps, row, 64)
                value = short_conv(vt, value_taps, row, 64)
                out_ref[row : row + 64, cols] = (key * value).astype(BF16)
        return carry

    lax.fori_loop(0, k_ref.shape[1] // (2 * LANES), pair, 0)


def feature_call(keys_in, values_in, short_taps):
    rows, width = keys_in.shape
    block = pl.BlockSpec((rows, WIDE), lambda p: (0, p))
    return pl.pallas_call(
        feature_kernel,
        grid=(width // WIDE,),
        in_specs=[block, block, pl.BlockSpec((3, 7, WIDE), lambda p: (0, 0, p))],
        out_specs=block,
        out_shape=jax.ShapeDtypeStruct((rows, width), BF16),
        scratch_shapes=[pltpu.VMEM((2, rows + 8, LANES), F32), pltpu.VMEM((2, rows + 8, LANES), F32)],
        compiler_params=params(),
        cost_estimate=cost(rows * width * 30, rows * width * 6),
        name="features",
    )(keys_in, values_in, short_taps)


def route_kernel(pred_ref, in_ref, out_ref, sems):
    copies = []
    for j in range(in_ref.shape[0]):
        source = jnp.maximum(pred_ref[j], 0)
        copies.append(pltpu.make_async_copy(in_ref.at[source], out_ref.at[j], sems.at[j]))
        copies[-1].start()
    for copy in copies:
        copy.wait()


def route_call(predecessor, received):
    return pl.pallas_call(
        route_kernel,
        in_specs=[pl.BlockSpec(memory_space=pltpu.SMEM), pl.BlockSpec(memory_space=pl.ANY)],
        out_specs=pl.BlockSpec(memory_space=pl.ANY),
        out_shape=jax.ShapeDtypeStruct(received.shape, BF16),
        scratch_shapes=[pltpu.SemaphoreType.DMA((received.shape[0],))],
        compiler_params=params(),
        cost_estimate=cost(0, received.size * 4),
        name="route",
    )(predecessor, received)


def all_taps(filt_ref):
    if len(filt_ref.shape) == 2:
        return filt_ref[...]
    rows = []
    for j in range(filt_ref.shape[0]):
        last = filt_ref[j].astype(F32)[8:]
        rows += [last[:, :LANES], last[:, LANES:]]
    return jnp.concatenate(rows).astype(BF16)


def spread_taps(filter_rows):
    shape = (filter_rows.shape[0], WINDOW)
    tap = lax.broadcasted_iota(jnp.int32, shape, 0)
    place = lax.broadcasted_iota(jnp.int32, shape, 1)
    onehot = (place == WINDOW - BLOCK - tap).astype(BF16)
    return lax.dot_general(filter_rows, onehot, (((0,), (0,)), ((), ())), preferred_element_type=F32)


def toeplitz(lines):
    blocks = []
    for g in range(lines.shape[0]):
        line = jnp.broadcast_to(lines[g : g + 1], (BLOCK, WINDOW))
        blocks.append(pltpu.roll(line, 0, 1, stride=1, stride_axis=0).astype(BF16))
    return jnp.concatenate(blocks)


def pick_groups(result, group_size, rows=BLOCK):
    shape = (rows, result.shape[1])
    group = (lax.broadcasted_iota(jnp.int32, shape, 1) & (LANES - 1)) // group_size
    picked = result[:rows]
    for g in range(1, LANES // group_size):
        picked = jnp.where(group == g, result[g * rows : (g + 1) * rows], picked)
    return picked


def main_kernel(group_size, len_ref, q_ref, u_ref, res_ref, taps_ref, filt_ref, mixed_ref, sum_ref, lines_ref, qs, acc):
    step = pl.program_id(0)
    rows = q_ref.shape[0]
    per_lane = LANES // group_size
    length = len_ref[lax.axis_index("seq")]

    @pl.when(step == 0)
    def _():
        lines_ref[...] = spread_taps(all_taps(filt_ref))
        acc[...] = jnp.zeros_like(acc)

    mixed_ref[0:128, :] = jnp.zeros((128, WIDE), BF16)

    def pair(index, carry):
        for tile in range(2):
            number = index * 2 + tile
            cols = pl.ds(pl.multiple_of(number * LANES, LANES), LANES)
            qt = qs.at[tile]
            qt[0:8, :] = jnp.zeros((8, LANES), F32)
            qt[8 : rows + 8, :] = q_ref[:, cols].astype(F32)
            query_taps = taps_ref[0, :, cols].astype(F32)
            base = pl.multiple_of((step * (WIDE // LANES) + number) * per_lane, per_lane)
            matrix = toeplitz(lines_ref[pl.ds(base, per_lane), :])
            for start in range(128, rows, 2 * BLOCK):
                windows = []
                for first in (start, start + BLOCK):
                    low = first + BLOCK - WINDOW
                    if low < 0:
                        windows.append(
                            jnp.concatenate([jnp.zeros((-low, LANES), BF16), u_ref[0 : first + BLOCK, cols]])
                        )
                    else:
                        windows.append(u_ref[low : first + BLOCK, cols])
                result = jnp.dot(matrix, jnp.concatenate(windows, axis=1), preferred_element_type=F32)
                picked = pick_groups(result, group_size)
                for half in range(2):
                    first = start + half * BLOCK
                    filtered = picked[:, half * LANES : (half + 1) * LANES]
                    query = short_conv(qt, query_taps, first, BLOCK)
                    row = lax.broadcasted_iota(jnp.int32, (BLOCK, LANES), 0) + first
                    mixed = jnp.where(row < length, query * filtered, 0.0).astype(BF16)
                    mixed_ref[first : first + BLOCK, cols] = mixed
                    summed = res_ref[first : first + BLOCK, cols].astype(F32) + mixed.astype(F32)
                    acc[first - 128 : first - 128 + BLOCK, :] += summed * summed
        return carry

    lax.fori_loop(0, WIDE // (2 * LANES), pair, 0)

    @pl.when(step == pl.num_programs(0) - 1)
    def _():
        sum_ref[...] = jnp.sum(acc[...].T, axis=0, keepdims=True)


def main_call(group_size, stretch_lengths, queries, mixed_in, residual, short_taps, filter_rows):
    rows, width = queries.shape
    groups = width // group_size
    if len(filter_rows.shape) == 2:
        filter_spec = pl.BlockSpec(filter_rows.shape, lambda p, *_: (0, 0))
    else:
        filter_spec = pl.BlockSpec((filter_rows.shape[0], 16, STEP), lambda p, *_: (0, PACKED // 16 - 1, 0))
    block = pl.BlockSpec((rows, WIDE), lambda p, *_: (0, p))
    return pl.pallas_call(
        functools.partial(main_kernel, group_size),
        grid_spec=pltpu.PrefetchScalarGridSpec(
            num_scalar_prefetch=1,
            grid=(width // WIDE,),
            in_specs=[
                block,
                block,
                block,
                pl.BlockSpec((3, 7, WIDE), lambda p, *_: (0, 0, p)),
                filter_spec,
            ],
            out_specs=[
                block,
                pl.BlockSpec((1, rows - 128), lambda p, *_: (0, 0)),
                pl.BlockSpec((groups, WINDOW), lambda p, *_: (0, 0)),
            ],
            scratch_shapes=[
                pltpu.VMEM((2, rows + 8, LANES), F32),
                pltpu.VMEM((rows - 128, LANES), F32),
            ],
        ),
        out_shape=[
            jax.ShapeDtypeStruct((rows, width), BF16),
            jax.ShapeDtypeStruct((1, rows - 128), F32),
            jax.ShapeDtypeStruct((groups, WINDOW), F32),
        ],
        compiler_params=params(),
        cost_estimate=cost(rows * width * 2 * WINDOW * 8, rows * width * 12),
        name="conv",
    )(stretch_lengths, queries, mixed_in, residual, short_taps, filter_rows)


def head_kernel(group_size, pred_ref, len_ref, held, q_ref, k_ref, v_ref, u_ref, res_ref, taps_ref, lines_ref, kept_ref, mixed_ref, sum_ref, qs, ks, vs, acc):
    del kept_ref
    step = pl.program_id(0)
    per_lane = LANES // group_size
    device = lax.axis_index("seq")
    length = len_ref[device]
    follows = pred_ref[device] >= 0

    @pl.when(step == 0)
    def _():
        acc[...] = jnp.zeros_like(acc)

    def pair(index, carry):
        for tile in range(2):
            number = index * 2 + tile
            cols = pl.ds(pl.multiple_of(number * LANES, LANES), LANES)
            here = slice(tile * LANES, (tile + 1) * LANES)
            qt, kt, vt = qs.at[tile], ks.at[tile], vs.at[tile]
            prev = jnp.where(follows, held[index, 128:PACKED, here].astype(F32), 0.0)
            qt[0:8, :] = prev[0:8]
            kt[0:8, :] = prev[8:16]
            vt[0:8, :] = prev[16:24]
            qt[8 : OPENING + 8, :] = q_ref[:, cols].astype(F32)
            kt[8:24, :] = k_ref[:, cols].astype(F32)
            vt[8:24, :] = v_ref[:, cols].astype(F32)
            query_taps = taps_ref[0, :, cols].astype(F32)
            key = short_conv(kt, taps_ref[1, :, cols].astype(F32), 0, 16)
            value = short_conv(vt, taps_ref[2, :, cols].astype(F32), 0, 16)
            opening = (key * value).astype(BF16)
            state = held[index, 0:128, here]
            state = jnp.where(follows, state, jnp.zeros_like(state))
            extended = jnp.concatenate([jnp.zeros((64, LANES), BF16), state, opening, u_ref[16:192, cols]])
            windows = jnp.concatenate([extended[0:WINDOW], extended[BLOCK : BLOCK + WINDOW]], axis=1)
            base = pl.multiple_of(number * per_lane, per_lane)
            matrix = toeplitz(lines_ref[pl.ds(base, per_lane), :])
            result = jnp.dot(matrix, windows, preferred_element_type=F32)
            picked = pick_groups(result, group_size)
            edge = OPENING - 2 * BLOCK
            edge_matrix = jnp.concatenate([matrix[g * BLOCK : g * BLOCK + edge] for g in range(per_lane)])
            edge_result = jnp.dot(edge_matrix, extended[2 * BLOCK : 2 * BLOCK + WINDOW], preferred_element_type=F32)
            parts = [
                (0, BLOCK, picked[:, :LANES]),
                (BLOCK, BLOCK, picked[:, LANES:]),
                (2 * BLOCK, edge, pick_groups(edge_result, group_size, edge)),
            ]
            for first, rows, filtered in parts:
                query = short_conv(qt, query_taps, first, rows)
                row = lax.broadcasted_iota(jnp.int32, (rows, LANES), 0) + first
                mixed = jnp.where(row < length, query * filtered, 0.0).astype(BF16)
                mixed_ref[first : first + rows, cols] = mixed
                summed = res_ref[first : first + rows, cols].astype(F32) + mixed.astype(F32)
                acc[first : first + rows, :] += summed * summed
        return carry

    lax.fori_loop(0, WIDE // STEP, pair, 0)

    @pl.when(step == pl.num_programs(0) - 1)
    def _():
        sum_ref[...] = jnp.sum(acc[...].T, axis=0, keepdims=True)


def head_call(group_size, predecessor, stretch_lengths, previous, queries, keys_in, values_in, mixed_in, residual, short_taps, lines, mixed):
    rows, width = queries.shape
    per_step = WIDE // group_size
    block = pl.BlockSpec((OPENING, WIDE), lambda p, *_: (0, p))
    small = pl.BlockSpec((16, WIDE), lambda p, *_: (0, p))
    return pl.pallas_call(
        functools.partial(head_kernel, group_size),
        grid_spec=pltpu.PrefetchScalarGridSpec(
            num_scalar_prefetch=2,
            grid=(width // WIDE,),
            in_specs=[
                pl.BlockSpec((WIDE // STEP, PACKED, STEP), lambda p, *_: (p, 0, 0)),
                block,
                small,
                small,
                pl.BlockSpec((192, WIDE), lambda p, *_: (0, p)),
                block,
                pl.BlockSpec((3, 7, WIDE), lambda p, *_: (0, 0, p)),
                pl.BlockSpec((per_step, WINDOW), lambda p, *_: (p, 0)),
                pl.BlockSpec(memory_space=pl.ANY),
            ],
            out_specs=[block, pl.BlockSpec((1, 256), lambda p, *_: (0, 0))],
            scratch_shapes=[
                pltpu.VMEM((2, OPENING + 8, LANES), F32),
                pltpu.VMEM((2, 24, LANES), F32),
                pltpu.VMEM((2, 24, LANES), F32),
                pltpu.VMEM((256, LANES), F32),
            ],
        ),
        out_shape=[
            jax.ShapeDtypeStruct((rows, width), BF16),
            jax.ShapeDtypeStruct((1, 256), F32),
        ],
        input_output_aliases={10: 0},
        compiler_params=params(),
        cost_estimate=cost(128 * width * 2 * WINDOW * 8, 128 * width * 12),
        name="head",
    )(predecessor, stretch_lengths, previous, queries, keys_in, values_in, mixed_in, residual, short_taps, lines, mixed)


def norm_kernel(channels, first_block, sums, len_ref, *refs):
    sum_refs, (mixed_ref, res_ref, gain_ref), out_ref = refs[:sums], refs[sums : sums + 3], refs[-1]
    rows = mixed_ref.shape[0]
    first = (pl.program_id(0) + first_block) * rows
    length = len_ref[lax.axis_index("seq")]
    total = sum_refs[0][...]
    for ref in sum_refs[1:]:
        total = total + ref[...]
    scale = jnp.broadcast_to(lax.rsqrt(total / channels + EPSILON), (LANES, total.shape[1])).T[:rows]
    scale = jnp.where(lax.broadcasted_iota(jnp.int32, (rows, LANES), 0) + first < length, scale, 0.0)
    for lane in range(0, mixed_ref.shape[1], LANES):
        cols = slice(lane, lane + LANES)
        gain = gain_ref[:, cols].astype(F32)
        summed = res_ref[:, cols].astype(F32) + mixed_ref[:, cols].astype(F32)
        out_ref[:, cols] = (summed * scale * gain).astype(BF16)


def norm_call(channels, opening, stretch_lengths, totals, mixed, residual, norm_gain, normed=None):
    rows, width = mixed.shape
    size, first_block, steps, lanes = (OPENING, 0, 1, 256) if opening else (128, 1, rows // 128 - 1, 128)
    chunk = width // (4 if opening else 2)
    block = pl.BlockSpec((size, chunk), lambda p, c, *_: (p + first_block, c))
    operands = [*totals, mixed, residual, norm_gain.reshape(1, width)]
    in_specs = [pl.BlockSpec((1, lanes), lambda p, c, *_: (0, p))] * len(totals)
    in_specs += [block, block, pl.BlockSpec((1, chunk), lambda p, c, *_: (0, c))]
    aliases = {}
    if normed is not None:
        aliases = {len(operands) + 1: 0}
        operands.append(normed)
        in_specs.append(pl.BlockSpec(memory_space=pl.ANY))
    return pl.pallas_call(
        functools.partial(norm_kernel, channels, first_block, len(totals)),
        grid_spec=pltpu.PrefetchScalarGridSpec(
            num_scalar_prefetch=1, grid=(steps, width // chunk), in_specs=in_specs, out_specs=block
        ),
        out_shape=jax.ShapeDtypeStruct((rows, width), BF16),
        input_output_aliases=aliases,
        compiler_params=params(),
        cost_estimate=cost(steps * size * width * 6, steps * size * width * 6),
        name="norm_opening" if opening else "norm",
    )(stretch_lengths, *operands)


def swap(array, axis, distance):
    size = lax.axis_size(axis)
    return lax.ppermute(array, axis, [(i, i ^ distance) for i in range(size)])


def exchange(pieces):
    return lax.all_to_all(pieces, "seq", split_axis=0, concat_axis=0, tiled=True)


def shares(squares):
    parts = lax.axis_size("mp")
    if parts != 4:
        return [lax.psum(squares, "mp")]
    return [squares] + [swap(squares, "mp", k) for k in range(1, parts)]


def body(queries, keys_in, values_in, residual, short_taps, mr_filter, norm_gain, predecessor, stretch_lengths):
    rows, width = queries.shape
    count = lax.axis_size("seq")
    channels = width * lax.axis_size("mp")
    group_size = width // mr_filter.shape[1]
    two_phase = width // STEP == count == 8 and mr_filter.shape == (16, LANES)
    packed = tail_call(two_phase, queries, keys_in, values_in, short_taps, mr_filter)
    mixed_in = feature_call(keys_in, values_in, short_taps)
    if two_phase:
        received = exchange(packed)
        received, mixed_in = lax.optimization_barrier((received, mixed_in))
        routed, filter_rows = lax.optimization_barrier((route_call(predecessor, received), received))
        previous = exchange(routed)
    else:
        gathered = lax.all_gather(packed[None], "seq", axis=0, tiled=True)
        source = jnp.clip(predecessor[lax.axis_index("seq")], 0, count - 1)
        previous = lax.dynamic_index_in_dim(gathered, source, 0, keepdims=False)
        filter_rows = lax.all_gather(mr_filter, "seq", axis=0, tiled=True)
    mixed, squares, lines = main_call(
        group_size, stretch_lengths, queries, mixed_in, residual, short_taps, filter_rows
    )
    normed = norm_call(channels, False, stretch_lengths, shares(squares), mixed, residual, norm_gain)
    previous, normed = lax.optimization_barrier((previous, normed))
    mixed, squares = head_call(
        group_size, predecessor, stretch_lengths, previous, queries, keys_in, values_in,
        mixed_in, residual, short_taps, lines, mixed,
    )
    normed = norm_call(channels, True, stretch_lengths, shares(squares), mixed, residual, norm_gain, normed)
    return (mixed, normed)


def solution(mesh):
    in_specs = (
        P("seq", "mp"),
        P("seq", "mp"),
        P("seq", "mp"),
        P("seq", "mp"),
        P(None, None, "mp"),
        P("seq", "mp"),
        P("mp"),
        P(),
        P(),
    )
    out_specs = (P("seq", "mp"), P("seq", "mp"))
    return jax.shard_map(body, mesh=mesh, in_specs=in_specs, out_specs=out_specs, check_vma=False)
```

```python
import functools

import jax
import jax.numpy as jnp
from jax import lax
from jax.experimental import pallas as pl
from jax.experimental.pallas import tpu as pltpu
from jax.sharding import PartitionSpec as P

EPSILON = 1e-06
F32 = jnp.float32
BF16 = jnp.bfloat16
LANES = 128
STEP = 256
WIDE = 512
BLOCK = 32
WINDOW = 256
PACKED = 160
OPENING = 144
VMEM_LIMIT = 64 * 1024 * 1024


def params():
    return pltpu.CompilerParams(vmem_limit_bytes=VMEM_LIMIT)


def cost(flops, bytes_accessed):
    return pl.CostEstimate(flops=flops, bytes_accessed=bytes_accessed, transcendentals=0)


def short_conv(scratch, taps, start, rows):
    total = None
    for offset in range(taps.shape[0]):
        term = taps[offset : offset + 1] * scratch[pl.ds(start + 8 - offset, rows), :]
        total = term if total is None else total + term
    return total


def tail_kernel(packed, q_ref, k_ref, v_ref, kb_ref, vb_ref, taps_ref, filt_ref, out_ref, ks, vs):
    def piece(slot, carry):
        lasts = []
        for tile in range(STEP // LANES):
            cols = pl.ds(pl.multiple_of(slot * STEP + tile * LANES, LANES), LANES)
            here = slice(tile * LANES, (tile + 1) * LANES)
            kt, vt = ks.at[tile], vs.at[tile]
            kt[0:16, :] = kb_ref[:, cols].astype(F32)
            vt[0:16, :] = vb_ref[:, cols].astype(F32)
            kt[16:144, :] = k_ref[:, cols].astype(F32)
            vt[16:144, :] = v_ref[:, cols].astype(F32)
            key_taps = taps_ref[1, :, cols].astype(F32)
            value_taps = taps_ref[2, :, cols].astype(F32)
            for row in range(0, 128, 64):
                key = short_conv(kt, key_taps, row + 8, 64)
                value = short_conv(vt, value_taps, row + 8, 64)
                out_ref[slot, row : row + 64, here] = (key * value).astype(BF16)
            last = [q_ref[:, cols].astype(F32)[8:], kt[136:144, :], vt[136:144, :]]
            if packed:
                last.append(filt_ref[...].astype(F32)[8 * tile : 8 * tile + 8])
            else:
                last.append(jnp.zeros((8, LANES), F32))
            lasts.append(jnp.concatenate(last))
        out_ref[slot, 128:PACKED, :] = jnp.concatenate(lasts, axis=1).astype(BF16)
        return carry

    lax.fori_loop(0, out_ref.shape[0], piece, 0)


def tail_call(packed, queries, keys_in, values_in, short_taps, mr_filter):
    rows, width = queries.shape
    slots = width // STEP
    return pl.pallas_call(
        functools.partial(tail_kernel, packed),
        grid=(1,),
        in_specs=[
            pl.BlockSpec((16, width), lambda p: (rows // 16 - 1, 0)),
            pl.BlockSpec((128, width), lambda p: (rows // 128 - 1, 0)),
            pl.BlockSpec((128, width), lambda p: (rows // 128 - 1, 0)),
            pl.BlockSpec((16, width), lambda p: (rows // 16 - 9, 0)),
            pl.BlockSpec((16, width), lambda p: (rows // 16 - 9, 0)),
            pl.BlockSpec(short_taps.shape, lambda p: (0, 0, 0)),
            pl.BlockSpec(mr_filter.shape, lambda p: (0, 0)),
        ],
        out_specs=pl.BlockSpec((slots, PACKED, STEP), lambda p: (0, 0, 0)),
        out_shape=jax.ShapeDtypeStruct((slots, PACKED, STEP), BF16),
        scratch_shapes=[pltpu.VMEM((2, 144, LANES), F32), pltpu.VMEM((2, 144, LANES), F32)],
        compiler_params=params(),
        cost_estimate=cost(128 * width * 30, 128 * width * 6),
        name="tail",
    )(queries, keys_in, values_in, keys_in, values_in, short_taps, mr_filter)


def feature_kernel(k_ref, v_ref, taps_ref, out_ref, ks, vs):
    rows = k_ref.shape[0]

    def pair(index, carry):
        for tile in range(2):
            cols = pl.ds(pl.multiple_of(index * 2 * LANES + tile * LANES, LANES), LANES)
            kt, vt = ks.at[tile], vs.at[tile]
            kt[0:8, :] = jnp.zeros((8, LANES), F32)
            vt[0:8, :] = jnp.zeros((8, LANES), F32)
            kt[8 : rows + 8, :] = k_ref[:, cols].astype(F32)
            vt[8 : rows + 8, :] = v_ref[:, cols].astype(F32)
            key_taps = taps_ref[1, :, cols].astype(F32)
            value_taps = taps_ref[2, :, cols].astype(F32)
            for row in range(0, rows, 64):
                key = short_conv(kt, key_taps, row, 64)
                value = short_conv(vt, value_taps, row, 64)
                out_ref[row : row + 64, cols] = (key * value).astype(BF16)
        return carry

    lax.fori_loop(0, k_ref.shape[1] // (2 * LANES), pair, 0)


def feature_call(keys_in, values_in, short_taps):
    rows, width = keys_in.shape
    block = pl.BlockSpec((rows, WIDE), lambda p: (0, p))
    return pl.pallas_call(
        feature_kernel,
        grid=(width // WIDE,),
        in_specs=[block, block, pl.BlockSpec((3, 7, WIDE), lambda p: (0, 0, p))],
        out_specs=block,
        out_shape=jax.ShapeDtypeStruct((rows, width), BF16),
        scratch_shapes=[pltpu.VMEM((2, rows + 8, LANES), F32), pltpu.VMEM((2, rows + 8, LANES), F32)],
        compiler_params=params(),
        cost_estimate=cost(rows * width * 30, rows * width * 6),
        name="features",
    )(keys_in, values_in, short_taps)


def route_kernel(pred_ref, in_ref, out_ref, sems):
    copies = []
    for j in range(in_ref.shape[0]):
        source = jnp.maximum(pred_ref[j], 0)
        copies.append(pltpu.make_async_copy(in_ref.at[source], out_ref.at[j], sems.at[j]))
        copies[-1].start()
    for copy in copies:
        copy.wait()


def route_call(predecessor, received):
    return pl.pallas_call(
        route_kernel,
        in_specs=[pl.BlockSpec(memory_space=pltpu.SMEM), pl.BlockSpec(memory_space=pl.ANY)],
        out_specs=pl.BlockSpec(memory_space=pltpu.VMEM),
        out_shape=jax.ShapeDtypeStruct(received.shape, BF16),
        scratch_shapes=[pltpu.SemaphoreType.DMA((received.shape[0],))],
        compiler_params=params(),
        cost_estimate=cost(0, received.size * 4),
        name="route",
    )(predecessor, received)


def all_taps(filt_ref):
    if len(filt_ref.shape) == 2:
        return filt_ref[...]
    rows = []
    for j in range(filt_ref.shape[0]):
        last = filt_ref[j].astype(F32)[8:]
        rows += [last[:, :LANES], last[:, LANES:]]
    return jnp.concatenate(rows).astype(BF16)


def spread_taps(filter_rows):
    shape = (filter_rows.shape[0], WINDOW)
    tap = lax.broadcasted_iota(jnp.int32, shape, 0)
    place = lax.broadcasted_iota(jnp.int32, shape, 1)
    onehot = (place == WINDOW - BLOCK - tap).astype(BF16)
    return lax.dot_general(filter_rows, onehot, (((0,), (0,)), ((), ())), preferred_element_type=F32)


def toeplitz(lines):
    blocks = []
    for g in range(lines.shape[0]):
        line = jnp.broadcast_to(lines[g : g + 1], (BLOCK, WINDOW))
        blocks.append(pltpu.roll(line, 0, 1, stride=1, stride_axis=0).astype(BF16))
    return jnp.concatenate(blocks)


def pick_groups(result, group_size, rows=BLOCK):
    shape = (rows, result.shape[1])
    group = (lax.broadcasted_iota(jnp.int32, shape, 1) & (LANES - 1)) // group_size
    picked = result[:rows]
    for g in range(1, LANES // group_size):
        picked = jnp.where(group == g, result[g * rows : (g + 1) * rows], picked)
    return picked


def main_kernel(group_size, len_ref, q_ref, u_ref, res_ref, taps_ref, filt_ref, mixed_ref, sum_ref, lines_ref, qs, acc):
    step = pl.program_id(0)
    rows = q_ref.shape[0]
    per_lane = LANES // group_size
    length = len_ref[lax.axis_index("seq")]

    @pl.when(step == 0)
    def _():
        lines_ref[...] = spread_taps(all_taps(filt_ref))
        acc[...] = jnp.zeros_like(acc)

    mixed_ref[0:128, :] = jnp.zeros((128, WIDE), BF16)

    def pair(index, carry):
        for tile in range(2):
            number = index * 2 + tile
            cols = pl.ds(pl.multiple_of(number * LANES, LANES), LANES)
            qt = qs.at[tile]
            qt[0:8, :] = jnp.zeros((8, LANES), F32)
            qt[8 : rows + 8, :] = q_ref[:, cols].astype(F32)
            query_taps = taps_ref[0, :, cols].astype(F32)
            base = pl.multiple_of((step * (WIDE // LANES) + number) * per_lane, per_lane)
            matrix = toeplitz(lines_ref[pl.ds(base, per_lane), :])
            for start in range(128, rows, 2 * BLOCK):
                windows = []
                for first in (start, start + BLOCK):
                    low = first + BLOCK - WINDOW
                    if low < 0:
                        windows.append(
                            jnp.concatenate([jnp.zeros((-low, LANES), BF16), u_ref[0 : first + BLOCK, cols]])
                        )
                    else:
                        windows.append(u_ref[low : first + BLOCK, cols])
                result = jnp.dot(matrix, jnp.concatenate(windows, axis=1), preferred_element_type=F32)
                picked = pick_groups(result, group_size)
                filtered = jnp.concatenate([picked[:, :LANES], picked[:, LANES:]])
                query = short_conv(qt, query_taps, start, 2 * BLOCK)
                row = lax.broadcasted_iota(jnp.int32, (2 * BLOCK, LANES), 0) + start
                mixed = jnp.where(row < length, query * filtered, 0.0).astype(BF16)
                mixed_ref[start : start + 2 * BLOCK, cols] = mixed
                summed = res_ref[start : start + 2 * BLOCK, cols].astype(F32) + mixed.astype(F32)
                acc[start - 128 : start - 128 + 2 * BLOCK, :] += summed * summed
        return carry

    lax.fori_loop(0, WIDE // (2 * LANES), pair, 0)

    @pl.when(step == pl.num_programs(0) - 1)
    def _():
        sum_ref[...] = jnp.sum(acc[...].T, axis=0, keepdims=True)


def main_call(group_size, stretch_lengths, queries, mixed_in, residual, short_taps, filter_rows):
    rows, width = queries.shape
    groups = width // group_size
    if len(filter_rows.shape) == 2:
        filter_spec = pl.BlockSpec(filter_rows.shape, lambda p, *_: (0, 0))
    else:
        filter_spec = pl.BlockSpec((filter_rows.shape[0], 16, STEP), lambda p, *_: (0, PACKED // 16 - 1, 0))
    block = pl.BlockSpec((rows, WIDE), lambda p, *_: (0, p))
    return pl.pallas_call(
        functools.partial(main_kernel, group_size),
        grid_spec=pltpu.PrefetchScalarGridSpec(
            num_scalar_prefetch=1,
            grid=(width // WIDE,),
            in_specs=[
                block,
                block,
                block,
                pl.BlockSpec((3, 7, WIDE), lambda p, *_: (0, 0, p)),
                filter_spec,
            ],
            out_specs=[
                block,
                pl.BlockSpec((1, rows - 128), lambda p, *_: (0, 0)),
                pl.BlockSpec((groups, WINDOW), lambda p, *_: (0, 0)),
            ],
            scratch_shapes=[
                pltpu.VMEM((2, rows + 8, LANES), F32),
                pltpu.VMEM((rows - 128, LANES), F32),
            ],
        ),
        out_shape=[
            jax.ShapeDtypeStruct((rows, width), BF16),
            jax.ShapeDtypeStruct((1, rows - 128), F32),
            jax.ShapeDtypeStruct((groups, WINDOW), F32),
        ],
        compiler_params=params(),
        cost_estimate=cost(rows * width * 2 * WINDOW * 8, rows * width * 12),
        name="conv",
    )(stretch_lengths, queries, mixed_in, residual, short_taps, filter_rows)


def head_kernel(group_size, pred_ref, len_ref, held, q_ref, k_ref, v_ref, u_ref, res_ref, taps_ref, lines_ref, kept_ref, mixed_ref, sum_ref, qs, ks, vs, acc):
    del kept_ref
    step = pl.program_id(0)
    per_lane = LANES // group_size
    device = lax.axis_index("seq")
    length = len_ref[device]
    follows = pred_ref[device] >= 0

    @pl.when(step == 0)
    def _():
        acc[...] = jnp.zeros_like(acc)

    def pair(index, carry):
        for tile in range(2):
            number = index * 2 + tile
            cols = pl.ds(pl.multiple_of(number * LANES, LANES), LANES)
            here = slice(tile * LANES, (tile + 1) * LANES)
            qt, kt, vt = qs.at[tile], ks.at[tile], vs.at[tile]
            prev = jnp.where(follows, held[index, 128:PACKED, here].astype(F32), 0.0)
            qt[0:8, :] = prev[0:8]
            kt[0:8, :] = prev[8:16]
            vt[0:8, :] = prev[16:24]
            qt[8 : OPENING + 8, :] = q_ref[:, cols].astype(F32)
            kt[8:24, :] = k_ref[:, cols].astype(F32)
            vt[8:24, :] = v_ref[:, cols].astype(F32)
            query_taps = taps_ref[0, :, cols].astype(F32)
            key = short_conv(kt, taps_ref[1, :, cols].astype(F32), 0, 16)
            value = short_conv(vt, taps_ref[2, :, cols].astype(F32), 0, 16)
            opening = (key * value).astype(BF16)
            state = held[index, 0:128, here]
            state = jnp.where(follows, state, jnp.zeros_like(state))
            pad = jnp.zeros((WINDOW - BLOCK - 128, LANES), BF16)
            extended = jnp.concatenate([pad, state, opening, u_ref[16:192, cols]])
            base = pl.multiple_of(number * per_lane, per_lane)
            matrix = toeplitz(lines_ref[pl.ds(base, per_lane), :])
            parts = []
            for first in range(0, 128, 2 * BLOCK):
                windows = [extended[low : low + WINDOW] for low in (first, first + BLOCK)]
                result = jnp.dot(matrix, jnp.concatenate(windows, axis=1), preferred_element_type=F32)
                picked = pick_groups(result, group_size)
                parts.append((first, 2 * BLOCK, jnp.concatenate([picked[:, :LANES], picked[:, LANES:]])))
            edge = OPENING - 128
            edge_matrix = jnp.concatenate([matrix[g * BLOCK : g * BLOCK + edge] for g in range(per_lane)])
            edge_result = jnp.dot(edge_matrix, extended[128 : 128 + WINDOW], preferred_element_type=F32)
            parts.append((128, edge, pick_groups(edge_result, group_size, edge)))
            for first, rows, filtered in parts:
                query = short_conv(qt, query_taps, first, rows)
                row = lax.broadcasted_iota(jnp.int32, (rows, LANES), 0) + first
                mixed = jnp.where(row < length, query * filtered, 0.0).astype(BF16)
                mixed_ref[first : first + rows, cols] = mixed
                summed = res_ref[first : first + rows, cols].astype(F32) + mixed.astype(F32)
                acc[first : first + rows, :] += summed * summed
        return carry

    lax.fori_loop(0, WIDE // STEP, pair, 0)

    @pl.when(step == pl.num_programs(0) - 1)
    def _():
        sum_ref[...] = jnp.sum(acc[...].T, axis=0, keepdims=True)


def head_call(group_size, predecessor, stretch_lengths, previous, queries, keys_in, values_in, mixed_in, residual, short_taps, lines, mixed):
    rows, width = queries.shape
    per_step = WIDE // group_size
    block = pl.BlockSpec((OPENING, WIDE), lambda p, *_: (0, p))
    small = pl.BlockSpec((16, WIDE), lambda p, *_: (0, p))
    return pl.pallas_call(
        functools.partial(head_kernel, group_size),
        grid_spec=pltpu.PrefetchScalarGridSpec(
            num_scalar_prefetch=2,
            grid=(width // WIDE,),
            in_specs=[
                pl.BlockSpec((WIDE // STEP, PACKED, STEP), lambda p, *_: (p, 0, 0)),
                block,
                small,
                small,
                pl.BlockSpec((192, WIDE), lambda p, *_: (0, p)),
                block,
                pl.BlockSpec((3, 7, WIDE), lambda p, *_: (0, 0, p)),
                pl.BlockSpec((per_step, WINDOW), lambda p, *_: (p, 0)),
                pl.BlockSpec(memory_space=pl.ANY),
            ],
            out_specs=[block, pl.BlockSpec((1, 256), lambda p, *_: (0, 0))],
            scratch_shapes=[
                pltpu.VMEM((2, OPENING + 8, LANES), F32),
                pltpu.VMEM((2, 24, LANES), F32),
                pltpu.VMEM((2, 24, LANES), F32),
                pltpu.VMEM((256, LANES), F32),
            ],
        ),
        out_shape=[
            jax.ShapeDtypeStruct((rows, width), BF16),
            jax.ShapeDtypeStruct((1, 256), F32),
        ],
        input_output_aliases={10: 0},
        compiler_params=params(),
        cost_estimate=cost(128 * width * 2 * WINDOW * 8, 128 * width * 12),
        name="head",
    )(predecessor, stretch_lengths, previous, queries, keys_in, values_in, mixed_in, residual, short_taps, lines, mixed)


def norm_kernel(channels, first_block, sums, len_ref, *refs):
    sum_refs, (mixed_ref, res_ref, gain_ref), out_ref = refs[:sums], refs[sums : sums + 3], refs[-1]
    rows = mixed_ref.shape[0]
    first = (pl.program_id(0) + first_block) * rows
    length = len_ref[lax.axis_index("seq")]
    total = sum_refs[0][...]
    for ref in sum_refs[1:]:
        total = total + ref[...]
    scale = jnp.broadcast_to(lax.rsqrt(total / channels + EPSILON), (LANES, total.shape[1])).T[:rows]
    scale = jnp.where(lax.broadcasted_iota(jnp.int32, (rows, LANES), 0) + first < length, scale, 0.0)
    for lane in range(0, mixed_ref.shape[1], LANES):
        cols = slice(lane, lane + LANES)
        gain = gain_ref[:, cols].astype(F32)
        summed = res_ref[:, cols].astype(F32) + mixed_ref[:, cols].astype(F32)
        out_ref[:, cols] = (summed * scale * gain).astype(BF16)


def norm_call(channels, opening, stretch_lengths, totals, mixed, residual, gain, normed=None):
    rows, width = mixed.shape
    size, first_block, steps, lanes = (OPENING, 0, 1, 256) if opening else (128, 1, rows // 128 - 1, 128)
    block = pl.BlockSpec((size, width), lambda p, *_: (p + first_block, 0))
    operands = [*totals, mixed, residual, gain]
    in_specs = [pl.BlockSpec((1, lanes), lambda p, *_: (0, p))] * len(totals)
    in_specs += [block, block, pl.BlockSpec((1, width), lambda p, *_: (0, 0))]
    aliases = {}
    if normed is not None:
        aliases = {len(operands) + 1: 0}
        operands.append(normed)
        in_specs.append(pl.BlockSpec(memory_space=pl.ANY))
    return pl.pallas_call(
        functools.partial(norm_kernel, channels, first_block, len(totals)),
        grid_spec=pltpu.PrefetchScalarGridSpec(
            num_scalar_prefetch=1, grid=(steps,), in_specs=in_specs, out_specs=block
        ),
        out_shape=jax.ShapeDtypeStruct((rows, width), BF16),
        input_output_aliases=aliases,
        compiler_params=params(),
        cost_estimate=cost(steps * size * width * 6, steps * size * width * 6),
        name="norm_opening" if opening else "norm",
    )(stretch_lengths, *operands)


def swap(array, axis, distance):
    size = lax.axis_size(axis)
    return lax.ppermute(array, axis, [(i, i ^ distance) for i in range(size)])


def exchange(pieces):
    return lax.all_to_all(pieces, "seq", split_axis=0, concat_axis=0, tiled=True)


def shares(squares):
    parts = lax.axis_size("mp")
    if parts != 4:
        return [lax.psum(squares, "mp")]
    return [squares] + [swap(squares, "mp", k) for k in range(1, parts)]


def body(queries, keys_in, values_in, residual, short_taps, mr_filter, norm_gain, predecessor, stretch_lengths):
    rows, width = queries.shape
    count = lax.axis_size("seq")
    channels = width * lax.axis_size("mp")
    group_size = width // mr_filter.shape[1]
    two_phase = width // STEP == count == 8 and mr_filter.shape == (16, LANES)
    gain = norm_gain.reshape(1, width)
    packed = tail_call(two_phase, queries, keys_in, values_in, short_taps, mr_filter)
    mixed_in = feature_call(keys_in, values_in, short_taps)
    if two_phase:
        received = exchange(packed)
        received, mixed_in, gain = lax.optimization_barrier((received, mixed_in, gain))
        routed, filter_rows = lax.optimization_barrier((route_call(predecessor, received), received))
        previous = exchange(routed)
    else:
        gathered = lax.all_gather(packed[None], "seq", axis=0, tiled=True)
        source = jnp.clip(predecessor[lax.axis_index("seq")], 0, count - 1)
        previous = lax.dynamic_index_in_dim(gathered, source, 0, keepdims=False)
        filter_rows = lax.all_gather(mr_filter, "seq", axis=0, tiled=True)
    mixed, squares, lines = main_call(
        group_size, stretch_lengths, queries, mixed_in, residual, short_taps, filter_rows
    )
    normed = norm_call(channels, False, stretch_lengths, shares(squares), mixed, residual, gain)
    previous, normed = lax.optimization_barrier((previous, normed))
    mixed, squares = head_call(
        group_size, predecessor, stretch_lengths, previous, queries, keys_in, values_in,
        mixed_in, residual, short_taps, lines, mixed,
    )
    normed = norm_call(channels, True, stretch_lengths, shares(squares), mixed, residual, gain, normed)
    return (mixed, normed)


def solution(mesh):
    in_specs = (
        P("seq", "mp"),
        P("seq", "mp"),
        P("seq", "mp"),
        P("seq", "mp"),
        P(None, None, "mp"),
        P("seq", "mp"),
        P("mp"),
        P(),
        P(),
    )
    out_specs = (P("seq", "mp"), P("seq", "mp"))
    return jax.shard_map(body, mesh=mesh, in_specs=in_specs, out_specs=out_specs, check_vma=False)
```

```python
import functools

import jax
import jax.numpy as jnp
from jax import lax
from jax.experimental import pallas as pl
from jax.experimental.pallas import tpu as pltpu
from jax.sharding import PartitionSpec as P

EPSILON = 1e-06
F32 = jnp.float32
BF16 = jnp.bfloat16
LANES = 128
STEP = 256
WIDE = 512
BLOCK = 32
WINDOW = 256
PACKED = 160
OPENING = 144
VMEM_LIMIT = 64 * 1024 * 1024


def params():
    return pltpu.CompilerParams(vmem_limit_bytes=VMEM_LIMIT)


def cost(flops, bytes_accessed):
    return pl.CostEstimate(flops=flops, bytes_accessed=bytes_accessed, transcendentals=0)


def short_conv(scratch, taps, start, rows):
    total = None
    for offset in range(taps.shape[0]):
        term = taps[offset : offset + 1] * scratch[pl.ds(start + 8 - offset, rows), :]
        total = term if total is None else total + term
    return total


def tail_kernel(packed, q_ref, k_ref, v_ref, kb_ref, vb_ref, taps_ref, filt_ref, out_ref, ks, vs):
    def piece(slot, carry):
        lasts = []
        for tile in range(STEP // LANES):
            cols = pl.ds(pl.multiple_of(slot * STEP + tile * LANES, LANES), LANES)
            here = slice(tile * LANES, (tile + 1) * LANES)
            kt, vt = ks.at[tile], vs.at[tile]
            kt[0:16, :] = kb_ref[:, cols].astype(F32)
            vt[0:16, :] = vb_ref[:, cols].astype(F32)
            kt[16:144, :] = k_ref[:, cols].astype(F32)
            vt[16:144, :] = v_ref[:, cols].astype(F32)
            key_taps = taps_ref[1, :, cols].astype(F32)
            value_taps = taps_ref[2, :, cols].astype(F32)
            for row in range(0, 128, 64):
                key = short_conv(kt, key_taps, row + 8, 64)
                value = short_conv(vt, value_taps, row + 8, 64)
                out_ref[slot, row : row + 64, here] = (key * value).astype(BF16)
            last = [q_ref[:, cols].astype(F32)[8:], kt[136:144, :], vt[136:144, :]]
            if packed:
                last.append(filt_ref[...].astype(F32)[8 * tile : 8 * tile + 8])
            else:
                last.append(jnp.zeros((8, LANES), F32))
            lasts.append(jnp.concatenate(last))
        out_ref[slot, 128:PACKED, :] = jnp.concatenate(lasts, axis=1).astype(BF16)
        return carry

    lax.fori_loop(0, out_ref.shape[0], piece, 0)


def tail_call(packed, queries, keys_in, values_in, short_taps, mr_filter):
    rows, width = queries.shape
    slots = width // STEP
    return pl.pallas_call(
        functools.partial(tail_kernel, packed),
        grid=(1,),
        in_specs=[
            pl.BlockSpec((16, width), lambda p: (rows // 16 - 1, 0)),
            pl.BlockSpec((128, width), lambda p: (rows // 128 - 1, 0)),
            pl.BlockSpec((128, width), lambda p: (rows // 128 - 1, 0)),
            pl.BlockSpec((16, width), lambda p: (rows // 16 - 9, 0)),
            pl.BlockSpec((16, width), lambda p: (rows // 16 - 9, 0)),
            pl.BlockSpec(short_taps.shape, lambda p: (0, 0, 0)),
            pl.BlockSpec(mr_filter.shape, lambda p: (0, 0)),
        ],
        out_specs=pl.BlockSpec((slots, PACKED, STEP), lambda p: (0, 0, 0)),
        out_shape=jax.ShapeDtypeStruct((slots, PACKED, STEP), BF16),
        scratch_shapes=[pltpu.VMEM((2, 144, LANES), F32), pltpu.VMEM((2, 144, LANES), F32)],
        compiler_params=params(),
        cost_estimate=cost(128 * width * 30, 128 * width * 6),
        name="tail",
    )(queries, keys_in, values_in, keys_in, values_in, short_taps, mr_filter)


def feature_kernel(q_ref, k_ref, v_ref, taps_ref, out_ref, opening_ref, later_ref, qs, ks, vs):
    rows = k_ref.shape[0]

    def pair(index, carry):
        for tile in range(2):
            cols = pl.ds(pl.multiple_of(index * 2 * LANES + tile * LANES, LANES), LANES)
            scratches = (qs.at[tile], ks.at[tile], vs.at[tile])
            taps = [taps_ref[i, :, cols].astype(F32) for i in range(3)]
            for scratch, ref in zip(scratches, (q_ref, k_ref, v_ref)):
                scratch[0:8, :] = jnp.zeros((8, LANES), F32)
                scratch[8 : rows + 8, :] = ref[:, cols].astype(F32)
            for row in range(0, rows, 64):
                query, key, value = [short_conv(x, t, row, 64) for x, t in zip(scratches, taps)]
                out_ref[row : row + 64, cols] = (key * value).astype(BF16)
                if row < OPENING:
                    count = min(64, OPENING - row)
                    opening_ref[row : row + count, cols] = query[:count]
                if row >= 128:
                    later_ref[row - 128 : row - 64, cols] = query
        return carry

    lax.fori_loop(0, k_ref.shape[1] // (2 * LANES), pair, 0)


def feature_call(queries, keys_in, values_in, short_taps):
    rows, width = keys_in.shape
    heights = (rows, OPENING, rows - 128)
    blocks = [pl.BlockSpec((height, WIDE), lambda p: (0, p)) for height in heights]
    scratch = pltpu.VMEM((2, rows + 8, LANES), F32)
    return pl.pallas_call(
        feature_kernel,
        grid=(width // WIDE,),
        in_specs=[blocks[0]] * 3 + [pl.BlockSpec((3, 7, WIDE), lambda p: (0, 0, p))],
        out_specs=blocks,
        out_shape=[
            jax.ShapeDtypeStruct((height, width), kind) for height, kind in zip(heights, (BF16, F32, F32))
        ],
        scratch_shapes=[scratch] * 3,
        compiler_params=params(),
        cost_estimate=cost(rows * width * 45, rows * width * 13),
        name="features",
    )(queries, keys_in, values_in, short_taps)


def route_kernel(pred_ref, in_ref, out_ref):
    for j in range(in_ref.shape[0]):
        out_ref[j] = in_ref[jnp.maximum(pred_ref[j], 0)]


def route_call(predecessor, received):
    return pl.pallas_call(
        route_kernel,
        in_specs=[pl.BlockSpec(memory_space=pltpu.SMEM), pl.BlockSpec(memory_space=pltpu.VMEM)],
        out_specs=pl.BlockSpec(memory_space=pltpu.VMEM),
        out_shape=jax.ShapeDtypeStruct(received.shape, BF16),
        compiler_params=params(),
        cost_estimate=cost(0, received.size * 4),
        name="route",
    )(predecessor, received)


def all_taps(filt_ref):
    if len(filt_ref.shape) == 2:
        return filt_ref[...]
    rows = []
    for j in range(filt_ref.shape[0]):
        last = filt_ref[j].astype(F32)[8:]
        rows += [last[:, :LANES], last[:, LANES:]]
    return jnp.concatenate(rows).astype(BF16)


def spread_taps(filter_rows):
    shape = (filter_rows.shape[0], WINDOW)
    tap = lax.broadcasted_iota(jnp.int32, shape, 0)
    place = lax.broadcasted_iota(jnp.int32, shape, 1)
    onehot = (place == WINDOW - BLOCK - tap).astype(BF16)
    return lax.dot_general(filter_rows, onehot, (((0,), (0,)), ((), ())), preferred_element_type=F32)


def toeplitz(lines):
    blocks = []
    for g in range(lines.shape[0]):
        line = jnp.broadcast_to(lines[g : g + 1], (BLOCK, WINDOW))
        blocks.append(pltpu.roll(line, 0, 1, stride=1, stride_axis=0).astype(BF16))
    return jnp.concatenate(blocks)


def pick_groups(result, group_size, rows=BLOCK):
    shape = (rows, result.shape[1])
    group = (lax.broadcasted_iota(jnp.int32, shape, 1) & (LANES - 1)) // group_size
    picked = result[:rows]
    for g in range(1, LANES // group_size):
        picked = jnp.where(group == g, result[g * rows : (g + 1) * rows], picked)
    return picked


def main_kernel(group_size, len_ref, query_ref, u_ref, res_ref, filt_ref, mixed_ref, sum_ref, lines_ref, acc):
    step = pl.program_id(0)
    rows = u_ref.shape[0]
    per_lane = LANES // group_size
    length = len_ref[lax.axis_index("seq")]

    @pl.when(step == 0)
    def _():
        lines_ref[...] = spread_taps(all_taps(filt_ref))
        acc[...] = jnp.zeros_like(acc)

    mixed_ref[0:128, :] = jnp.zeros((128, WIDE), BF16)

    def pair(index, carry):
        for tile in range(2):
            number = index * 2 + tile
            cols = pl.ds(pl.multiple_of(number * LANES, LANES), LANES)
            base = pl.multiple_of((step * (WIDE // LANES) + number) * per_lane, per_lane)
            matrix = toeplitz(lines_ref[pl.ds(base, per_lane), :])
            for start in range(128, rows, 2 * BLOCK):
                windows = []
                for first in (start, start + BLOCK):
                    low = first + BLOCK - WINDOW
                    if low < 0:
                        windows.append(
                            jnp.concatenate([jnp.zeros((-low, LANES), BF16), u_ref[0 : first + BLOCK, cols]])
                        )
                    else:
                        windows.append(u_ref[low : first + BLOCK, cols])
                result = jnp.dot(matrix, jnp.concatenate(windows, axis=1), preferred_element_type=F32)
                picked = pick_groups(result, group_size)
                filtered = jnp.concatenate([picked[:, :LANES], picked[:, LANES:]])
                query = query_ref[start - 128 : start - 128 + 2 * BLOCK, cols]
                row = lax.broadcasted_iota(jnp.int32, (2 * BLOCK, LANES), 0) + start
                mixed = jnp.where(row < length, query * filtered, 0.0).astype(BF16)
                mixed_ref[start : start + 2 * BLOCK, cols] = mixed
                summed = res_ref[start : start + 2 * BLOCK, cols].astype(F32) + mixed.astype(F32)
                acc[start - 128 : start - 128 + 2 * BLOCK, :] += summed * summed
        return carry

    lax.fori_loop(0, WIDE // (2 * LANES), pair, 0)

    @pl.when(step == pl.num_programs(0) - 1)
    def _():
        sum_ref[...] = jnp.sum(acc[...].T, axis=0, keepdims=True)


def main_call(group_size, stretch_lengths, query_later, mixed_in, residual, filter_rows):
    rows, width = residual.shape
    groups = width // group_size
    if len(filter_rows.shape) == 2:
        filter_spec = pl.BlockSpec(filter_rows.shape, lambda p, *_: (0, 0))
    else:
        filter_spec = pl.BlockSpec((filter_rows.shape[0], 16, STEP), lambda p, *_: (0, PACKED // 16 - 1, 0))
    block = pl.BlockSpec((rows, WIDE), lambda p, *_: (0, p))
    return pl.pallas_call(
        functools.partial(main_kernel, group_size),
        grid_spec=pltpu.PrefetchScalarGridSpec(
            num_scalar_prefetch=1,
            grid=(width // WIDE,),
            in_specs=[
                pl.BlockSpec((rows - 128, WIDE), lambda p, *_: (0, p)),
                block,
                block,
                filter_spec,
            ],
            out_specs=[
                block,
                pl.BlockSpec((1, rows - 128), lambda p, *_: (0, 0)),
                pl.BlockSpec((groups, WINDOW), lambda p, *_: (0, 0)),
            ],
            scratch_shapes=[
                pltpu.VMEM((rows - 128, LANES), F32),
            ],
        ),
        out_shape=[
            jax.ShapeDtypeStruct((rows, width), BF16),
            jax.ShapeDtypeStruct((1, rows - 128), F32),
            jax.ShapeDtypeStruct((groups, WINDOW), F32),
        ],
        compiler_params=params(),
        cost_estimate=cost(rows * width * 2 * WINDOW * 8, rows * width * 12),
        name="conv",
    )(stretch_lengths, query_later, mixed_in, residual, filter_rows)


def head_kernel(group_size, pred_ref, len_ref, held, query_ref, q_ref, k_ref, v_ref, u_ref, res_ref, taps_ref, lines_ref, kept_ref, mixed_ref, sum_ref, qs, ks, vs, acc):
    del kept_ref
    step = pl.program_id(0)
    per_lane = LANES // group_size
    device = lax.axis_index("seq")
    length = len_ref[device]
    follows = pred_ref[device] >= 0

    @pl.when(step == 0)
    def _():
        acc[...] = jnp.zeros_like(acc)

    def pair(index, carry):
        for tile in range(2):
            number = index * 2 + tile
            cols = pl.ds(pl.multiple_of(number * LANES, LANES), LANES)
            here = slice(tile * LANES, (tile + 1) * LANES)
            qt, kt, vt = qs.at[tile], ks.at[tile], vs.at[tile]
            prev = jnp.where(follows, held[index, 128:PACKED, here].astype(F32), 0.0)
            qt[0:8, :] = prev[0:8]
            kt[0:8, :] = prev[8:16]
            vt[0:8, :] = prev[16:24]
            qt[8:24, :] = q_ref[:, cols].astype(F32)
            kt[8:24, :] = k_ref[:, cols].astype(F32)
            vt[8:24, :] = v_ref[:, cols].astype(F32)
            first_query = short_conv(qt, taps_ref[0, :, cols].astype(F32), 0, 16)
            key = short_conv(kt, taps_ref[1, :, cols].astype(F32), 0, 16)
            value = short_conv(vt, taps_ref[2, :, cols].astype(F32), 0, 16)
            opening = (key * value).astype(BF16)
            state = held[index, 0:128, here]
            state = jnp.where(follows, state, jnp.zeros_like(state))
            pad = jnp.zeros((WINDOW - BLOCK - 128, LANES), BF16)
            extended = jnp.concatenate([pad, state, opening, u_ref[16:192, cols]])
            base = pl.multiple_of(number * per_lane, per_lane)
            matrix = toeplitz(lines_ref[pl.ds(base, per_lane), :])
            parts = []
            for first in range(0, 128, 2 * BLOCK):
                windows = [extended[low : low + WINDOW] for low in (first, first + BLOCK)]
                result = jnp.dot(matrix, jnp.concatenate(windows, axis=1), preferred_element_type=F32)
                picked = pick_groups(result, group_size)
                parts.append((first, 2 * BLOCK, jnp.concatenate([picked[:, :LANES], picked[:, LANES:]])))
            edge = OPENING - 128
            edge_matrix = jnp.concatenate([matrix[g * BLOCK : g * BLOCK + edge] for g in range(per_lane)])
            edge_result = jnp.dot(edge_matrix, extended[128 : 128 + WINDOW], preferred_element_type=F32)
            parts.append((128, edge, pick_groups(edge_result, group_size, edge)))
            for first, rows, filtered in parts:
                query = query_ref[first : first + rows, cols]
                if first == 0:
                    query = jnp.concatenate([first_query, query[16:]])
                row = lax.broadcasted_iota(jnp.int32, (rows, LANES), 0) + first
                mixed = jnp.where(row < length, query * filtered, 0.0).astype(BF16)
                mixed_ref[first : first + rows, cols] = mixed
                summed = res_ref[first : first + rows, cols].astype(F32) + mixed.astype(F32)
                acc[first : first + rows, :] += summed * summed
        return carry

    lax.fori_loop(0, WIDE // STEP, pair, 0)

    @pl.when(step == pl.num_programs(0) - 1)
    def _():
        sum_ref[...] = jnp.sum(acc[...].T, axis=0, keepdims=True)


def head_call(group_size, predecessor, stretch_lengths, previous, query_opening, queries, keys_in, values_in, mixed_in, residual, short_taps, lines, mixed):
    rows, width = queries.shape
    per_step = WIDE // group_size
    block = pl.BlockSpec((OPENING, WIDE), lambda p, *_: (0, p))
    small = pl.BlockSpec((16, WIDE), lambda p, *_: (0, p))
    return pl.pallas_call(
        functools.partial(head_kernel, group_size),
        grid_spec=pltpu.PrefetchScalarGridSpec(
            num_scalar_prefetch=2,
            grid=(width // WIDE,),
            in_specs=[
                pl.BlockSpec((WIDE // STEP, PACKED, STEP), lambda p, *_: (p, 0, 0)),
                block,
                small,
                small,
                small,
                pl.BlockSpec((192, WIDE), lambda p, *_: (0, p)),
                block,
                pl.BlockSpec((3, 7, WIDE), lambda p, *_: (0, 0, p)),
                pl.BlockSpec((per_step, WINDOW), lambda p, *_: (p, 0)),
                pl.BlockSpec(memory_space=pl.ANY),
            ],
            out_specs=[block, pl.BlockSpec((1, 256), lambda p, *_: (0, 0))],
            scratch_shapes=[
                pltpu.VMEM((2, 24, LANES), F32),
                pltpu.VMEM((2, 24, LANES), F32),
                pltpu.VMEM((2, 24, LANES), F32),
                pltpu.VMEM((256, LANES), F32),
            ],
        ),
        out_shape=[
            jax.ShapeDtypeStruct((rows, width), BF16),
            jax.ShapeDtypeStruct((1, 256), F32),
        ],
        input_output_aliases={11: 0},
        compiler_params=params(),
        cost_estimate=cost(128 * width * 2 * WINDOW * 8, 128 * width * 12),
        name="head",
    )(predecessor, stretch_lengths, previous, query_opening, queries, keys_in, values_in, mixed_in, residual, short_taps, lines, mixed)


def norm_kernel(channels, first_block, sums, len_ref, *refs):
    sum_refs, (mixed_ref, res_ref, gain_ref), out_ref = refs[:sums], refs[sums : sums + 3], refs[-1]
    rows = mixed_ref.shape[0]
    first = (pl.program_id(0) + first_block) * rows
    length = len_ref[lax.axis_index("seq")]
    total = sum_refs[0][...]
    for ref in sum_refs[1:]:
        total = total + ref[...]
    scale = jnp.broadcast_to(lax.rsqrt(total / channels + EPSILON), (LANES, total.shape[1])).T[:rows]
    scale = jnp.where(lax.broadcasted_iota(jnp.int32, (rows, LANES), 0) + first < length, scale, 0.0)
    for lane in range(0, mixed_ref.shape[1], LANES):
        cols = slice(lane, lane + LANES)
        gain = gain_ref[:, cols].astype(F32)
        summed = res_ref[:, cols].astype(F32) + mixed_ref[:, cols].astype(F32)
        out_ref[:, cols] = (summed * scale * gain).astype(BF16)


def norm_call(channels, opening, stretch_lengths, totals, mixed, residual, gain, normed=None):
    rows, width = mixed.shape
    size, first_block, steps, lanes = (OPENING, 0, 1, 256) if opening else (128, 1, rows // 128 - 1, 128)
    block = pl.BlockSpec((size, width), lambda p, *_: (p + first_block, 0))
    operands = [*totals, mixed, residual, gain]
    in_specs = [pl.BlockSpec((1, lanes), lambda p, *_: (0, p))] * len(totals)
    in_specs += [block, block, pl.BlockSpec((1, width), lambda p, *_: (0, 0))]
    aliases = {}
    if normed is not None:
        aliases = {len(operands) + 1: 0}
        operands.append(normed)
        in_specs.append(pl.BlockSpec(memory_space=pl.ANY))
    return pl.pallas_call(
        functools.partial(norm_kernel, channels, first_block, len(totals)),
        grid_spec=pltpu.PrefetchScalarGridSpec(
            num_scalar_prefetch=1, grid=(steps,), in_specs=in_specs, out_specs=block
        ),
        out_shape=jax.ShapeDtypeStruct((rows, width), BF16),
        input_output_aliases=aliases,
        compiler_params=params(),
        cost_estimate=cost(steps * size * width * 6, steps * size * width * 6),
        name="norm_opening" if opening else "norm",
    )(stretch_lengths, *operands)


def swap(array, axis, distance):
    size = lax.axis_size(axis)
    return lax.ppermute(array, axis, [(i, i ^ distance) for i in range(size)])


def exchange(pieces):
    return lax.all_to_all(pieces, "seq", split_axis=0, concat_axis=0, tiled=True)


def shares(squares):
    parts = lax.axis_size("mp")
    if parts != 4:
        return [lax.psum(squares, "mp")]
    return [squares] + [swap(squares, "mp", k) for k in range(1, parts)]


def body(queries, keys_in, values_in, residual, short_taps, mr_filter, norm_gain, predecessor, stretch_lengths):
    rows, width = queries.shape
    count = lax.axis_size("seq")
    channels = width * lax.axis_size("mp")
    group_size = width // mr_filter.shape[1]
    two_phase = width // STEP == count == 8 and mr_filter.shape == (16, LANES)
    gain = norm_gain.reshape(1, width)
    packed = tail_call(two_phase, queries, keys_in, values_in, short_taps, mr_filter)
    mixed_in, query_opening, query_later = feature_call(queries, keys_in, values_in, short_taps)
    if two_phase:
        received = exchange(packed)
        received, mixed_in, gain = lax.optimization_barrier((received, mixed_in, gain))
        routed, filter_rows = lax.optimization_barrier((route_call(predecessor, received), received))
        previous = exchange(routed)
    else:
        gathered = lax.all_gather(packed[None], "seq", axis=0, tiled=True)
        source = jnp.clip(predecessor[lax.axis_index("seq")], 0, count - 1)
        previous = lax.dynamic_index_in_dim(gathered, source, 0, keepdims=False)
        filter_rows = lax.all_gather(mr_filter, "seq", axis=0, tiled=True)
    mixed, squares, lines = main_call(
        group_size, stretch_lengths, query_later, mixed_in, residual, filter_rows
    )
    normed = norm_call(channels, False, stretch_lengths, shares(squares), mixed, residual, gain)
    previous, normed = lax.optimization_barrier((previous, normed))
    mixed, squares = head_call(
        group_size, predecessor, stretch_lengths, previous, query_opening, queries, keys_in, values_in,
        mixed_in, residual, short_taps, lines, mixed,
    )
    normed = norm_call(channels, True, stretch_lengths, shares(squares), mixed, residual, gain, normed)
    return (mixed, normed)


def solution(mesh):
    in_specs = (
        P("seq", "mp"),
        P("seq", "mp"),
        P("seq", "mp"),
        P("seq", "mp"),
        P(None, None, "mp"),
        P("seq", "mp"),
        P("mp"),
        P(),
        P(),
    )
    out_specs = (P("seq", "mp"), P("seq", "mp"))
    return jax.shard_map(body, mesh=mesh, in_specs=in_specs, out_specs=out_specs, check_vma=False)
```

```python
import functools

import jax
import jax.numpy as jnp
from jax import lax
from jax.experimental import pallas as pl
from jax.experimental.pallas import tpu as pltpu
from jax.sharding import PartitionSpec as P

EPSILON = 1e-06
F32 = jnp.float32
BF16 = jnp.bfloat16
LANES = 128
STEP = 256
WIDE = 512
SIDE = 4
BLOCK = 32
WINDOW = 256
PACKED = 160
OPENING = 144
VMEM_LIMIT = 64 * 1024 * 1024


def unfold(picked):
    return jnp.concatenate([picked[:, i * LANES : (i + 1) * LANES] for i in range(picked.shape[1] // LANES)])


def params():
    return pltpu.CompilerParams(vmem_limit_bytes=VMEM_LIMIT)


def cost(flops, bytes_accessed):
    return pl.CostEstimate(flops=flops, bytes_accessed=bytes_accessed, transcendentals=0)


def short_conv(scratch, taps, start, rows):
    total = None
    for offset in range(taps.shape[0]):
        term = taps[offset : offset + 1] * scratch[pl.ds(start + 8 - offset, rows), :]
        total = term if total is None else total + term
    return total


def tail_kernel(packed, q_ref, k_ref, v_ref, kb_ref, vb_ref, taps_ref, filt_ref, out_ref, ks, vs):
    def piece(slot, carry):
        lasts = []
        for tile in range(STEP // LANES):
            cols = pl.ds(pl.multiple_of(slot * STEP + tile * LANES, LANES), LANES)
            here = slice(tile * LANES, (tile + 1) * LANES)
            kt, vt = ks.at[tile], vs.at[tile]
            kt[0:16, :] = kb_ref[:, cols].astype(F32)
            vt[0:16, :] = vb_ref[:, cols].astype(F32)
            kt[16:144, :] = k_ref[:, cols].astype(F32)
            vt[16:144, :] = v_ref[:, cols].astype(F32)
            key_taps = taps_ref[1, :, cols].astype(F32)
            value_taps = taps_ref[2, :, cols].astype(F32)
            for row in range(0, 128, 64):
                key = short_conv(kt, key_taps, row + 8, 64)
                value = short_conv(vt, value_taps, row + 8, 64)
                out_ref[slot, row : row + 64, here] = (key * value).astype(BF16)
            last = [q_ref[:, cols].astype(F32)[8:], kt[136:144, :], vt[136:144, :]]
            if packed:
                last.append(filt_ref[...].astype(F32)[8 * tile : 8 * tile + 8])
            else:
                last.append(jnp.zeros((8, LANES), F32))
            lasts.append(jnp.concatenate(last))
        out_ref[slot, 128:PACKED, :] = jnp.concatenate(lasts, axis=1).astype(BF16)
        return carry

    lax.fori_loop(0, out_ref.shape[0], piece, 0)


def tail_call(packed, queries, keys_in, values_in, short_taps, mr_filter):
    rows, width = queries.shape
    slots = width // STEP
    return pl.pallas_call(
        functools.partial(tail_kernel, packed),
        grid=(1,),
        in_specs=[
            pl.BlockSpec((16, width), lambda p: (rows // 16 - 1, 0)),
            pl.BlockSpec((128, width), lambda p: (rows // 128 - 1, 0)),
            pl.BlockSpec((128, width), lambda p: (rows // 128 - 1, 0)),
            pl.BlockSpec((16, width), lambda p: (rows // 16 - 9, 0)),
            pl.BlockSpec((16, width), lambda p: (rows // 16 - 9, 0)),
            pl.BlockSpec(short_taps.shape, lambda p: (0, 0, 0)),
            pl.BlockSpec(mr_filter.shape, lambda p: (0, 0)),
        ],
        out_specs=pl.BlockSpec((slots, PACKED, STEP), lambda p: (0, 0, 0)),
        out_shape=jax.ShapeDtypeStruct((slots, PACKED, STEP), BF16),
        scratch_shapes=[pltpu.VMEM((2, 144, LANES), F32), pltpu.VMEM((2, 144, LANES), F32)],
        compiler_params=params(),
        cost_estimate=cost(128 * width * 30, 128 * width * 6),
        name="tail",
    )(queries, keys_in, values_in, keys_in, values_in, short_taps, mr_filter)


def feature_kernel(q_ref, k_ref, v_ref, taps_ref, out_ref, opening_ref, later_ref, qs, ks, vs):
    rows = k_ref.shape[0]

    def pair(index, carry):
        for tile in range(2):
            cols = pl.ds(pl.multiple_of(index * 2 * LANES + tile * LANES, LANES), LANES)
            scratches = (qs.at[tile], ks.at[tile], vs.at[tile])
            taps = [taps_ref[i, :, cols].astype(F32) for i in range(3)]
            for scratch, ref in zip(scratches, (q_ref, k_ref, v_ref)):
                scratch[0:8, :] = jnp.zeros((8, LANES), F32)
                scratch[8 : rows + 8, :] = ref[:, cols].astype(F32)
            for row in range(0, rows, 64):
                query, key, value = [short_conv(x, t, row, 64) for x, t in zip(scratches, taps)]
                out_ref[row : row + 64, cols] = (key * value).astype(BF16)
                if row < OPENING:
                    count = min(64, OPENING - row)
                    opening_ref[row : row + count, cols] = query[:count]
                if row >= 128:
                    later_ref[row - 128 : row - 64, cols] = query
        return carry

    lax.fori_loop(0, k_ref.shape[1] // (2 * LANES), pair, 0)


def feature_call(queries, keys_in, values_in, short_taps):
    rows, width = keys_in.shape
    heights = (rows, OPENING, rows - 128)
    blocks = [pl.BlockSpec((height, WIDE), lambda p: (0, p)) for height in heights]
    scratch = pltpu.VMEM((2, rows + 8, LANES), F32)
    return pl.pallas_call(
        feature_kernel,
        grid=(width // WIDE,),
        in_specs=[blocks[0]] * 3 + [pl.BlockSpec((3, 7, WIDE), lambda p: (0, 0, p))],
        out_specs=blocks,
        out_shape=[
            jax.ShapeDtypeStruct((height, width), kind) for height, kind in zip(heights, (BF16, F32, F32))
        ],
        scratch_shapes=[scratch] * 3,
        compiler_params=params(),
        cost_estimate=cost(rows * width * 45, rows * width * 13),
        name="features",
    )(queries, keys_in, values_in, short_taps)


def route_kernel(pred_ref, in_ref, out_ref):
    for j in range(in_ref.shape[0]):
        out_ref[j] = in_ref[jnp.maximum(pred_ref[j], 0)]


def route_call(predecessor, received):
    return pl.pallas_call(
        route_kernel,
        in_specs=[pl.BlockSpec(memory_space=pltpu.SMEM), pl.BlockSpec(memory_space=pltpu.VMEM)],
        out_specs=pl.BlockSpec(memory_space=pltpu.VMEM),
        out_shape=jax.ShapeDtypeStruct(received.shape, BF16),
        compiler_params=params(),
        cost_estimate=cost(0, received.size * 4),
        name="route",
    )(predecessor, received)


def all_taps(filt_ref):
    if len(filt_ref.shape) == 2:
        return filt_ref[...]
    rows = []
    for j in range(filt_ref.shape[0]):
        last = filt_ref[j].astype(F32)[8:]
        rows += [last[:, :LANES], last[:, LANES:]]
    return jnp.concatenate(rows).astype(BF16)


def spread_taps(filter_rows):
    shape = (filter_rows.shape[0], WINDOW)
    tap = lax.broadcasted_iota(jnp.int32, shape, 0)
    place = lax.broadcasted_iota(jnp.int32, shape, 1)
    onehot = (place == WINDOW - BLOCK - tap).astype(BF16)
    return lax.dot_general(filter_rows, onehot, (((0,), (0,)), ((), ())), preferred_element_type=F32)


def toeplitz(lines):
    blocks = []
    for g in range(lines.shape[0]):
        line = jnp.broadcast_to(lines[g : g + 1], (BLOCK, WINDOW))
        blocks.append(pltpu.roll(line, 0, 1, stride=1, stride_axis=0).astype(BF16))
    return jnp.concatenate(blocks)


def pick_groups(result, group_size, rows=BLOCK):
    shape = (rows, result.shape[1])
    group = (lax.broadcasted_iota(jnp.int32, shape, 1) & (LANES - 1)) // group_size
    picked = result[:rows]
    for g in range(1, LANES // group_size):
        picked = jnp.where(group == g, result[g * rows : (g + 1) * rows], picked)
    return picked


def main_kernel(group_size, len_ref, query_ref, u_ref, res_ref, filt_ref, mixed_ref, sum_ref, lines_ref, acc):
    step = pl.program_id(0)
    rows = u_ref.shape[0]
    per_lane = LANES // group_size
    length = len_ref[lax.axis_index("seq")]

    @pl.when(step == 0)
    def _():
        lines_ref[...] = spread_taps(all_taps(filt_ref))
        acc[...] = jnp.zeros_like(acc)

    def pair(index, carry):
        for tile in range(2):
            number = index * 2 + tile
            cols = pl.ds(pl.multiple_of(number * LANES, LANES), LANES)
            base = pl.multiple_of((step * (WIDE // LANES) + number) * per_lane, per_lane)
            matrix = toeplitz(lines_ref[pl.ds(base, per_lane), :])
            for start in range(128, rows, SIDE * BLOCK):
                windows = []
                for first in range(start, start + SIDE * BLOCK, BLOCK):
                    low = first + BLOCK - WINDOW
                    if low < 0:
                        windows.append(
                            jnp.concatenate([jnp.zeros((-low, LANES), BF16), u_ref[0 : first + BLOCK, cols]])
                        )
                    else:
                        windows.append(u_ref[low : first + BLOCK, cols])
                result = jnp.dot(matrix, jnp.concatenate(windows, axis=1), preferred_element_type=F32)
                picked = pick_groups(result, group_size)
                filtered = unfold(picked)
                here = slice(start - 128, start - 128 + SIDE * BLOCK)
                row = lax.broadcasted_iota(jnp.int32, filtered.shape, 0) + start
                mixed = jnp.where(row < length, query_ref[here, cols] * filtered, 0.0).astype(BF16)
                mixed_ref[here, cols] = mixed
                summed = res_ref[here, cols].astype(F32) + mixed.astype(F32)
                acc[here, :] += summed * summed
        return carry

    lax.fori_loop(0, WIDE // (2 * LANES), pair, 0)

    @pl.when(step == pl.num_programs(0) - 1)
    def _():
        sum_ref[...] = jnp.sum(acc[...].T, axis=0, keepdims=True)


def main_call(group_size, stretch_lengths, query_later, mixed_in, residual, filter_rows):
    rows, width = residual.shape
    groups = width // group_size
    if len(filter_rows.shape) == 2:
        filter_spec = pl.BlockSpec(filter_rows.shape, lambda p, *_: (0, 0))
    else:
        filter_spec = pl.BlockSpec((filter_rows.shape[0], 16, STEP), lambda p, *_: (0, PACKED // 16 - 1, 0))
    block = pl.BlockSpec((rows, WIDE), lambda p, *_: (0, p))
    later = pl.BlockSpec((pl.Element(rows - 128), pl.Element(WIDE)), lambda p, *_: (128, p * WIDE))
    return pl.pallas_call(
        functools.partial(main_kernel, group_size),
        grid_spec=pltpu.PrefetchScalarGridSpec(
            num_scalar_prefetch=1,
            grid=(width // WIDE,),
            in_specs=[
                pl.BlockSpec((rows - 128, WIDE), lambda p, *_: (0, p)),
                block,
                later,
                filter_spec,
            ],
            out_specs=[
                later,
                pl.BlockSpec((1, rows - 128), lambda p, *_: (0, 0)),
                pl.BlockSpec((groups, WINDOW), lambda p, *_: (0, 0)),
            ],
            scratch_shapes=[
                pltpu.VMEM((rows - 128, LANES), F32),
            ],
        ),
        out_shape=[
            jax.ShapeDtypeStruct((rows, width), BF16),
            jax.ShapeDtypeStruct((1, rows - 128), F32),
            jax.ShapeDtypeStruct((groups, WINDOW), F32),
        ],
        compiler_params=params(),
        cost_estimate=cost(rows * width * 2 * WINDOW * 8, rows * width * 12),
        name="conv",
    )(stretch_lengths, query_later, mixed_in, residual, filter_rows)


def head_kernel(group_size, pred_ref, len_ref, held, query_ref, q_ref, k_ref, v_ref, u_ref, res_ref, taps_ref, lines_ref, kept_ref, mixed_ref, sum_ref, qs, ks, vs, acc):
    del kept_ref
    step = pl.program_id(0)
    per_lane = LANES // group_size
    device = lax.axis_index("seq")
    length = len_ref[device]
    follows = pred_ref[device] >= 0

    @pl.when(step == 0)
    def _():
        acc[...] = jnp.zeros_like(acc)

    def pair(index, carry):
        for tile in range(2):
            number = index * 2 + tile
            cols = pl.ds(pl.multiple_of(number * LANES, LANES), LANES)
            here = slice(tile * LANES, (tile + 1) * LANES)
            qt, kt, vt = qs.at[tile], ks.at[tile], vs.at[tile]
            prev = jnp.where(follows, held[index, 128:PACKED, here].astype(F32), 0.0)
            qt[0:8, :] = prev[0:8]
            kt[0:8, :] = prev[8:16]
            vt[0:8, :] = prev[16:24]
            qt[8:24, :] = q_ref[:, cols].astype(F32)
            kt[8:24, :] = k_ref[:, cols].astype(F32)
            vt[8:24, :] = v_ref[:, cols].astype(F32)
            first_query = short_conv(qt, taps_ref[0, :, cols].astype(F32), 0, 16)
            key = short_conv(kt, taps_ref[1, :, cols].astype(F32), 0, 16)
            value = short_conv(vt, taps_ref[2, :, cols].astype(F32), 0, 16)
            opening = (key * value).astype(BF16)
            state = held[index, 0:128, here]
            state = jnp.where(follows, state, jnp.zeros_like(state))
            pad = jnp.zeros((WINDOW - BLOCK - 128, LANES), BF16)
            extended = jnp.concatenate([pad, state, opening, u_ref[16:192, cols]])
            base = pl.multiple_of(number * per_lane, per_lane)
            matrix = toeplitz(lines_ref[pl.ds(base, per_lane), :])
            parts = []
            for first in range(0, 128, SIDE * BLOCK):
                lows = range(first, first + SIDE * BLOCK, BLOCK)
                windows = [extended[low : low + WINDOW] for low in lows]
                result = jnp.dot(matrix, jnp.concatenate(windows, axis=1), preferred_element_type=F32)
                picked = pick_groups(result, group_size)
                parts.append((first, SIDE * BLOCK, unfold(picked)))
            edge = OPENING - 128
            edge_matrix = jnp.concatenate([matrix[g * BLOCK : g * BLOCK + edge] for g in range(per_lane)])
            edge_result = jnp.dot(edge_matrix, extended[128 : 128 + WINDOW], preferred_element_type=F32)
            parts.append((128, edge, pick_groups(edge_result, group_size, edge)))
            for first, rows, filtered in parts:
                query = query_ref[first : first + rows, cols]
                if first == 0:
                    query = jnp.concatenate([first_query, query[16:]])
                row = lax.broadcasted_iota(jnp.int32, (rows, LANES), 0) + first
                mixed = jnp.where(row < length, query * filtered, 0.0).astype(BF16)
                mixed_ref[first : first + rows, cols] = mixed
                summed = res_ref[first : first + rows, cols].astype(F32) + mixed.astype(F32)
                acc[first : first + rows, :] += summed * summed
        return carry

    lax.fori_loop(0, WIDE // STEP, pair, 0)

    @pl.when(step == pl.num_programs(0) - 1)
    def _():
        sum_ref[...] = jnp.sum(acc[...].T, axis=0, keepdims=True)


def head_call(group_size, predecessor, stretch_lengths, previous, query_opening, queries, keys_in, values_in, mixed_in, residual, short_taps, lines, mixed):
    rows, width = queries.shape
    per_step = WIDE // group_size
    block = pl.BlockSpec((OPENING, WIDE), lambda p, *_: (0, p))
    small = pl.BlockSpec((16, WIDE), lambda p, *_: (0, p))
    return pl.pallas_call(
        functools.partial(head_kernel, group_size),
        grid_spec=pltpu.PrefetchScalarGridSpec(
            num_scalar_prefetch=2,
            grid=(width // WIDE,),
            in_specs=[
                pl.BlockSpec((WIDE // STEP, PACKED, STEP), lambda p, *_: (p, 0, 0)),
                block,
                small,
                small,
                small,
                pl.BlockSpec((192, WIDE), lambda p, *_: (0, p)),
                block,
                pl.BlockSpec((3, 7, WIDE), lambda p, *_: (0, 0, p)),
                pl.BlockSpec((per_step, WINDOW), lambda p, *_: (p, 0)),
                pl.BlockSpec(memory_space=pl.ANY),
            ],
            out_specs=[block, pl.BlockSpec((1, 256), lambda p, *_: (0, 0))],
            scratch_shapes=[
                pltpu.VMEM((2, 24, LANES), F32),
                pltpu.VMEM((2, 24, LANES), F32),
                pltpu.VMEM((2, 24, LANES), F32),
                pltpu.VMEM((256, LANES), F32),
            ],
        ),
        out_shape=[
            jax.ShapeDtypeStruct((rows, width), BF16),
            jax.ShapeDtypeStruct((1, 256), F32),
        ],
        input_output_aliases={11: 0},
        compiler_params=params(),
        cost_estimate=cost(128 * width * 2 * WINDOW * 8, 128 * width * 12),
        name="head",
    )(predecessor, stretch_lengths, previous, query_opening, queries, keys_in, values_in, mixed_in, residual, short_taps, lines, mixed)


def norm_kernel(channels, first_block, sums, len_ref, *refs):
    sum_refs, (mixed_ref, res_ref, gain_ref), out_ref = refs[:sums], refs[sums : sums + 3], refs[-1]
    rows = mixed_ref.shape[0]
    first = (pl.program_id(0) + first_block) * rows
    length = len_ref[lax.axis_index("seq")]
    total = sum_refs[0][...]
    for ref in sum_refs[1:]:
        total = total + ref[...]
    scale = jnp.broadcast_to(lax.rsqrt(total / channels + EPSILON), (LANES, total.shape[1])).T[:rows]
    scale = jnp.where(lax.broadcasted_iota(jnp.int32, (rows, LANES), 0) + first < length, scale, 0.0)
    for lane in range(0, mixed_ref.shape[1], LANES):
        cols = slice(lane, lane + LANES)
        gain = gain_ref[:, cols].astype(F32)
        summed = res_ref[:, cols].astype(F32) + mixed_ref[:, cols].astype(F32)
        out_ref[:, cols] = (summed * scale * gain).astype(BF16)


def norm_call(channels, opening, stretch_lengths, totals, mixed, residual, gain, normed=None):
    rows, width = mixed.shape
    size, first_block, steps, lanes = (OPENING, 0, 1, 256) if opening else (128, 1, rows // 128 - 1, 128)
    block = pl.BlockSpec((size, width), lambda p, *_: (p + first_block, 0))
    operands = [*totals, mixed, residual, gain]
    in_specs = [pl.BlockSpec((1, lanes), lambda p, *_: (0, p))] * len(totals)
    in_specs += [block, block, pl.BlockSpec((1, width), lambda p, *_: (0, 0))]
    aliases = {}
    if normed is not None:
        aliases = {len(operands) + 1: 0}
        operands.append(normed)
        in_specs.append(pl.BlockSpec(memory_space=pl.ANY))
    return pl.pallas_call(
        functools.partial(norm_kernel, channels, first_block, len(totals)),
        grid_spec=pltpu.PrefetchScalarGridSpec(
            num_scalar_prefetch=1, grid=(steps,), in_specs=in_specs, out_specs=block
        ),
        out_shape=jax.ShapeDtypeStruct((rows, width), BF16),
        input_output_aliases=aliases,
        compiler_params=params(),
        cost_estimate=cost(steps * size * width * 6, steps * size * width * 6),
        name="norm_opening" if opening else "norm",
    )(stretch_lengths, *operands)


def swap(array, axis, distance):
    size = lax.axis_size(axis)
    return lax.ppermute(array, axis, [(i, i ^ distance) for i in range(size)])


def exchange(pieces):
    return lax.all_to_all(pieces, "seq", split_axis=0, concat_axis=0, tiled=True)


def shares(squares):
    parts = lax.axis_size("mp")
    if parts != 4:
        return [lax.psum(squares, "mp")]
    return [squares] + [swap(squares, "mp", k) for k in range(1, parts)]


def body(queries, keys_in, values_in, residual, short_taps, mr_filter, norm_gain, predecessor, stretch_lengths):
    rows, width = queries.shape
    count = lax.axis_size("seq")
    channels = width * lax.axis_size("mp")
    group_size = width // mr_filter.shape[1]
    two_phase = width // STEP == count == 8 and mr_filter.shape == (16, LANES)
    gain = norm_gain.reshape(1, width)
    packed = tail_call(two_phase, queries, keys_in, values_in, short_taps, mr_filter)
    mixed_in, query_opening, query_later = feature_call(queries, keys_in, values_in, short_taps)
    if two_phase:
        received = exchange(packed)
        received, mixed_in, gain = lax.optimization_barrier((received, mixed_in, gain))
        routed, filter_rows = lax.optimization_barrier((route_call(predecessor, received), received))
        previous = exchange(routed)
    else:
        gathered = lax.all_gather(packed[None], "seq", axis=0, tiled=True)
        source = jnp.clip(predecessor[lax.axis_index("seq")], 0, count - 1)
        previous = lax.dynamic_index_in_dim(gathered, source, 0, keepdims=False)
        filter_rows = lax.all_gather(mr_filter, "seq", axis=0, tiled=True)
    mixed, squares, lines = main_call(
        group_size, stretch_lengths, query_later, mixed_in, residual, filter_rows
    )
    normed = norm_call(channels, False, stretch_lengths, shares(squares), mixed, residual, gain)
    previous, normed = lax.optimization_barrier((previous, normed))
    mixed, squares = head_call(
        group_size, predecessor, stretch_lengths, previous, query_opening, queries, keys_in, values_in,
        mixed_in, residual, short_taps, lines, mixed,
    )
    normed = norm_call(channels, True, stretch_lengths, shares(squares), mixed, residual, gain, normed)
    return (mixed, normed)


def solution(mesh):
    in_specs = (
        P("seq", "mp"),
        P("seq", "mp"),
        P("seq", "mp"),
        P("seq", "mp"),
        P(None, None, "mp"),
        P("seq", "mp"),
        P("mp"),
        P(),
        P(),
    )
    out_specs = (P("seq", "mp"), P("seq", "mp"))
    return jax.shard_map(body, mesh=mesh, in_specs=in_specs, out_specs=out_specs, check_vma=False)
```

```python
import functools

import jax
import jax.numpy as jnp
from jax import lax
from jax.experimental import pallas as pl
from jax.experimental.pallas import tpu as pltpu
from jax.sharding import PartitionSpec as P

EPSILON = 1e-06
F32 = jnp.float32
BF16 = jnp.bfloat16
LANES = 128
STEP = 256
WIDE = 512
SIDE = 4
BLOCK = 32
WINDOW = 256
PACKED = 160
OPENING = 144
VMEM_LIMIT = 64 * 1024 * 1024


def unfold(picked):
    return jnp.concatenate([picked[:, i * LANES : (i + 1) * LANES] for i in range(picked.shape[1] // LANES)])


def params():
    return pltpu.CompilerParams(vmem_limit_bytes=VMEM_LIMIT)


def cost(flops, bytes_accessed):
    return pl.CostEstimate(flops=flops, bytes_accessed=bytes_accessed, transcendentals=0)


def short_conv(scratch, taps, start, rows):
    total = None
    for offset in range(taps.shape[0]):
        term = taps[offset : offset + 1] * scratch[pl.ds(start + 8 - offset, rows), :]
        total = term if total is None else total + term
    return total


def tail_kernel(packed, q_ref, k_ref, v_ref, kb_ref, vb_ref, taps_ref, filt_ref, out_ref, ks, vs):
    def piece(slot, carry):
        lasts = []
        for tile in range(STEP // LANES):
            cols = pl.ds(pl.multiple_of(slot * STEP + tile * LANES, LANES), LANES)
            here = slice(tile * LANES, (tile + 1) * LANES)
            kt, vt = ks.at[tile], vs.at[tile]
            kt[0:16, :] = kb_ref[:, cols].astype(F32)
            vt[0:16, :] = vb_ref[:, cols].astype(F32)
            kt[16:144, :] = k_ref[:, cols].astype(F32)
            vt[16:144, :] = v_ref[:, cols].astype(F32)
            key_taps = taps_ref[1, :, cols].astype(F32)
            value_taps = taps_ref[2, :, cols].astype(F32)
            for row in range(0, 128, 64):
                key = short_conv(kt, key_taps, row + 8, 64)
                value = short_conv(vt, value_taps, row + 8, 64)
                out_ref[slot, row : row + 64, here] = (key * value).astype(BF16)
            last = [q_ref[:, cols].astype(F32)[8:], kt[136:144, :], vt[136:144, :]]
            if packed:
                last.append(filt_ref[...].astype(F32)[8 * tile : 8 * tile + 8])
            else:
                last.append(jnp.zeros((8, LANES), F32))
            lasts.append(jnp.concatenate(last))
        out_ref[slot, 128:PACKED, :] = jnp.concatenate(lasts, axis=1).astype(BF16)
        return carry

    lax.fori_loop(0, out_ref.shape[0], piece, 0)


def tail_call(packed, queries, keys_in, values_in, short_taps, mr_filter):
    rows, width = queries.shape
    slots = width // STEP
    return pl.pallas_call(
        functools.partial(tail_kernel, packed),
        grid=(1,),
        in_specs=[
            pl.BlockSpec((16, width), lambda p: (rows // 16 - 1, 0)),
            pl.BlockSpec((128, width), lambda p: (rows // 128 - 1, 0)),
            pl.BlockSpec((128, width), lambda p: (rows // 128 - 1, 0)),
            pl.BlockSpec((16, width), lambda p: (rows // 16 - 9, 0)),
            pl.BlockSpec((16, width), lambda p: (rows // 16 - 9, 0)),
            pl.BlockSpec(short_taps.shape, lambda p: (0, 0, 0)),
            pl.BlockSpec(mr_filter.shape, lambda p: (0, 0)),
        ],
        out_specs=pl.BlockSpec((slots, PACKED, STEP), lambda p: (0, 0, 0)),
        out_shape=jax.ShapeDtypeStruct((slots, PACKED, STEP), BF16),
        scratch_shapes=[pltpu.VMEM((2, 144, LANES), F32), pltpu.VMEM((2, 144, LANES), F32)],
        compiler_params=params(),
        cost_estimate=cost(128 * width * 30, 128 * width * 6),
        name="tail",
    )(queries, keys_in, values_in, keys_in, values_in, short_taps, mr_filter)


def feature_kernel(q_ref, k_ref, v_ref, taps_ref, out_ref, opening_ref, later_ref, qs, ks, vs):
    rows = k_ref.shape[0]

    def pair(index, carry):
        for tile in range(2):
            cols = pl.ds(pl.multiple_of(index * 2 * LANES + tile * LANES, LANES), LANES)
            scratches = (qs.at[tile], ks.at[tile], vs.at[tile])
            taps = [taps_ref[i, :, cols].astype(F32) for i in range(3)]
            for scratch, ref in zip(scratches, (q_ref, k_ref, v_ref)):
                scratch[0:8, :] = jnp.zeros((8, LANES), F32)
                scratch[8 : rows + 8, :] = ref[:, cols].astype(F32)
            for row in range(0, rows, 64):
                query, key, value = [short_conv(x, t, row, 64) for x, t in zip(scratches, taps)]
                out_ref[row : row + 64, cols] = (key * value).astype(BF16)
                if row < OPENING:
                    count = min(64, OPENING - row)
                    opening_ref[row : row + count, cols] = query[:count]
                if row >= 128:
                    later_ref[row - 128 : row - 64, cols] = query
        return carry

    lax.fori_loop(0, k_ref.shape[1] // (2 * LANES), pair, 0)


def feature_call(queries, keys_in, values_in, short_taps):
    rows, width = keys_in.shape
    heights = (rows, OPENING, rows - 128)
    blocks = [pl.BlockSpec((height, WIDE), lambda p: (0, p)) for height in heights]
    scratch = pltpu.VMEM((2, rows + 8, LANES), F32)
    return pl.pallas_call(
        feature_kernel,
        grid=(width // WIDE,),
        in_specs=[blocks[0]] * 3 + [pl.BlockSpec((3, 7, WIDE), lambda p: (0, 0, p))],
        out_specs=blocks,
        out_shape=[
            jax.ShapeDtypeStruct((height, width), kind) for height, kind in zip(heights, (BF16, F32, F32))
        ],
        scratch_shapes=[scratch] * 3,
        compiler_params=params(),
        cost_estimate=cost(rows * width * 45, rows * width * 13),
        name="features",
    )(queries, keys_in, values_in, short_taps)


def route_kernel(pred_ref, in_ref, out_ref):
    for j in range(in_ref.shape[0]):
        out_ref[j] = in_ref[jnp.maximum(pred_ref[j], 0)]


def route_call(predecessor, received):
    return pl.pallas_call(
        route_kernel,
        in_specs=[pl.BlockSpec(memory_space=pltpu.SMEM), pl.BlockSpec(memory_space=pltpu.VMEM)],
        out_specs=pl.BlockSpec(memory_space=pltpu.VMEM),
        out_shape=jax.ShapeDtypeStruct(received.shape, BF16),
        compiler_params=params(),
        cost_estimate=cost(0, received.size * 4),
        name="route",
    )(predecessor, received)


def all_taps(filt_ref):
    if len(filt_ref.shape) == 2:
        return filt_ref[...]
    rows = []
    for j in range(filt_ref.shape[0]):
        last = filt_ref[j].astype(F32)[8:]
        rows += [last[:, :LANES], last[:, LANES:]]
    return jnp.concatenate(rows).astype(BF16)


def spread_taps(filter_rows):
    shape = (filter_rows.shape[0], WINDOW)
    tap = lax.broadcasted_iota(jnp.int32, shape, 0)
    place = lax.broadcasted_iota(jnp.int32, shape, 1)
    onehot = (place == WINDOW - BLOCK - tap).astype(BF16)
    return lax.dot_general(filter_rows, onehot, (((0,), (0,)), ((), ())), preferred_element_type=F32)


def toeplitz(lines):
    blocks = []
    for g in range(lines.shape[0]):
        line = jnp.broadcast_to(lines[g : g + 1], (BLOCK, WINDOW))
        blocks.append(pltpu.roll(line, 0, 1, stride=1, stride_axis=0).astype(BF16))
    return jnp.concatenate(blocks)


def pick_groups(result, group_size, rows=BLOCK):
    shape = (rows, result.shape[1])
    group = (lax.broadcasted_iota(jnp.int32, shape, 1) & (LANES - 1)) // group_size
    picked = result[:rows]
    for g in range(1, LANES // group_size):
        picked = jnp.where(group == g, result[g * rows : (g + 1) * rows], picked)
    return picked


def main_kernel(group_size, len_ref, query_ref, u_ref, res_ref, filt_ref, mixed_ref, sum_ref, lines_ref, acc):
    step = pl.program_id(0)
    rows = u_ref.shape[0]
    per_lane = LANES // group_size
    length = len_ref[lax.axis_index("seq")]

    @pl.when(step == 0)
    def _():
        lines_ref[...] = spread_taps(all_taps(filt_ref))
        acc[...] = jnp.zeros_like(acc)

    def tiles():
        for number in range(WIDE // LANES):
            cols = slice(number * LANES, (number + 1) * LANES)
            base = pl.multiple_of((step * (WIDE // LANES) + number) * per_lane, per_lane)
            matrix = toeplitz(lines_ref[pl.ds(base, per_lane), :])
            for start in range(128, rows, SIDE * BLOCK):
                windows = []
                for first in range(start, start + SIDE * BLOCK, BLOCK):
                    low = first + BLOCK - WINDOW
                    if low < 0:
                        windows.append(
                            jnp.concatenate([jnp.zeros((-low, LANES), BF16), u_ref[0 : first + BLOCK, cols]])
                        )
                    else:
                        windows.append(u_ref[low : first + BLOCK, cols])
                result = jnp.dot(matrix, jnp.concatenate(windows, axis=1), preferred_element_type=F32)
                picked = pick_groups(result, group_size)
                filtered = unfold(picked)
                here = slice(start - 128, start - 128 + SIDE * BLOCK)
                row = lax.broadcasted_iota(jnp.int32, filtered.shape, 0) + start
                mixed = jnp.where(row < length, query_ref[here, cols] * filtered, 0.0).astype(BF16)
                mixed_ref[here, cols] = mixed
                summed = res_ref[here, cols].astype(F32) + mixed.astype(F32)
                acc[here, :] += summed * summed

    tiles()

    @pl.when(step == pl.num_programs(0) - 1)
    def _():
        sum_ref[...] = jnp.sum(acc[...].T, axis=0, keepdims=True)


def main_call(group_size, stretch_lengths, query_later, mixed_in, residual, filter_rows):
    rows, width = residual.shape
    groups = width // group_size
    if len(filter_rows.shape) == 2:
        filter_spec = pl.BlockSpec(filter_rows.shape, lambda p, *_: (0, 0))
    else:
        filter_spec = pl.BlockSpec((filter_rows.shape[0], 16, STEP), lambda p, *_: (0, PACKED // 16 - 1, 0))
    block = pl.BlockSpec((rows, WIDE), lambda p, *_: (0, p))
    later = pl.BlockSpec((pl.Element(rows - 128), pl.Element(WIDE)), lambda p, *_: (128, p * WIDE))
    return pl.pallas_call(
        functools.partial(main_kernel, group_size),
        grid_spec=pltpu.PrefetchScalarGridSpec(
            num_scalar_prefetch=1,
            grid=(width // WIDE,),
            in_specs=[
                pl.BlockSpec((rows - 128, WIDE), lambda p, *_: (0, p)),
                block,
                later,
                filter_spec,
            ],
            out_specs=[
                later,
                pl.BlockSpec((1, rows - 128), lambda p, *_: (0, 0)),
                pl.BlockSpec((groups, WINDOW), lambda p, *_: (0, 0)),
            ],
            scratch_shapes=[
                pltpu.VMEM((rows - 128, LANES), F32),
            ],
        ),
        out_shape=[
            jax.ShapeDtypeStruct((rows, width), BF16),
            jax.ShapeDtypeStruct((1, rows - 128), F32),
            jax.ShapeDtypeStruct((groups, WINDOW), F32),
        ],
        compiler_params=params(),
        cost_estimate=cost(rows * width * 2 * WINDOW * 8, rows * width * 12),
        name="conv",
    )(stretch_lengths, query_later, mixed_in, residual, filter_rows)


def head_kernel(group_size, pred_ref, len_ref, held, query_ref, q_ref, k_ref, v_ref, u_ref, res_ref, taps_ref, lines_ref, kept_ref, mixed_ref, sum_ref, qs, ks, vs, acc):
    del kept_ref
    step = pl.program_id(0)
    per_lane = LANES // group_size
    device = lax.axis_index("seq")
    length = len_ref[device]
    follows = pred_ref[device] >= 0

    @pl.when(step == 0)
    def _():
        acc[...] = jnp.zeros_like(acc)

    def tiles():
        for number in range(WIDE // LANES):
            index, tile = divmod(number, STEP // LANES)
            cols = slice(number * LANES, (number + 1) * LANES)
            here = slice(tile * LANES, (tile + 1) * LANES)
            qt, kt, vt = qs.at[number], ks.at[number], vs.at[number]
            prev = jnp.where(follows, held[index, 128:PACKED, here].astype(F32), 0.0)
            qt[0:8, :] = prev[0:8]
            kt[0:8, :] = prev[8:16]
            vt[0:8, :] = prev[16:24]
            qt[8:24, :] = q_ref[:, cols].astype(F32)
            kt[8:24, :] = k_ref[:, cols].astype(F32)
            vt[8:24, :] = v_ref[:, cols].astype(F32)
            first_query = short_conv(qt, taps_ref[0, :, cols].astype(F32), 0, 16)
            key = short_conv(kt, taps_ref[1, :, cols].astype(F32), 0, 16)
            value = short_conv(vt, taps_ref[2, :, cols].astype(F32), 0, 16)
            opening = (key * value).astype(BF16)
            state = held[index, 0:128, here]
            state = jnp.where(follows, state, jnp.zeros_like(state))
            pad = jnp.zeros((WINDOW - BLOCK - 128, LANES), BF16)
            extended = jnp.concatenate([pad, state, opening, u_ref[16:192, cols]])
            base = number * per_lane
            matrix = toeplitz(lines_ref[pl.ds(base, per_lane), :])
            parts = []
            for first in range(0, 128, SIDE * BLOCK):
                lows = range(first, first + SIDE * BLOCK, BLOCK)
                windows = [extended[low : low + WINDOW] for low in lows]
                result = jnp.dot(matrix, jnp.concatenate(windows, axis=1), preferred_element_type=F32)
                picked = pick_groups(result, group_size)
                parts.append((first, SIDE * BLOCK, unfold(picked)))
            edge = OPENING - 128
            edge_matrix = jnp.concatenate([matrix[g * BLOCK : g * BLOCK + edge] for g in range(per_lane)])
            edge_result = jnp.dot(edge_matrix, extended[128 : 128 + WINDOW], preferred_element_type=F32)
            parts.append((128, edge, pick_groups(edge_result, group_size, edge)))
            for first, rows, filtered in parts:
                query = query_ref[first : first + rows, cols]
                if first == 0:
                    query = jnp.concatenate([first_query, query[16:]])
                row = lax.broadcasted_iota(jnp.int32, (rows, LANES), 0) + first
                mixed = jnp.where(row < length, query * filtered, 0.0).astype(BF16)
                mixed_ref[first : first + rows, cols] = mixed
                summed = res_ref[first : first + rows, cols].astype(F32) + mixed.astype(F32)
                acc[first : first + rows, :] += summed * summed

    tiles()

    @pl.when(step == pl.num_programs(0) - 1)
    def _():
        sum_ref[...] = jnp.sum(acc[...].T, axis=0, keepdims=True)


def head_call(group_size, predecessor, stretch_lengths, previous, query_opening, queries, keys_in, values_in, mixed_in, residual, short_taps, lines, mixed):
    rows, width = queries.shape
    per_step = WIDE // group_size
    block = pl.BlockSpec((OPENING, WIDE), lambda p, *_: (0, p))
    small = pl.BlockSpec((16, WIDE), lambda p, *_: (0, p))
    return pl.pallas_call(
        functools.partial(head_kernel, group_size),
        grid_spec=pltpu.PrefetchScalarGridSpec(
            num_scalar_prefetch=2,
            grid=(width // WIDE,),
            in_specs=[
                pl.BlockSpec((WIDE // STEP, PACKED, STEP), lambda p, *_: (p, 0, 0)),
                block,
                small,
                small,
                small,
                pl.BlockSpec((192, WIDE), lambda p, *_: (0, p)),
                block,
                pl.BlockSpec((3, 7, WIDE), lambda p, *_: (0, 0, p)),
                pl.BlockSpec((per_step, WINDOW), lambda p, *_: (p, 0)),
                pl.BlockSpec(memory_space=pl.ANY),
            ],
            out_specs=[block, pl.BlockSpec((1, 256), lambda p, *_: (0, 0))],
            scratch_shapes=[
                pltpu.VMEM((WIDE // LANES, 24, LANES), F32),
                pltpu.VMEM((WIDE // LANES, 24, LANES), F32),
                pltpu.VMEM((WIDE // LANES, 24, LANES), F32),
                pltpu.VMEM((256, LANES), F32),
            ],
        ),
        out_shape=[
            jax.ShapeDtypeStruct((rows, width), BF16),
            jax.ShapeDtypeStruct((1, 256), F32),
        ],
        input_output_aliases={11: 0},
        compiler_params=params(),
        cost_estimate=cost(128 * width * 2 * WINDOW * 8, 128 * width * 12),
        name="head",
    )(predecessor, stretch_lengths, previous, query_opening, queries, keys_in, values_in, mixed_in, residual, short_taps, lines, mixed)


def norm_kernel(channels, first_block, sums, len_ref, *refs):
    sum_refs, (mixed_ref, res_ref, gain_ref), out_ref = refs[:sums], refs[sums : sums + 3], refs[-1]
    rows = mixed_ref.shape[0]
    first = (pl.program_id(0) + first_block) * rows
    length = len_ref[lax.axis_index("seq")]
    total = sum_refs[0][...]
    for ref in sum_refs[1:]:
        total = total + ref[...]
    scale = jnp.broadcast_to(lax.rsqrt(total / channels + EPSILON), (LANES, total.shape[1])).T[:rows]
    scale = jnp.where(lax.broadcasted_iota(jnp.int32, (rows, LANES), 0) + first < length, scale, 0.0)
    for lane in range(0, mixed_ref.shape[1], LANES):
        cols = slice(lane, lane + LANES)
        gain = gain_ref[:, cols].astype(F32)
        summed = res_ref[:, cols].astype(F32) + mixed_ref[:, cols].astype(F32)
        out_ref[:, cols] = (summed * scale * gain).astype(BF16)


def norm_call(channels, opening, stretch_lengths, totals, mixed, residual, gain, normed=None):
    rows, width = mixed.shape
    size, first_block, steps, lanes = (OPENING, 0, 1, 256) if opening else (128, 1, rows // 128 - 1, 128)
    block = pl.BlockSpec((size, width), lambda p, *_: (p + first_block, 0))
    operands = [*totals, mixed, residual, gain]
    in_specs = [pl.BlockSpec((1, lanes), lambda p, *_: (0, p))] * len(totals)
    in_specs += [block, block, pl.BlockSpec((1, width), lambda p, *_: (0, 0))]
    aliases = {}
    if normed is not None:
        aliases = {len(operands) + 1: 0}
        operands.append(normed)
        in_specs.append(pl.BlockSpec(memory_space=pl.ANY))
    return pl.pallas_call(
        functools.partial(norm_kernel, channels, first_block, len(totals)),
        grid_spec=pltpu.PrefetchScalarGridSpec(
            num_scalar_prefetch=1, grid=(steps,), in_specs=in_specs, out_specs=block
        ),
        out_shape=jax.ShapeDtypeStruct((rows, width), BF16),
        input_output_aliases=aliases,
        compiler_params=params(),
        cost_estimate=cost(steps * size * width * 6, steps * size * width * 6),
        name="norm_opening" if opening else "norm",
    )(stretch_lengths, *operands)


def swap(array, axis, distance):
    size = lax.axis_size(axis)
    return lax.ppermute(array, axis, [(i, i ^ distance) for i in range(size)])


def exchange(pieces):
    return lax.all_to_all(pieces, "seq", split_axis=0, concat_axis=0, tiled=True)


def shares(squares):
    parts = lax.axis_size("mp")
    if parts != 4:
        return [lax.psum(squares, "mp")]
    return [squares] + [swap(squares, "mp", k) for k in range(1, parts)]


def body(queries, keys_in, values_in, residual, short_taps, mr_filter, norm_gain, predecessor, stretch_lengths):
    rows, width = queries.shape
    count = lax.axis_size("seq")
    channels = width * lax.axis_size("mp")
    group_size = width // mr_filter.shape[1]
    two_phase = width // STEP == count == 8 and mr_filter.shape == (16, LANES)
    gain = norm_gain.reshape(1, width)
    packed = tail_call(two_phase, queries, keys_in, values_in, short_taps, mr_filter)
    mixed_in, query_opening, query_later = feature_call(queries, keys_in, values_in, short_taps)
    if two_phase:
        received = exchange(packed)
        received, mixed_in, gain = lax.optimization_barrier((received, mixed_in, gain))
        routed, filter_rows = lax.optimization_barrier((route_call(predecessor, received), received))
        previous = exchange(routed)
    else:
        gathered = lax.all_gather(packed[None], "seq", axis=0, tiled=True)
        source = jnp.clip(predecessor[lax.axis_index("seq")], 0, count - 1)
        previous = lax.dynamic_index_in_dim(gathered, source, 0, keepdims=False)
        filter_rows = lax.all_gather(mr_filter, "seq", axis=0, tiled=True)
    mixed, squares, lines = main_call(
        group_size, stretch_lengths, query_later, mixed_in, residual, filter_rows
    )
    normed = norm_call(channels, False, stretch_lengths, shares(squares), mixed, residual, gain)
    previous, normed = lax.optimization_barrier((previous, normed))
    mixed, squares = head_call(
        group_size, predecessor, stretch_lengths, previous, query_opening, queries, keys_in, values_in,
        mixed_in, residual, short_taps, lines, mixed,
    )
    normed = norm_call(channels, True, stretch_lengths, shares(squares), mixed, residual, gain, normed)
    return (mixed, normed)


def solution(mesh):
    in_specs = (
        P("seq", "mp"),
        P("seq", "mp"),
        P("seq", "mp"),
        P("seq", "mp"),
        P(None, None, "mp"),
        P("seq", "mp"),
        P("mp"),
        P(),
        P(),
    )
    out_specs = (P("seq", "mp"), P("seq", "mp"))
    return jax.shard_map(body, mesh=mesh, in_specs=in_specs, out_specs=out_specs, check_vma=False)
```

```python
import functools

import jax
import jax.numpy as jnp
from jax import lax
from jax.experimental import pallas as pl
from jax.experimental.pallas import tpu as pltpu
from jax.sharding import PartitionSpec as P

EPSILON = 1e-06
F32 = jnp.float32
BF16 = jnp.bfloat16
LANES = 128
STEP = 256
WIDE = 512
SIDE = 4
BLOCK = 32
WINDOW = 256
PACKED = 160
OPENING = 144
VMEM_LIMIT = 64 * 1024 * 1024


def unfold(picked):
    return jnp.concatenate([picked[:, i * LANES : (i + 1) * LANES] for i in range(picked.shape[1] // LANES)])


def params():
    return pltpu.CompilerParams(vmem_limit_bytes=VMEM_LIMIT)


def cost(flops, bytes_accessed):
    return pl.CostEstimate(flops=flops, bytes_accessed=bytes_accessed, transcendentals=0)


def short_conv(scratch, taps, start, rows):
    total = None
    for offset in range(taps.shape[0]):
        term = taps[offset : offset + 1] * scratch[pl.ds(start + 8 - offset, rows), :]
        total = term if total is None else total + term
    return total


def tail_kernel(packed, q_ref, k_ref, v_ref, kb_ref, vb_ref, taps_ref, filt_ref, out_ref, ks, vs):
    for slot in range(out_ref.shape[0]):
        lasts = []
        for tile in range(STEP // LANES):
            number = slot * (STEP // LANES) + tile
            cols = slice(number * LANES, (number + 1) * LANES)
            here = slice(tile * LANES, (tile + 1) * LANES)
            kt, vt = ks.at[number], vs.at[number]
            kt[0:16, :] = kb_ref[:, cols].astype(F32)
            vt[0:16, :] = vb_ref[:, cols].astype(F32)
            kt[16:144, :] = k_ref[:, cols].astype(F32)
            vt[16:144, :] = v_ref[:, cols].astype(F32)
            key_taps = taps_ref[1, :, cols].astype(F32)
            value_taps = taps_ref[2, :, cols].astype(F32)
            for row in range(0, 128, 64):
                key = short_conv(kt, key_taps, row + 8, 64)
                value = short_conv(vt, value_taps, row + 8, 64)
                out_ref[slot, row : row + 64, here] = (key * value).astype(BF16)
            last = [q_ref[:, cols].astype(F32)[8:], kt[136:144, :], vt[136:144, :]]
            if packed:
                last.append(filt_ref[...].astype(F32)[8 * tile : 8 * tile + 8])
            else:
                last.append(jnp.zeros((8, LANES), F32))
            lasts.append(jnp.concatenate(last))
        out_ref[slot, 128:PACKED, :] = jnp.concatenate(lasts, axis=1).astype(BF16)


def tail_call(packed, queries, keys_in, values_in, short_taps, mr_filter):
    rows, width = queries.shape
    slots = width // STEP
    part = width // 2
    count = part // LANES
    return pl.pallas_call(
        functools.partial(tail_kernel, packed),
        grid=(2,),
        in_specs=[
            pl.BlockSpec((16, part), lambda p: (rows // 16 - 1, p)),
            pl.BlockSpec((128, part), lambda p: (rows // 128 - 1, p)),
            pl.BlockSpec((128, part), lambda p: (rows // 128 - 1, p)),
            pl.BlockSpec((16, part), lambda p: (rows // 16 - 9, p)),
            pl.BlockSpec((16, part), lambda p: (rows // 16 - 9, p)),
            pl.BlockSpec((3, 7, part), lambda p: (0, 0, p)),
            pl.BlockSpec(mr_filter.shape, lambda p: (0, 0)),
        ],
        out_specs=pl.BlockSpec((slots // 2, PACKED, STEP), lambda p: (p, 0, 0)),
        out_shape=jax.ShapeDtypeStruct((slots, PACKED, STEP), BF16),
        scratch_shapes=[pltpu.VMEM((count, 144, LANES), F32)] * 2,
        compiler_params=params(),
        cost_estimate=cost(128 * width * 30, 128 * width * 6),
        name="tail",
    )(queries, keys_in, values_in, keys_in, values_in, short_taps, mr_filter)


def feature_kernel(q_ref, k_ref, v_ref, taps_ref, out_ref, opening_ref, later_ref, qs, ks, vs):
    rows = k_ref.shape[0]

    def pair(index, carry):
        for tile in range(2):
            cols = pl.ds(pl.multiple_of(index * 2 * LANES + tile * LANES, LANES), LANES)
            scratches = (qs.at[tile], ks.at[tile], vs.at[tile])
            taps = [taps_ref[i, :, cols].astype(F32) for i in range(3)]
            for scratch, ref in zip(scratches, (q_ref, k_ref, v_ref)):
                scratch[0:8, :] = jnp.zeros((8, LANES), F32)
                scratch[8 : rows + 8, :] = ref[:, cols].astype(F32)
            for row in range(0, rows, 64):
                query, key, value = [short_conv(x, t, row, 64) for x, t in zip(scratches, taps)]
                out_ref[row : row + 64, cols] = (key * value).astype(BF16)
                if row < OPENING:
                    count = min(64, OPENING - row)
                    opening_ref[row : row + count, cols] = query[:count]
                if row >= 128:
                    later_ref[row - 128 : row - 64, cols] = query
        return carry

    lax.fori_loop(0, k_ref.shape[1] // (2 * LANES), pair, 0)


def feature_call(queries, keys_in, values_in, short_taps):
    rows, width = keys_in.shape
    heights = (rows, OPENING, rows - 128)
    blocks = [pl.BlockSpec((height, WIDE), lambda p: (0, p)) for height in heights]
    scratch = pltpu.VMEM((2, rows + 8, LANES), F32)
    return pl.pallas_call(
        feature_kernel,
        grid=(width // WIDE,),
        in_specs=[blocks[0]] * 3 + [pl.BlockSpec((3, 7, WIDE), lambda p: (0, 0, p))],
        out_specs=blocks,
        out_shape=[
            jax.ShapeDtypeStruct((height, width), kind) for height, kind in zip(heights, (BF16, F32, F32))
        ],
        scratch_shapes=[scratch] * 3,
        compiler_params=params(),
        cost_estimate=cost(rows * width * 45, rows * width * 13),
        name="features",
    )(queries, keys_in, values_in, short_taps)


def route_kernel(pred_ref, in_ref, out_ref):
    for j in range(in_ref.shape[0]):
        out_ref[j] = in_ref[jnp.maximum(pred_ref[j], 0)]


def route_call(predecessor, received):
    return pl.pallas_call(
        route_kernel,
        in_specs=[pl.BlockSpec(memory_space=pltpu.SMEM), pl.BlockSpec(memory_space=pltpu.VMEM)],
        out_specs=pl.BlockSpec(memory_space=pltpu.VMEM),
        out_shape=jax.ShapeDtypeStruct(received.shape, BF16),
        compiler_params=params(),
        cost_estimate=cost(0, received.size * 4),
        name="route",
    )(predecessor, received)


def all_taps(filt_ref):
    if len(filt_ref.shape) == 2:
        return filt_ref[...]
    rows = []
    for j in range(filt_ref.shape[0]):
        last = filt_ref[j].astype(F32)[8:]
        rows += [last[:, :LANES], last[:, LANES:]]
    return jnp.concatenate(rows).astype(BF16)


def spread_taps(filter_rows):
    shape = (filter_rows.shape[0], WINDOW)
    tap = lax.broadcasted_iota(jnp.int32, shape, 0)
    place = lax.broadcasted_iota(jnp.int32, shape, 1)
    onehot = (place == WINDOW - BLOCK - tap).astype(BF16)
    return lax.dot_general(filter_rows, onehot, (((0,), (0,)), ((), ())), preferred_element_type=F32)


def toeplitz(lines):
    blocks = []
    for g in range(lines.shape[0]):
        line = jnp.broadcast_to(lines[g : g + 1], (BLOCK, WINDOW))
        blocks.append(pltpu.roll(line, 0, 1, stride=1, stride_axis=0).astype(BF16))
    return jnp.concatenate(blocks)


def pick_groups(result, group_size, rows=BLOCK):
    shape = (rows, result.shape[1])
    group = (lax.broadcasted_iota(jnp.int32, shape, 1) & (LANES - 1)) // group_size
    picked = result[:rows]
    for g in range(1, LANES // group_size):
        picked = jnp.where(group == g, result[g * rows : (g + 1) * rows], picked)
    return picked


def main_kernel(group_size, len_ref, query_ref, u_ref, res_ref, filt_ref, mixed_ref, sum_ref, lines_ref, acc):
    step = pl.program_id(0)
    rows = u_ref.shape[0]
    per_lane = LANES // group_size
    length = len_ref[lax.axis_index("seq")]

    @pl.when(step == 0)
    def _():
        lines_ref[...] = spread_taps(all_taps(filt_ref))
        acc[...] = jnp.zeros_like(acc)

    def tiles():
        for number in range(WIDE // LANES):
            cols = slice(number * LANES, (number + 1) * LANES)
            base = pl.multiple_of((step * (WIDE // LANES) + number) * per_lane, per_lane)
            matrix = toeplitz(lines_ref[pl.ds(base, per_lane), :])
            for start in range(128, rows, SIDE * BLOCK):
                windows = []
                for first in range(start, start + SIDE * BLOCK, BLOCK):
                    low = first + BLOCK - WINDOW
                    if low < 0:
                        windows.append(
                            jnp.concatenate([jnp.zeros((-low, LANES), BF16), u_ref[0 : first + BLOCK, cols]])
                        )
                    else:
                        windows.append(u_ref[low : first + BLOCK, cols])
                result = jnp.dot(matrix, jnp.concatenate(windows, axis=1), preferred_element_type=F32)
                picked = pick_groups(result, group_size)
                filtered = unfold(picked)
                here = slice(start - 128, start - 128 + SIDE * BLOCK)
                row = lax.broadcasted_iota(jnp.int32, filtered.shape, 0) + start
                mixed = jnp.where(row < length, query_ref[here, cols] * filtered, 0.0).astype(BF16)
                mixed_ref[here, cols] = mixed
                summed = res_ref[here, cols].astype(F32) + mixed.astype(F32)
                acc[here, :] += summed * summed

    tiles()

    @pl.when(step == pl.num_programs(0) - 1)
    def _():
        sum_ref[...] = jnp.sum(acc[...].T, axis=0, keepdims=True)


def main_call(group_size, stretch_lengths, query_later, mixed_in, residual, filter_rows):
    rows, width = residual.shape
    groups = width // group_size
    if len(filter_rows.shape) == 2:
        filter_spec = pl.BlockSpec(filter_rows.shape, lambda p, *_: (0, 0))
    else:
        filter_spec = pl.BlockSpec((filter_rows.shape[0], 16, STEP), lambda p, *_: (0, PACKED // 16 - 1, 0))
    block = pl.BlockSpec((rows, WIDE), lambda p, *_: (0, p))
    later = pl.BlockSpec((pl.Element(rows - 128), pl.Element(WIDE)), lambda p, *_: (128, p * WIDE))
    return pl.pallas_call(
        functools.partial(main_kernel, group_size),
        grid_spec=pltpu.PrefetchScalarGridSpec(
            num_scalar_prefetch=1,
            grid=(width // WIDE,),
            in_specs=[
                pl.BlockSpec((rows - 128, WIDE), lambda p, *_: (0, p)),
                block,
                later,
                filter_spec,
            ],
            out_specs=[
                later,
                pl.BlockSpec((1, rows - 128), lambda p, *_: (0, 0)),
                pl.BlockSpec((groups, WINDOW), lambda p, *_: (0, 0)),
            ],
            scratch_shapes=[
                pltpu.VMEM((rows - 128, LANES), F32),
            ],
        ),
        out_shape=[
            jax.ShapeDtypeStruct((rows, width), BF16),
            jax.ShapeDtypeStruct((1, rows - 128), F32),
            jax.ShapeDtypeStruct((groups, WINDOW), F32),
        ],
        compiler_params=params(),
        cost_estimate=cost(rows * width * 2 * WINDOW * 8, rows * width * 12),
        name="conv",
    )(stretch_lengths, query_later, mixed_in, residual, filter_rows)


def head_kernel(group_size, pred_ref, len_ref, held, query_ref, q_ref, k_ref, v_ref, u_ref, res_ref, taps_ref, lines_ref, kept_ref, mixed_ref, sum_ref, qs, ks, vs, acc):
    del kept_ref
    step = pl.program_id(0)
    per_lane = LANES // group_size
    device = lax.axis_index("seq")
    length = len_ref[device]
    follows = pred_ref[device] >= 0

    @pl.when(step == 0)
    def _():
        acc[...] = jnp.zeros_like(acc)

    def tiles():
        for number in range(WIDE // LANES):
            index, tile = divmod(number, STEP // LANES)
            cols = slice(number * LANES, (number + 1) * LANES)
            here = slice(tile * LANES, (tile + 1) * LANES)
            qt, kt, vt = qs.at[number], ks.at[number], vs.at[number]
            prev = jnp.where(follows, held[index, 128:PACKED, here].astype(F32), 0.0)
            qt[0:8, :] = prev[0:8]
            kt[0:8, :] = prev[8:16]
            vt[0:8, :] = prev[16:24]
            qt[8:24, :] = q_ref[:, cols].astype(F32)
            kt[8:24, :] = k_ref[:, cols].astype(F32)
            vt[8:24, :] = v_ref[:, cols].astype(F32)
            first_query = short_conv(qt, taps_ref[0, :, cols].astype(F32), 0, 16)
            key = short_conv(kt, taps_ref[1, :, cols].astype(F32), 0, 16)
            value = short_conv(vt, taps_ref[2, :, cols].astype(F32), 0, 16)
            opening = (key * value).astype(BF16)
            state = held[index, 0:128, here]
            state = jnp.where(follows, state, jnp.zeros_like(state))
            pad = jnp.zeros((WINDOW - BLOCK - 128, LANES), BF16)
            extended = jnp.concatenate([pad, state, opening, u_ref[16:192, cols]])
            base = number * per_lane
            matrix = toeplitz(lines_ref[pl.ds(base, per_lane), :])
            parts = []
            for first in range(0, 128, SIDE * BLOCK):
                lows = range(first, first + SIDE * BLOCK, BLOCK)
                windows = [extended[low : low + WINDOW] for low in lows]
                result = jnp.dot(matrix, jnp.concatenate(windows, axis=1), preferred_element_type=F32)
                picked = pick_groups(result, group_size)
                parts.append((first, SIDE * BLOCK, unfold(picked)))
            edge = OPENING - 128
            edge_matrix = jnp.concatenate([matrix[g * BLOCK : g * BLOCK + edge] for g in range(per_lane)])
            edge_result = jnp.dot(edge_matrix, extended[128 : 128 + WINDOW], preferred_element_type=F32)
            parts.append((128, edge, pick_groups(edge_result, group_size, edge)))
            for first, rows, filtered in parts:
                query = query_ref[first : first + rows, cols]
                if first == 0:
                    query = jnp.concatenate([first_query, query[16:]])
                row = lax.broadcasted_iota(jnp.int32, (rows, LANES), 0) + first
                mixed = jnp.where(row < length, query * filtered, 0.0).astype(BF16)
                mixed_ref[first : first + rows, cols] = mixed
                summed = res_ref[first : first + rows, cols].astype(F32) + mixed.astype(F32)
                acc[first : first + rows, :] += summed * summed

    tiles()

    @pl.when(step == pl.num_programs(0) - 1)
    def _():
        sum_ref[...] = jnp.sum(acc[...].T, axis=0, keepdims=True)


def head_call(group_size, predecessor, stretch_lengths, previous, query_opening, queries, keys_in, values_in, mixed_in, residual, short_taps, lines, mixed):
    rows, width = queries.shape
    per_step = WIDE // group_size
    block = pl.BlockSpec((OPENING, WIDE), lambda p, *_: (0, p))
    small = pl.BlockSpec((16, WIDE), lambda p, *_: (0, p))
    return pl.pallas_call(
        functools.partial(head_kernel, group_size),
        grid_spec=pltpu.PrefetchScalarGridSpec(
            num_scalar_prefetch=2,
            grid=(width // WIDE,),
            in_specs=[
                pl.BlockSpec((WIDE // STEP, PACKED, STEP), lambda p, *_: (p, 0, 0)),
                block,
                small,
                small,
                small,
                pl.BlockSpec((192, WIDE), lambda p, *_: (0, p)),
                block,
                pl.BlockSpec((3, 7, WIDE), lambda p, *_: (0, 0, p)),
                pl.BlockSpec((per_step, WINDOW), lambda p, *_: (p, 0)),
                pl.BlockSpec(memory_space=pl.ANY),
            ],
            out_specs=[block, pl.BlockSpec((1, 256), lambda p, *_: (0, 0))],
            scratch_shapes=[
                pltpu.VMEM((WIDE // LANES, 24, LANES), F32),
                pltpu.VMEM((WIDE // LANES, 24, LANES), F32),
                pltpu.VMEM((WIDE // LANES, 24, LANES), F32),
                pltpu.VMEM((256, LANES), F32),
            ],
        ),
        out_shape=[
            jax.ShapeDtypeStruct((rows, width), BF16),
            jax.ShapeDtypeStruct((1, 256), F32),
        ],
        input_output_aliases={11: 0},
        compiler_params=params(),
        cost_estimate=cost(128 * width * 2 * WINDOW * 8, 128 * width * 12),
        name="head",
    )(predecessor, stretch_lengths, previous, query_opening, queries, keys_in, values_in, mixed_in, residual, short_taps, lines, mixed)


def norm_kernel(channels, first_block, sums, len_ref, *refs):
    sum_refs, (mixed_ref, res_ref, gain_ref), out_ref = refs[:sums], refs[sums : sums + 3], refs[-1]
    rows = mixed_ref.shape[0]
    first = (pl.program_id(0) + first_block) * rows
    length = len_ref[lax.axis_index("seq")]
    total = sum_refs[0][...]
    for ref in sum_refs[1:]:
        total = total + ref[...]
    scale = jnp.broadcast_to(lax.rsqrt(total / channels + EPSILON), (LANES, total.shape[1])).T[:rows]
    scale = jnp.where(lax.broadcasted_iota(jnp.int32, (rows, LANES), 0) + first < length, scale, 0.0)
    for lane in range(0, mixed_ref.shape[1], LANES):
        cols = slice(lane, lane + LANES)
        gain = gain_ref[:, cols].astype(F32)
        summed = res_ref[:, cols].astype(F32) + mixed_ref[:, cols].astype(F32)
        out_ref[:, cols] = (summed * scale * gain).astype(BF16)


def norm_call(channels, steps, first_block, stretch_lengths, totals, mixed, residual, gain, normed=None):
    rows, width = mixed.shape
    opening = first_block == 0
    size, lanes, skip = (OPENING, 256, 0) if opening else (128, 128, first_block - 1)
    block = pl.BlockSpec((size, width), lambda p, *_: (p + first_block, 0))
    operands = [*totals, mixed, residual, gain]
    in_specs = [pl.BlockSpec((1, lanes), lambda p, *_: (0, p + skip))] * len(totals)
    in_specs += [block, block, pl.BlockSpec((1, width), lambda p, *_: (0, 0))]
    aliases = {}
    if normed is not None:
        aliases = {len(operands) + 1: 0}
        operands.append(normed)
        in_specs.append(pl.BlockSpec(memory_space=pl.ANY))
    return pl.pallas_call(
        functools.partial(norm_kernel, channels, first_block, len(totals)),
        grid_spec=pltpu.PrefetchScalarGridSpec(
            num_scalar_prefetch=1, grid=(steps,), in_specs=in_specs, out_specs=block
        ),
        out_shape=jax.ShapeDtypeStruct((rows, width), BF16),
        input_output_aliases=aliases,
        compiler_params=params(),
        cost_estimate=cost(steps * size * width * 6, steps * size * width * 6),
        name="norm%d" % first_block,
    )(stretch_lengths, *operands)


def swap(array, axis, distance):
    size = lax.axis_size(axis)
    return lax.ppermute(array, axis, [(i, i ^ distance) for i in range(size)])


def exchange(pieces):
    return lax.all_to_all(pieces, "seq", split_axis=0, concat_axis=0, tiled=True)


def shares(squares):
    parts = lax.axis_size("mp")
    if parts != 4:
        return [lax.psum(squares, "mp")]
    return [squares] + [swap(squares, "mp", k) for k in range(1, parts)]


def body(queries, keys_in, values_in, residual, short_taps, mr_filter, norm_gain, predecessor, stretch_lengths):
    rows, width = queries.shape
    count = lax.axis_size("seq")
    channels = width * lax.axis_size("mp")
    group_size = width // mr_filter.shape[1]
    two_phase = width // STEP == count == 8 and mr_filter.shape == (16, LANES)
    gain = norm_gain.reshape(1, width)
    packed = tail_call(two_phase, queries, keys_in, values_in, short_taps, mr_filter)
    mixed_in, query_opening, query_later = feature_call(queries, keys_in, values_in, short_taps)
    if two_phase:
        received = exchange(packed)
        received, mixed_in, gain = lax.optimization_barrier((received, mixed_in, gain))
        routed, filter_rows = lax.optimization_barrier((route_call(predecessor, received), received))
        previous = exchange(routed)
    else:
        gathered = lax.all_gather(packed[None], "seq", axis=0, tiled=True)
        source = jnp.clip(predecessor[lax.axis_index("seq")], 0, count - 1)
        previous = lax.dynamic_index_in_dim(gathered, source, 0, keepdims=False)
        filter_rows = lax.all_gather(mr_filter, "seq", axis=0, tiled=True)
    mixed, squares, lines = main_call(
        group_size, stretch_lengths, query_later, mixed_in, residual, filter_rows
    )
    totals = shares(squares)
    early = rows // 128 - 2
    normed = norm_call(channels, early, 1, stretch_lengths, totals, mixed, residual, gain)
    previous, normed = lax.optimization_barrier((previous, normed))
    mixed, squares = head_call(
        group_size, predecessor, stretch_lengths, previous, query_opening, queries, keys_in, values_in,
        mixed_in, residual, short_taps, lines, mixed,
    )
    opening_totals = shares(squares)
    normed = norm_call(channels, 1, early + 1, stretch_lengths, totals, mixed, residual, gain, normed)
    normed = norm_call(channels, 1, 0, stretch_lengths, opening_totals, mixed, residual, gain, normed)
    return (mixed, normed)


def solution(mesh):
    in_specs = (
        P("seq", "mp"),
        P("seq", "mp"),
        P("seq", "mp"),
        P("seq", "mp"),
        P(None, None, "mp"),
        P("seq", "mp"),
        P("mp"),
        P(),
        P(),
    )
    out_specs = (P("seq", "mp"), P("seq", "mp"))
    return jax.shard_map(body, mesh=mesh, in_specs=in_specs, out_specs=out_specs, check_vma=False)
```

```python
import functools

import jax
import jax.numpy as jnp
from jax import lax
from jax.experimental import pallas as pl
from jax.experimental.pallas import tpu as pltpu
from jax.sharding import PartitionSpec as P

EPSILON = 1e-06
F32 = jnp.float32
BF16 = jnp.bfloat16
LANES = 128
STEP = 256
WIDE = 512
HEAD_WIDE = 1024
SIDE = 4
BLOCK = 32
WINDOW = 256
PACKED = 160
OPENING = 144
VMEM_LIMIT = 64 * 1024 * 1024


def unfold(picked):
    return jnp.concatenate([picked[:, i * LANES : (i + 1) * LANES] for i in range(picked.shape[1] // LANES)])


def params():
    return pltpu.CompilerParams(vmem_limit_bytes=VMEM_LIMIT)


def cost(flops, bytes_accessed):
    return pl.CostEstimate(flops=flops, bytes_accessed=bytes_accessed, transcendentals=0)


def short_conv(scratch, taps, start, rows):
    total = None
    for offset in range(taps.shape[0]):
        term = taps[offset : offset + 1] * scratch[pl.ds(start + 8 - offset, rows), :]
        total = term if total is None else total + term
    return total


def tail_kernel(packed, q_ref, k_ref, v_ref, kb_ref, vb_ref, taps_ref, filt_ref, out_ref, ks, vs):
    for slot in range(out_ref.shape[0]):
        lasts = []
        for tile in range(STEP // LANES):
            number = slot * (STEP // LANES) + tile
            cols = slice(number * LANES, (number + 1) * LANES)
            here = slice(tile * LANES, (tile + 1) * LANES)
            kt, vt = ks.at[number], vs.at[number]
            kt[0:16, :] = kb_ref[:, cols].astype(F32)
            vt[0:16, :] = vb_ref[:, cols].astype(F32)
            kt[16:144, :] = k_ref[:, cols].astype(F32)
            vt[16:144, :] = v_ref[:, cols].astype(F32)
            key_taps = taps_ref[1, :, cols].astype(F32)
            value_taps = taps_ref[2, :, cols].astype(F32)
            for row in range(0, 128, 64):
                key = short_conv(kt, key_taps, row + 8, 64)
                value = short_conv(vt, value_taps, row + 8, 64)
                out_ref[slot, row : row + 64, here] = (key * value).astype(BF16)
            last = [q_ref[:, cols].astype(F32)[8:], kt[136:144, :], vt[136:144, :]]
            if packed:
                last.append(filt_ref[...].astype(F32)[8 * tile : 8 * tile + 8])
            else:
                last.append(jnp.zeros((8, LANES), F32))
            lasts.append(jnp.concatenate(last))
        out_ref[slot, 128:PACKED, :] = jnp.concatenate(lasts, axis=1).astype(BF16)


def tail_call(packed, queries, keys_in, values_in, short_taps, mr_filter):
    rows, width = queries.shape
    slots = width // STEP
    part = width // 2
    count = part // LANES
    return pl.pallas_call(
        functools.partial(tail_kernel, packed),
        grid=(2,),
        in_specs=[
            pl.BlockSpec((16, part), lambda p: (rows // 16 - 1, p)),
            pl.BlockSpec((128, part), lambda p: (rows // 128 - 1, p)),
            pl.BlockSpec((128, part), lambda p: (rows // 128 - 1, p)),
            pl.BlockSpec((16, part), lambda p: (rows // 16 - 9, p)),
            pl.BlockSpec((16, part), lambda p: (rows // 16 - 9, p)),
            pl.BlockSpec((3, 7, part), lambda p: (0, 0, p)),
            pl.BlockSpec(mr_filter.shape, lambda p: (0, 0)),
        ],
        out_specs=pl.BlockSpec((slots // 2, PACKED, STEP), lambda p: (p, 0, 0)),
        out_shape=jax.ShapeDtypeStruct((slots, PACKED, STEP), BF16),
        scratch_shapes=[pltpu.VMEM((count, 144, LANES), F32)] * 2,
        compiler_params=params(),
        cost_estimate=cost(128 * width * 30, 128 * width * 6),
        name="tail",
    )(queries, keys_in, values_in, keys_in, values_in, short_taps, mr_filter)


def feature_kernel(q_ref, k_ref, v_ref, taps_ref, out_ref, opening_ref, later_ref, qs, ks, vs):
    rows = k_ref.shape[0]

    def pair(index, carry):
        for tile in range(2):
            cols = pl.ds(pl.multiple_of(index * 2 * LANES + tile * LANES, LANES), LANES)
            scratches = (qs.at[tile], ks.at[tile], vs.at[tile])
            taps = [taps_ref[i, :, cols].astype(F32) for i in range(3)]
            for scratch, ref in zip(scratches, (q_ref, k_ref, v_ref)):
                scratch[0:8, :] = jnp.zeros((8, LANES), F32)
                scratch[8 : rows + 8, :] = ref[:, cols].astype(F32)
            for row in range(0, rows, 64):
                query, key, value = [short_conv(x, t, row, 64) for x, t in zip(scratches, taps)]
                out_ref[row : row + 64, cols] = (key * value).astype(BF16)
                if row < OPENING:
                    count = min(64, OPENING - row)
                    opening_ref[row : row + count, cols] = query[:count]
                if row >= 128:
                    later_ref[row - 128 : row - 64, cols] = query
        return carry

    lax.fori_loop(0, k_ref.shape[1] // (2 * LANES), pair, 0)


def feature_call(queries, keys_in, values_in, short_taps):
    rows, width = keys_in.shape
    heights = (rows, OPENING, rows - 128)
    blocks = [pl.BlockSpec((height, WIDE), lambda p: (0, p)) for height in heights]
    scratch = pltpu.VMEM((2, rows + 8, LANES), F32)
    return pl.pallas_call(
        feature_kernel,
        grid=(width // WIDE,),
        in_specs=[blocks[0]] * 3 + [pl.BlockSpec((3, 7, WIDE), lambda p: (0, 0, p))],
        out_specs=blocks,
        out_shape=[
            jax.ShapeDtypeStruct((height, width), kind) for height, kind in zip(heights, (BF16, F32, F32))
        ],
        scratch_shapes=[scratch] * 3,
        compiler_params=params(),
        cost_estimate=cost(rows * width * 45, rows * width * 13),
        name="features",
    )(queries, keys_in, values_in, short_taps)


def route_kernel(pred_ref, in_ref, out_ref):
    for j in range(in_ref.shape[0]):
        out_ref[j] = in_ref[jnp.maximum(pred_ref[j], 0)]


def route_call(predecessor, received):
    return pl.pallas_call(
        route_kernel,
        in_specs=[pl.BlockSpec(memory_space=pltpu.SMEM), pl.BlockSpec(memory_space=pltpu.VMEM)],
        out_specs=pl.BlockSpec(memory_space=pltpu.VMEM),
        out_shape=jax.ShapeDtypeStruct(received.shape, BF16),
        compiler_params=params(),
        cost_estimate=cost(0, received.size * 4),
        name="route",
    )(predecessor, received)


def all_taps(filt_ref):
    if len(filt_ref.shape) == 2:
        return filt_ref[...]
    rows = []
    for j in range(filt_ref.shape[0]):
        last = filt_ref[j].astype(F32)[8:]
        rows += [last[:, :LANES], last[:, LANES:]]
    return jnp.concatenate(rows).astype(BF16)


def spread_taps(filter_rows):
    shape = (filter_rows.shape[0], WINDOW)
    tap = lax.broadcasted_iota(jnp.int32, shape, 0)
    place = lax.broadcasted_iota(jnp.int32, shape, 1)
    onehot = (place == WINDOW - BLOCK - tap).astype(BF16)
    return lax.dot_general(filter_rows, onehot, (((0,), (0,)), ((), ())), preferred_element_type=F32)


def toeplitz(lines):
    blocks = []
    for g in range(lines.shape[0]):
        line = jnp.broadcast_to(lines[g : g + 1], (BLOCK, WINDOW))
        blocks.append(pltpu.roll(line, 0, 1, stride=1, stride_axis=0).astype(BF16))
    return jnp.concatenate(blocks)


def pick_groups(result, group_size, rows=BLOCK):
    shape = (rows, result.shape[1])
    group = (lax.broadcasted_iota(jnp.int32, shape, 1) & (LANES - 1)) // group_size
    picked = result[:rows]
    for g in range(1, LANES // group_size):
        picked = jnp.where(group == g, result[g * rows : (g + 1) * rows], picked)
    return picked


def main_kernel(group_size, len_ref, query_ref, u_ref, res_ref, filt_ref, mixed_ref, sum_ref, lines_ref, acc):
    step = pl.program_id(0)
    rows = u_ref.shape[0]
    per_lane = LANES // group_size
    length = len_ref[lax.axis_index("seq")]

    @pl.when(step == 0)
    def _():
        lines_ref[...] = spread_taps(all_taps(filt_ref))
        acc[...] = jnp.zeros_like(acc)

    def tiles():
        for number in range(WIDE // LANES):
            cols = slice(number * LANES, (number + 1) * LANES)
            base = pl.multiple_of((step * (WIDE // LANES) + number) * per_lane, per_lane)
            matrix = toeplitz(lines_ref[pl.ds(base, per_lane), :])
            for start in range(128, rows, SIDE * BLOCK):
                windows = []
                for first in range(start, start + SIDE * BLOCK, BLOCK):
                    low = first + BLOCK - WINDOW
                    if low < 0:
                        windows.append(
                            jnp.concatenate([jnp.zeros((-low, LANES), BF16), u_ref[0 : first + BLOCK, cols]])
                        )
                    else:
                        windows.append(u_ref[low : first + BLOCK, cols])
                result = jnp.dot(matrix, jnp.concatenate(windows, axis=1), preferred_element_type=F32)
                picked = pick_groups(result, group_size)
                filtered = unfold(picked)
                here = slice(start - 128, start - 128 + SIDE * BLOCK)
                row = lax.broadcasted_iota(jnp.int32, filtered.shape, 0) + start
                mixed = jnp.where(row < length, query_ref[here, cols] * filtered, 0.0).astype(BF16)
                mixed_ref[here, cols] = mixed
                summed = res_ref[here, cols].astype(F32) + mixed.astype(F32)
                acc[here, :] += summed * summed

    tiles()

    @pl.when(step == pl.num_programs(0) - 1)
    def _():
        sum_ref[...] = jnp.sum(acc[...].T, axis=0, keepdims=True)


def main_call(group_size, stretch_lengths, query_later, mixed_in, residual, filter_rows):
    rows, width = residual.shape
    groups = width // group_size
    if len(filter_rows.shape) == 2:
        filter_spec = pl.BlockSpec(filter_rows.shape, lambda p, *_: (0, 0))
    else:
        filter_spec = pl.BlockSpec((filter_rows.shape[0], 16, STEP), lambda p, *_: (0, PACKED // 16 - 1, 0))
    block = pl.BlockSpec((rows, WIDE), lambda p, *_: (0, p))
    later = pl.BlockSpec((pl.Element(rows - 128), pl.Element(WIDE)), lambda p, *_: (128, p * WIDE))
    return pl.pallas_call(
        functools.partial(main_kernel, group_size),
        grid_spec=pltpu.PrefetchScalarGridSpec(
            num_scalar_prefetch=1,
            grid=(width // WIDE,),
            in_specs=[
                pl.BlockSpec((rows - 128, WIDE), lambda p, *_: (0, p)),
                block,
                later,
                filter_spec,
            ],
            out_specs=[
                later,
                pl.BlockSpec((1, rows - 128), lambda p, *_: (0, 0)),
                pl.BlockSpec((groups, WINDOW), lambda p, *_: (0, 0)),
            ],
            scratch_shapes=[
                pltpu.VMEM((rows - 128, LANES), F32),
            ],
        ),
        out_shape=[
            jax.ShapeDtypeStruct((rows, width), BF16),
            jax.ShapeDtypeStruct((1, rows - 128), F32),
            jax.ShapeDtypeStruct((groups, WINDOW), F32),
        ],
        compiler_params=params(),
        cost_estimate=cost(rows * width * 2 * WINDOW * 8, rows * width * 12),
        name="conv",
    )(stretch_lengths, query_later, mixed_in, residual, filter_rows)


def head_kernel(group_size, pred_ref, len_ref, held, query_ref, q_ref, k_ref, v_ref, u_ref, res_ref, taps_ref, lines_ref, kept_ref, mixed_ref, sum_ref, qs, ks, vs, acc):
    del kept_ref
    step = pl.program_id(0)
    per_lane = LANES // group_size
    device = lax.axis_index("seq")
    length = len_ref[device]
    follows = pred_ref[device] >= 0

    @pl.when(step == 0)
    def _():
        acc[...] = jnp.zeros_like(acc)

    def tiles():
        for number in range(HEAD_WIDE // LANES):
            index, tile = divmod(number, STEP // LANES)
            cols = slice(number * LANES, (number + 1) * LANES)
            here = slice(tile * LANES, (tile + 1) * LANES)
            qt, kt, vt = qs.at[number], ks.at[number], vs.at[number]
            prev = jnp.where(follows, held[index, 128:PACKED, here].astype(F32), 0.0)
            qt[0:8, :] = prev[0:8]
            kt[0:8, :] = prev[8:16]
            vt[0:8, :] = prev[16:24]
            qt[8:24, :] = q_ref[:, cols].astype(F32)
            kt[8:24, :] = k_ref[:, cols].astype(F32)
            vt[8:24, :] = v_ref[:, cols].astype(F32)
            first_query = short_conv(qt, taps_ref[0, :, cols].astype(F32), 0, 16)
            key = short_conv(kt, taps_ref[1, :, cols].astype(F32), 0, 16)
            value = short_conv(vt, taps_ref[2, :, cols].astype(F32), 0, 16)
            opening = (key * value).astype(BF16)
            state = held[index, 0:128, here]
            state = jnp.where(follows, state, jnp.zeros_like(state))
            pad = jnp.zeros((WINDOW - BLOCK - 128, LANES), BF16)
            extended = jnp.concatenate([pad, state, opening, u_ref[16:192, cols]])
            base = number * per_lane
            matrix = toeplitz(lines_ref[pl.ds(base, per_lane), :])
            parts = []
            for first in range(0, 128, SIDE * BLOCK):
                lows = range(first, first + SIDE * BLOCK, BLOCK)
                windows = [extended[low : low + WINDOW] for low in lows]
                result = jnp.dot(matrix, jnp.concatenate(windows, axis=1), preferred_element_type=F32)
                picked = pick_groups(result, group_size)
                parts.append((first, SIDE * BLOCK, unfold(picked)))
            edge = OPENING - 128
            edge_matrix = jnp.concatenate([matrix[g * BLOCK : g * BLOCK + edge] for g in range(per_lane)])
            edge_result = jnp.dot(edge_matrix, extended[128 : 128 + WINDOW], preferred_element_type=F32)
            parts.append((128, edge, pick_groups(edge_result, group_size, edge)))
            for first, rows, filtered in parts:
                query = query_ref[first : first + rows, cols]
                if first == 0:
                    query = jnp.concatenate([first_query, query[16:]])
                row = lax.broadcasted_iota(jnp.int32, (rows, LANES), 0) + first
                mixed = jnp.where(row < length, query * filtered, 0.0).astype(BF16)
                mixed_ref[first : first + rows, cols] = mixed
                summed = res_ref[first : first + rows, cols].astype(F32) + mixed.astype(F32)
                acc[first : first + rows, :] += summed * summed

    tiles()

    @pl.when(step == pl.num_programs(0) - 1)
    def _():
        sum_ref[...] = jnp.sum(acc[...].T, axis=0, keepdims=True)


def head_call(group_size, predecessor, stretch_lengths, previous, query_opening, queries, keys_in, values_in, mixed_in, residual, short_taps, lines, mixed):
    rows, width = queries.shape
    per_step = HEAD_WIDE // group_size
    block = pl.BlockSpec((OPENING, HEAD_WIDE), lambda p, *_: (0, p))
    small = pl.BlockSpec((16, HEAD_WIDE), lambda p, *_: (0, p))
    return pl.pallas_call(
        functools.partial(head_kernel, group_size),
        grid_spec=pltpu.PrefetchScalarGridSpec(
            num_scalar_prefetch=2,
            grid=(width // HEAD_WIDE,),
            in_specs=[
                pl.BlockSpec((HEAD_WIDE // STEP, PACKED, STEP), lambda p, *_: (p, 0, 0)),
                block,
                small,
                small,
                small,
                pl.BlockSpec((192, HEAD_WIDE), lambda p, *_: (0, p)),
                block,
                pl.BlockSpec((3, 7, HEAD_WIDE), lambda p, *_: (0, 0, p)),
                pl.BlockSpec((per_step, WINDOW), lambda p, *_: (p, 0)),
                pl.BlockSpec(memory_space=pl.ANY),
            ],
            out_specs=[block, pl.BlockSpec((1, 256), lambda p, *_: (0, 0))],
            scratch_shapes=[
                pltpu.VMEM((HEAD_WIDE // LANES, 24, LANES), F32),
                pltpu.VMEM((HEAD_WIDE // LANES, 24, LANES), F32),
                pltpu.VMEM((HEAD_WIDE // LANES, 24, LANES), F32),
                pltpu.VMEM((256, LANES), F32),
            ],
        ),
        out_shape=[
            jax.ShapeDtypeStruct((rows, width), BF16),
            jax.ShapeDtypeStruct((1, 256), F32),
        ],
        input_output_aliases={11: 0},
        compiler_params=params(),
        cost_estimate=cost(128 * width * 2 * WINDOW * 8, 128 * width * 12),
        name="head",
    )(predecessor, stretch_lengths, previous, query_opening, queries, keys_in, values_in, mixed_in, residual, short_taps, lines, mixed)


def norm_kernel(channels, first_block, sums, len_ref, *refs):
    sum_refs, (mixed_ref, res_ref, gain_ref), out_ref = refs[:sums], refs[sums : sums + 3], refs[-1]
    rows = mixed_ref.shape[0]
    first = (pl.program_id(0) + first_block) * rows
    length = len_ref[lax.axis_index("seq")]
    total = sum_refs[0][...]
    for ref in sum_refs[1:]:
        total = total + ref[...]
    scale = jnp.broadcast_to(lax.rsqrt(total / channels + EPSILON), (LANES, total.shape[1])).T[:rows]
    scale = jnp.where(lax.broadcasted_iota(jnp.int32, (rows, LANES), 0) + first < length, scale, 0.0)
    for lane in range(0, mixed_ref.shape[1], LANES):
        cols = slice(lane, lane + LANES)
        gain = gain_ref[:, cols].astype(F32)
        summed = res_ref[:, cols].astype(F32) + mixed_ref[:, cols].astype(F32)
        out_ref[:, cols] = (summed * scale * gain).astype(BF16)


def norm_call(channels, steps, first_block, stretch_lengths, totals, mixed, residual, gain, normed=None):
    rows, width = mixed.shape
    opening = first_block == 0
    size, lanes, skip = (OPENING, 256, 0) if opening else (128, 128, first_block - 1)
    block = pl.BlockSpec((size, width), lambda p, *_: (p + first_block, 0))
    operands = [*totals, mixed, residual, gain]
    in_specs = [pl.BlockSpec((1, lanes), lambda p, *_: (0, p + skip))] * len(totals)
    in_specs += [block, block, pl.BlockSpec((1, width), lambda p, *_: (0, 0))]
    aliases = {}
    if normed is not None:
        aliases = {len(operands) + 1: 0}
        operands.append(normed)
        in_specs.append(pl.BlockSpec(memory_space=pl.ANY))
    return pl.pallas_call(
        functools.partial(norm_kernel, channels, first_block, len(totals)),
        grid_spec=pltpu.PrefetchScalarGridSpec(
            num_scalar_prefetch=1, grid=(steps,), in_specs=in_specs, out_specs=block
        ),
        out_shape=jax.ShapeDtypeStruct((rows, width), BF16),
        input_output_aliases=aliases,
        compiler_params=params(),
        cost_estimate=cost(steps * size * width * 6, steps * size * width * 6),
        name="norm%d" % first_block,
    )(stretch_lengths, *operands)


def swap(array, axis, distance):
    size = lax.axis_size(axis)
    return lax.ppermute(array, axis, [(i, i ^ distance) for i in range(size)])


def exchange(pieces):
    return lax.all_to_all(pieces, "seq", split_axis=0, concat_axis=0, tiled=True)


def shares(squares):
    parts = lax.axis_size("mp")
    if parts != 4:
        return [lax.psum(squares, "mp")]
    return [squares] + [swap(squares, "mp", k) for k in range(1, parts)]


def body(queries, keys_in, values_in, residual, short_taps, mr_filter, norm_gain, predecessor, stretch_lengths):
    rows, width = queries.shape
    count = lax.axis_size("seq")
    channels = width * lax.axis_size("mp")
    group_size = width // mr_filter.shape[1]
    two_phase = width // STEP == count == 8 and mr_filter.shape == (16, LANES)
    gain = norm_gain.reshape(1, width)
    packed = tail_call(two_phase, queries, keys_in, values_in, short_taps, mr_filter)
    mixed_in, query_opening, query_later = feature_call(queries, keys_in, values_in, short_taps)
    if two_phase:
        received = exchange(packed)
        received, mixed_in, gain = lax.optimization_barrier((received, mixed_in, gain))
        routed, filter_rows = lax.optimization_barrier((route_call(predecessor, received), received))
        previous = exchange(routed)
    else:
        gathered = lax.all_gather(packed[None], "seq", axis=0, tiled=True)
        source = jnp.clip(predecessor[lax.axis_index("seq")], 0, count - 1)
        previous = lax.dynamic_index_in_dim(gathered, source, 0, keepdims=False)
        filter_rows = lax.all_gather(mr_filter, "seq", axis=0, tiled=True)
    mixed, squares, lines = main_call(
        group_size, stretch_lengths, query_later, mixed_in, residual, filter_rows
    )
    totals = shares(squares)
    early = rows // 128 - 2
    normed = norm_call(channels, early, 1, stretch_lengths, totals, mixed, residual, gain)
    previous, normed = lax.optimization_barrier((previous, normed))
    mixed, squares = head_call(
        group_size, predecessor, stretch_lengths, previous, query_opening, queries, keys_in, values_in,
        mixed_in, residual, short_taps, lines, mixed,
    )
    opening_totals = shares(squares)
    normed = norm_call(channels, 1, early + 1, stretch_lengths, totals, mixed, residual, gain, normed)
    normed = norm_call(channels, 1, 0, stretch_lengths, opening_totals, mixed, residual, gain, normed)
    return (mixed, normed)


def solution(mesh):
    in_specs = (
        P("seq", "mp"),
        P("seq", "mp"),
        P("seq", "mp"),
        P("seq", "mp"),
        P(None, None, "mp"),
        P("seq", "mp"),
        P("mp"),
        P(),
        P(),
    )
    out_specs = (P("seq", "mp"), P("seq", "mp"))
    return jax.shard_map(body, mesh=mesh, in_specs=in_specs, out_specs=out_specs, check_vma=False)
```

```python
import functools

import jax
import jax.numpy as jnp
from jax import lax
from jax.experimental import pallas as pl
from jax.experimental.pallas import tpu as pltpu
from jax.sharding import PartitionSpec as P

EPSILON = 1e-06
F32 = jnp.float32
BF16 = jnp.bfloat16
LANES = 128
STEP = 256
WIDE = 512
BROAD = 1024
SIDE = 4
BLOCK = 32
WINDOW = 256
PACKED = 160
OPENING = 144
VMEM_LIMIT = 64 * 1024 * 1024


def unfold(picked):
    return jnp.concatenate([picked[:, i * LANES : (i + 1) * LANES] for i in range(picked.shape[1] // LANES)])


def params():
    return pltpu.CompilerParams(vmem_limit_bytes=VMEM_LIMIT)


def cost(flops, bytes_accessed):
    return pl.CostEstimate(flops=flops, bytes_accessed=bytes_accessed, transcendentals=0)


def short_conv(scratch, taps, start, rows):
    total = None
    for offset in range(taps.shape[0]):
        term = taps[offset : offset + 1] * scratch[pl.ds(start + 8 - offset, rows), :]
        total = term if total is None else total + term
    return total


def tail_kernel(packed, q_ref, k_ref, v_ref, kb_ref, vb_ref, taps_ref, filt_ref, out_ref, ks, vs):
    for slot in range(out_ref.shape[0]):
        lasts = []
        for tile in range(STEP // LANES):
            number = slot * (STEP // LANES) + tile
            cols = slice(number * LANES, (number + 1) * LANES)
            here = slice(tile * LANES, (tile + 1) * LANES)
            kt, vt = ks.at[number], vs.at[number]
            kt[0:16, :] = kb_ref[:, cols].astype(F32)
            vt[0:16, :] = vb_ref[:, cols].astype(F32)
            kt[16:144, :] = k_ref[:, cols].astype(F32)
            vt[16:144, :] = v_ref[:, cols].astype(F32)
            key_taps = taps_ref[1, :, cols].astype(F32)
            value_taps = taps_ref[2, :, cols].astype(F32)
            for row in range(0, 128, 64):
                key = short_conv(kt, key_taps, row + 8, 64)
                value = short_conv(vt, value_taps, row + 8, 64)
                out_ref[slot, row : row + 64, here] = (key * value).astype(BF16)
            last = [q_ref[:, cols].astype(F32)[8:], kt[136:144, :], vt[136:144, :]]
            if packed:
                last.append(filt_ref[...].astype(F32)[8 * tile : 8 * tile + 8])
            else:
                last.append(jnp.zeros((8, LANES), F32))
            lasts.append(jnp.concatenate(last))
        out_ref[slot, 128:PACKED, :] = jnp.concatenate(lasts, axis=1).astype(BF16)


def tail_call(packed, queries, keys_in, values_in, short_taps, mr_filter):
    rows, width = queries.shape
    slots = width // STEP
    part = width // 2
    count = part // LANES
    return pl.pallas_call(
        functools.partial(tail_kernel, packed),
        grid=(2,),
        in_specs=[
            pl.BlockSpec((16, part), lambda p: (rows // 16 - 1, p)),
            pl.BlockSpec((128, part), lambda p: (rows // 128 - 1, p)),
            pl.BlockSpec((128, part), lambda p: (rows // 128 - 1, p)),
            pl.BlockSpec((16, part), lambda p: (rows // 16 - 9, p)),
            pl.BlockSpec((16, part), lambda p: (rows // 16 - 9, p)),
            pl.BlockSpec((3, 7, part), lambda p: (0, 0, p)),
            pl.BlockSpec(mr_filter.shape, lambda p: (0, 0)),
        ],
        out_specs=pl.BlockSpec((slots // 2, PACKED, STEP), lambda p: (p, 0, 0)),
        out_shape=jax.ShapeDtypeStruct((slots, PACKED, STEP), BF16),
        scratch_shapes=[pltpu.VMEM((count, 144, LANES), F32)] * 2,
        compiler_params=params(),
        cost_estimate=cost(128 * width * 30, 128 * width * 6),
        name="tail",
    )(queries, keys_in, values_in, keys_in, values_in, short_taps, mr_filter)


def feature_kernel(q_ref, k_ref, v_ref, taps_ref, out_ref, opening_ref, later_ref, qs, ks, vs):
    rows = k_ref.shape[0]

    def pair(index, carry):
        for tile in range(2):
            cols = pl.ds(pl.multiple_of(index * 2 * LANES + tile * LANES, LANES), LANES)
            scratches = (qs.at[tile], ks.at[tile], vs.at[tile])
            taps = [taps_ref[i, :, cols].astype(F32) for i in range(3)]
            for scratch, ref in zip(scratches, (q_ref, k_ref, v_ref)):
                scratch[0:8, :] = jnp.zeros((8, LANES), F32)
                scratch[8 : rows + 8, :] = ref[:, cols].astype(F32)
            for row in range(0, rows, 64):
                query, key, value = [short_conv(x, t, row, 64) for x, t in zip(scratches, taps)]
                out_ref[row : row + 64, cols] = (key * value).astype(BF16)
                if row < OPENING:
                    count = min(64, OPENING - row)
                    opening_ref[row : row + count, cols] = query[:count]
                if row >= 128:
                    later_ref[row - 128 : row - 64, cols] = query
        return carry

    lax.fori_loop(0, k_ref.shape[1] // (2 * LANES), pair, 0)


def feature_call(queries, keys_in, values_in, short_taps):
    rows, width = keys_in.shape
    heights = (rows, OPENING, rows - 128)
    blocks = [pl.BlockSpec((height, WIDE), lambda p: (0, p)) for height in heights]
    scratch = pltpu.VMEM((2, rows + 8, LANES), F32)
    return pl.pallas_call(
        feature_kernel,
        grid=(width // WIDE,),
        in_specs=[blocks[0]] * 3 + [pl.BlockSpec((3, 7, WIDE), lambda p: (0, 0, p))],
        out_specs=blocks,
        out_shape=[
            jax.ShapeDtypeStruct((height, width), kind) for height, kind in zip(heights, (BF16, F32, F32))
        ],
        scratch_shapes=[scratch] * 3,
        compiler_params=params(),
        cost_estimate=cost(rows * width * 45, rows * width * 13),
        name="features",
    )(queries, keys_in, values_in, short_taps)


def route_kernel(pred_ref, in_ref, out_ref):
    for j in range(in_ref.shape[0]):
        out_ref[j] = in_ref[jnp.maximum(pred_ref[j], 0)]


def route_call(predecessor, received):
    return pl.pallas_call(
        route_kernel,
        in_specs=[pl.BlockSpec(memory_space=pltpu.SMEM), pl.BlockSpec(memory_space=pltpu.VMEM)],
        out_specs=pl.BlockSpec(memory_space=pltpu.VMEM),
        out_shape=jax.ShapeDtypeStruct(received.shape, BF16),
        compiler_params=params(),
        cost_estimate=cost(0, received.size * 4),
        name="route",
    )(predecessor, received)


def all_taps(filt_ref):
    if len(filt_ref.shape) == 2:
        return filt_ref[...]
    rows = []
    for j in range(filt_ref.shape[0]):
        last = filt_ref[j].astype(F32)[8:]
        rows += [last[:, :LANES], last[:, LANES:]]
    return jnp.concatenate(rows).astype(BF16)


def spread_taps(filter_rows):
    shape = (filter_rows.shape[0], WINDOW)
    tap = lax.broadcasted_iota(jnp.int32, shape, 0)
    place = lax.broadcasted_iota(jnp.int32, shape, 1)
    onehot = (place == WINDOW - BLOCK - tap).astype(BF16)
    return lax.dot_general(filter_rows, onehot, (((0,), (0,)), ((), ())), preferred_element_type=F32)


def toeplitz(lines):
    blocks = []
    for g in range(lines.shape[0]):
        line = jnp.broadcast_to(lines[g : g + 1], (BLOCK, WINDOW))
        blocks.append(pltpu.roll(line, 0, 1, stride=1, stride_axis=0).astype(BF16))
    return jnp.concatenate(blocks)


def pick_groups(result, group_size, rows=BLOCK):
    shape = (rows, result.shape[1])
    group = (lax.broadcasted_iota(jnp.int32, shape, 1) & (LANES - 1)) // group_size
    picked = result[:rows]
    for g in range(1, LANES // group_size):
        picked = jnp.where(group == g, result[g * rows : (g + 1) * rows], picked)
    return picked


def main_kernel(group_size, len_ref, query_ref, u_ref, res_ref, filt_ref, mixed_ref, sum_ref, lines_ref, acc):
    step = pl.program_id(0)
    rows = u_ref.shape[0]
    per_lane = LANES // group_size
    length = len_ref[lax.axis_index("seq")]

    @pl.when(step == 0)
    def _():
        lines_ref[...] = spread_taps(all_taps(filt_ref))
        acc[...] = jnp.zeros_like(acc)

    def tiles():
        for number in range(BROAD // LANES):
            cols = slice(number * LANES, (number + 1) * LANES)
            base = pl.multiple_of((step * (BROAD // LANES) + number) * per_lane, per_lane)
            matrix = toeplitz(lines_ref[pl.ds(base, per_lane), :])
            for start in range(128, rows, SIDE * BLOCK):
                windows = []
                for first in range(start, start + SIDE * BLOCK, BLOCK):
                    low = first + BLOCK - WINDOW
                    if low < 0:
                        windows.append(
                            jnp.concatenate([jnp.zeros((-low, LANES), BF16), u_ref[0 : first + BLOCK, cols]])
                        )
                    else:
                        windows.append(u_ref[low : first + BLOCK, cols])
                result = jnp.dot(matrix, jnp.concatenate(windows, axis=1), preferred_element_type=F32)
                picked = pick_groups(result, group_size)
                filtered = unfold(picked)
                here = slice(start - 128, start - 128 + SIDE * BLOCK)
                row = lax.broadcasted_iota(jnp.int32, filtered.shape, 0) + start
                mixed = jnp.where(row < length, query_ref[here, cols] * filtered, 0.0).astype(BF16)
                mixed_ref[here, cols] = mixed
                summed = res_ref[here, cols].astype(F32) + mixed.astype(F32)
                acc[here, :] += summed * summed

    tiles()

    @pl.when(step == pl.num_programs(0) - 1)
    def _():
        sum_ref[...] = jnp.sum(acc[...].T, axis=0, keepdims=True)


def main_call(group_size, stretch_lengths, query_later, mixed_in, residual, filter_rows):
    rows, width = residual.shape
    groups = width // group_size
    if len(filter_rows.shape) == 2:
        filter_spec = pl.BlockSpec(filter_rows.shape, lambda p, *_: (0, 0))
    else:
        filter_spec = pl.BlockSpec((filter_rows.shape[0], 16, STEP), lambda p, *_: (0, PACKED // 16 - 1, 0))
    block = pl.BlockSpec((rows, BROAD), lambda p, *_: (0, p))
    later = pl.BlockSpec((pl.Element(rows - 128), pl.Element(BROAD)), lambda p, *_: (128, p * BROAD))
    return pl.pallas_call(
        functools.partial(main_kernel, group_size),
        grid_spec=pltpu.PrefetchScalarGridSpec(
            num_scalar_prefetch=1,
            grid=(width // BROAD,),
            in_specs=[
                pl.BlockSpec((rows - 128, BROAD), lambda p, *_: (0, p)),
                block,
                later,
                filter_spec,
            ],
            out_specs=[
                later,
                pl.BlockSpec((1, rows - 128), lambda p, *_: (0, 0)),
                pl.BlockSpec((groups, WINDOW), lambda p, *_: (0, 0)),
            ],
            scratch_shapes=[
                pltpu.VMEM((rows - 128, LANES), F32),
            ],
        ),
        out_shape=[
            jax.ShapeDtypeStruct((rows, width), BF16),
            jax.ShapeDtypeStruct((1, rows - 128), F32),
            jax.ShapeDtypeStruct((groups, WINDOW), F32),
        ],
        compiler_params=params(),
        cost_estimate=cost(rows * width * 2 * WINDOW * 8, rows * width * 12),
        name="conv",
    )(stretch_lengths, query_later, mixed_in, residual, filter_rows)


def head_kernel(group_size, pred_ref, len_ref, held, query_ref, q_ref, k_ref, v_ref, u_ref, res_ref, taps_ref, lines_ref, kept_ref, mixed_ref, sum_ref, qs, ks, vs, acc):
    del kept_ref
    step = pl.program_id(0)
    per_lane = LANES // group_size
    device = lax.axis_index("seq")
    length = len_ref[device]
    follows = pred_ref[device] >= 0

    @pl.when(step == 0)
    def _():
        acc[...] = jnp.zeros_like(acc)

    def tiles():
        for number in range(BROAD // LANES):
            index, tile = divmod(number, STEP // LANES)
            cols = slice(number * LANES, (number + 1) * LANES)
            here = slice(tile * LANES, (tile + 1) * LANES)
            qt, kt, vt = qs.at[number], ks.at[number], vs.at[number]
            prev = jnp.where(follows, held[index, 128:PACKED, here].astype(F32), 0.0)
            qt[0:8, :] = prev[0:8]
            kt[0:8, :] = prev[8:16]
            vt[0:8, :] = prev[16:24]
            qt[8:24, :] = q_ref[:, cols].astype(F32)
            kt[8:24, :] = k_ref[:, cols].astype(F32)
            vt[8:24, :] = v_ref[:, cols].astype(F32)
            first_query = short_conv(qt, taps_ref[0, :, cols].astype(F32), 0, 16)
            key = short_conv(kt, taps_ref[1, :, cols].astype(F32), 0, 16)
            value = short_conv(vt, taps_ref[2, :, cols].astype(F32), 0, 16)
            opening = (key * value).astype(BF16)
            state = held[index, 0:128, here]
            state = jnp.where(follows, state, jnp.zeros_like(state))
            pad = jnp.zeros((WINDOW - BLOCK - 128, LANES), BF16)
            extended = jnp.concatenate([pad, state, opening, u_ref[16:192, cols]])
            base = number * per_lane
            matrix = toeplitz(lines_ref[pl.ds(base, per_lane), :])
            parts = []
            for first in range(0, 128, SIDE * BLOCK):
                lows = range(first, first + SIDE * BLOCK, BLOCK)
                windows = [extended[low : low + WINDOW] for low in lows]
                result = jnp.dot(matrix, jnp.concatenate(windows, axis=1), preferred_element_type=F32)
                picked = pick_groups(result, group_size)
                parts.append((first, SIDE * BLOCK, unfold(picked)))
            edge = OPENING - 128
            edge_matrix = jnp.concatenate([matrix[g * BLOCK : g * BLOCK + edge] for g in range(per_lane)])
            edge_result = jnp.dot(edge_matrix, extended[128 : 128 + WINDOW], preferred_element_type=F32)
            parts.append((128, edge, pick_groups(edge_result, group_size, edge)))
            for first, rows, filtered in parts:
                query = query_ref[first : first + rows, cols]
                if first == 0:
                    query = jnp.concatenate([first_query, query[16:]])
                row = lax.broadcasted_iota(jnp.int32, (rows, LANES), 0) + first
                mixed = jnp.where(row < length, query * filtered, 0.0).astype(BF16)
                mixed_ref[first : first + rows, cols] = mixed
                summed = res_ref[first : first + rows, cols].astype(F32) + mixed.astype(F32)
                acc[first : first + rows, :] += summed * summed

    tiles()

    @pl.when(step == pl.num_programs(0) - 1)
    def _():
        sum_ref[...] = jnp.sum(acc[...].T, axis=0, keepdims=True)


def head_call(group_size, predecessor, stretch_lengths, previous, query_opening, queries, keys_in, values_in, mixed_in, residual, short_taps, lines, mixed):
    rows, width = queries.shape
    per_step = BROAD // group_size
    block = pl.BlockSpec((OPENING, BROAD), lambda p, *_: (0, p))
    small = pl.BlockSpec((16, BROAD), lambda p, *_: (0, p))
    return pl.pallas_call(
        functools.partial(head_kernel, group_size),
        grid_spec=pltpu.PrefetchScalarGridSpec(
            num_scalar_prefetch=2,
            grid=(width // BROAD,),
            in_specs=[
                pl.BlockSpec((BROAD // STEP, PACKED, STEP), lambda p, *_: (p, 0, 0)),
                block,
                small,
                small,
                small,
                pl.BlockSpec((192, BROAD), lambda p, *_: (0, p)),
                block,
                pl.BlockSpec((3, 7, BROAD), lambda p, *_: (0, 0, p)),
                pl.BlockSpec((per_step, WINDOW), lambda p, *_: (p, 0)),
                pl.BlockSpec(memory_space=pl.ANY),
            ],
            out_specs=[block, pl.BlockSpec((1, 256), lambda p, *_: (0, 0))],
            scratch_shapes=[
                pltpu.VMEM((BROAD // LANES, 24, LANES), F32),
                pltpu.VMEM((BROAD // LANES, 24, LANES), F32),
                pltpu.VMEM((BROAD // LANES, 24, LANES), F32),
                pltpu.VMEM((256, LANES), F32),
            ],
        ),
        out_shape=[
            jax.ShapeDtypeStruct((rows, width), BF16),
            jax.ShapeDtypeStruct((1, 256), F32),
        ],
        input_output_aliases={11: 0},
        compiler_params=params(),
        cost_estimate=cost(128 * width * 2 * WINDOW * 8, 128 * width * 12),
        name="head",
    )(predecessor, stretch_lengths, previous, query_opening, queries, keys_in, values_in, mixed_in, residual, short_taps, lines, mixed)


def norm_kernel(channels, first_block, sums, len_ref, *refs):
    sum_refs, (mixed_ref, res_ref, gain_ref), out_ref = refs[:sums], refs[sums : sums + 3], refs[-1]
    rows = mixed_ref.shape[0]
    first = (pl.program_id(0) + first_block) * rows
    length = len_ref[lax.axis_index("seq")]
    total = sum_refs[0][...]
    for ref in sum_refs[1:]:
        total = total + ref[...]
    scale = jnp.broadcast_to(lax.rsqrt(total / channels + EPSILON), (LANES, total.shape[1])).T[:rows]
    scale = jnp.where(lax.broadcasted_iota(jnp.int32, (rows, LANES), 0) + first < length, scale, 0.0)
    for lane in range(0, mixed_ref.shape[1], LANES):
        cols = slice(lane, lane + LANES)
        gain = gain_ref[:, cols].astype(F32)
        summed = res_ref[:, cols].astype(F32) + mixed_ref[:, cols].astype(F32)
        out_ref[:, cols] = (summed * scale * gain).astype(BF16)


def norm_call(channels, steps, first_block, stretch_lengths, totals, mixed, residual, gain, normed=None):
    rows, width = mixed.shape
    opening = first_block == 0
    size, lanes, skip = (OPENING, 256, 0) if opening else (128, 128, first_block - 1)
    block = pl.BlockSpec((size, width), lambda p, *_: (p + first_block, 0))
    operands = [*totals, mixed, residual, gain]
    in_specs = [pl.BlockSpec((1, lanes), lambda p, *_: (0, p + skip))] * len(totals)
    in_specs += [block, block, pl.BlockSpec((1, width), lambda p, *_: (0, 0))]
    aliases = {}
    if normed is not None:
        aliases = {len(operands) + 1: 0}
        operands.append(normed)
        in_specs.append(pl.BlockSpec(memory_space=pl.ANY))
    return pl.pallas_call(
        functools.partial(norm_kernel, channels, first_block, len(totals)),
        grid_spec=pltpu.PrefetchScalarGridSpec(
            num_scalar_prefetch=1, grid=(steps,), in_specs=in_specs, out_specs=block
        ),
        out_shape=jax.ShapeDtypeStruct((rows, width), BF16),
        input_output_aliases=aliases,
        compiler_params=params(),
        cost_estimate=cost(steps * size * width * 6, steps * size * width * 6),
        name="norm%d" % first_block,
    )(stretch_lengths, *operands)


def swap(array, axis, distance):
    size = lax.axis_size(axis)
    return lax.ppermute(array, axis, [(i, i ^ distance) for i in range(size)])


def exchange(pieces):
    return lax.all_to_all(pieces, "seq", split_axis=0, concat_axis=0, tiled=True)


def shares(squares):
    parts = lax.axis_size("mp")
    if parts != 4:
        return [lax.psum(squares, "mp")]
    return [squares] + [swap(squares, "mp", k) for k in range(1, parts)]


def body(queries, keys_in, values_in, residual, short_taps, mr_filter, norm_gain, predecessor, stretch_lengths):
    rows, width = queries.shape
    count = lax.axis_size("seq")
    channels = width * lax.axis_size("mp")
    group_size = width // mr_filter.shape[1]
    two_phase = width // STEP == count == 8 and mr_filter.shape == (16, LANES)
    gain = norm_gain.reshape(1, width)
    packed = tail_call(two_phase, queries, keys_in, values_in, short_taps, mr_filter)
    mixed_in, query_opening, query_later = feature_call(queries, keys_in, values_in, short_taps)
    if two_phase:
        received = exchange(packed)
        received, mixed_in, gain = lax.optimization_barrier((received, mixed_in, gain))
        routed, filter_rows = lax.optimization_barrier((route_call(predecessor, received), received))
        previous = exchange(routed)
    else:
        gathered = lax.all_gather(packed[None], "seq", axis=0, tiled=True)
        source = jnp.clip(predecessor[lax.axis_index("seq")], 0, count - 1)
        previous = lax.dynamic_index_in_dim(gathered, source, 0, keepdims=False)
        filter_rows = lax.all_gather(mr_filter, "seq", axis=0, tiled=True)
    mixed, squares, lines = main_call(
        group_size, stretch_lengths, query_later, mixed_in, residual, filter_rows
    )
    totals = shares(squares)
    early = rows // 128 - 2
    normed = norm_call(channels, early, 1, stretch_lengths, totals, mixed, residual, gain)
    previous, normed = lax.optimization_barrier((previous, normed))
    mixed, squares = head_call(
        group_size, predecessor, stretch_lengths, previous, query_opening, queries, keys_in, values_in,
        mixed_in, residual, short_taps, lines, mixed,
    )
    opening_totals = shares(squares)
    normed = norm_call(channels, 1, early + 1, stretch_lengths, totals, mixed, residual, gain, normed)
    normed = norm_call(channels, 1, 0, stretch_lengths, opening_totals, mixed, residual, gain, normed)
    return (mixed, normed)


def solution(mesh):
    in_specs = (
        P("seq", "mp"),
        P("seq", "mp"),
        P("seq", "mp"),
        P("seq", "mp"),
        P(None, None, "mp"),
        P("seq", "mp"),
        P("mp"),
        P(),
        P(),
    )
    out_specs = (P("seq", "mp"), P("seq", "mp"))
    return jax.shard_map(body, mesh=mesh, in_specs=in_specs, out_specs=out_specs, check_vma=False)
```

```python
import functools

import jax
import jax.numpy as jnp
from jax import lax
from jax.experimental import pallas as pl
from jax.experimental.pallas import tpu as pltpu
from jax.sharding import PartitionSpec as P

EPSILON = 1e-06
F32 = jnp.float32
BF16 = jnp.bfloat16
LANES = 128
STEP = 256
WIDE = 512
HEAD_WIDE = 1024
SIDE = 4
BLOCK = 32
WINDOW = 256
PACKED = 160
OPENING = 144
VMEM_LIMIT = 64 * 1024 * 1024


def unfold(picked):
    return jnp.concatenate([picked[:, i * LANES : (i + 1) * LANES] for i in range(picked.shape[1] // LANES)])


def params():
    return pltpu.CompilerParams(vmem_limit_bytes=VMEM_LIMIT)


def cost(flops, bytes_accessed):
    return pl.CostEstimate(flops=flops, bytes_accessed=bytes_accessed, transcendentals=0)


def short_conv(scratch, taps, start, rows):
    total = None
    for offset in range(taps.shape[0]):
        term = taps[offset : offset + 1] * scratch[pl.ds(start + 8 - offset, rows), :]
        total = term if total is None else total + term
    return total


def split_conv(scratch, taps, start, rows):
    reads = [scratch[pl.ds(start - offset, rows + 8), :] for offset in (0, 2, 4)]
    odd = taps[1:2] * reads[0] + taps[3:4] * reads[1] + taps[5:6] * reads[2]
    even = taps[0:1] * reads[0] + taps[2:3] * reads[1] + taps[4:5] * reads[2]
    total = (even + pltpu.roll(odd, 1, 0))[8:]
    return total + taps[6:7] * scratch[pl.ds(start + 8 - 6, rows), :]


def tail_kernel(packed, q_ref, k_ref, v_ref, kb_ref, vb_ref, taps_ref, filt_ref, out_ref, ks, vs):
    for slot in range(out_ref.shape[0]):
        lasts = []
        for tile in range(STEP // LANES):
            number = slot * (STEP // LANES) + tile
            cols = slice(number * LANES, (number + 1) * LANES)
            here = slice(tile * LANES, (tile + 1) * LANES)
            kt, vt = ks.at[number], vs.at[number]
            kt[0:16, :] = kb_ref[:, cols].astype(F32)
            vt[0:16, :] = vb_ref[:, cols].astype(F32)
            kt[16:144, :] = k_ref[:, cols].astype(F32)
            vt[16:144, :] = v_ref[:, cols].astype(F32)
            key_taps = taps_ref[1, :, cols].astype(F32)
            value_taps = taps_ref[2, :, cols].astype(F32)
            for row in range(0, 128, 64):
                key = split_conv(kt, key_taps, row + 8, 64)
                value = split_conv(vt, value_taps, row + 8, 64)
                out_ref[slot, row : row + 64, here] = (key * value).astype(BF16)
            last = [q_ref[:, cols].astype(F32)[8:], kt[136:144, :], vt[136:144, :]]
            if packed:
                last.append(filt_ref[...].astype(F32)[8 * tile : 8 * tile + 8])
            else:
                last.append(jnp.zeros((8, LANES), F32))
            lasts.append(jnp.concatenate(last))
        out_ref[slot, 128:PACKED, :] = jnp.concatenate(lasts, axis=1).astype(BF16)


def tail_call(packed, queries, keys_in, values_in, short_taps, mr_filter):
    rows, width = queries.shape
    slots = width // STEP
    part = width // 2
    count = part // LANES
    return pl.pallas_call(
        functools.partial(tail_kernel, packed),
        grid=(2,),
        in_specs=[
            pl.BlockSpec((16, part), lambda p: (rows // 16 - 1, p)),
            pl.BlockSpec((128, part), lambda p: (rows // 128 - 1, p)),
            pl.BlockSpec((128, part), lambda p: (rows // 128 - 1, p)),
            pl.BlockSpec((16, part), lambda p: (rows // 16 - 9, p)),
            pl.BlockSpec((16, part), lambda p: (rows // 16 - 9, p)),
            pl.BlockSpec((3, 7, part), lambda p: (0, 0, p)),
            pl.BlockSpec(mr_filter.shape, lambda p: (0, 0)),
        ],
        out_specs=pl.BlockSpec((slots // 2, PACKED, STEP), lambda p: (p, 0, 0)),
        out_shape=jax.ShapeDtypeStruct((slots, PACKED, STEP), BF16),
        scratch_shapes=[pltpu.VMEM((count, 144, LANES), F32)] * 2,
        compiler_params=params(),
        cost_estimate=cost(128 * width * 30, 128 * width * 6),
        name="tail",
    )(queries, keys_in, values_in, keys_in, values_in, short_taps, mr_filter)


def feature_kernel(q_ref, k_ref, v_ref, taps_ref, out_ref, opening_ref, later_ref, qs, ks, vs):
    rows = k_ref.shape[0]

    def pair(index, carry):
        for tile in range(2):
            cols = pl.ds(pl.multiple_of(index * 2 * LANES + tile * LANES, LANES), LANES)
            scratches = (qs.at[tile], ks.at[tile], vs.at[tile])
            taps = [taps_ref[i, :, cols].astype(F32) for i in range(3)]
            for scratch, ref in zip(scratches, (q_ref, k_ref, v_ref)):
                scratch[0:8, :] = jnp.zeros((8, LANES), F32)
                scratch[8 : rows + 8, :] = ref[:, cols].astype(F32)
            for row in range(0, rows, 64):
                query, key, value = [short_conv(x, t, row, 64) for x, t in zip(scratches, taps)]
                out_ref[row : row + 64, cols] = (key * value).astype(BF16)
                if row < OPENING:
                    count = min(64, OPENING - row)
                    opening_ref[row : row + count, cols] = query[:count]
                if row >= 128:
                    later_ref[row - 128 : row - 64, cols] = query
        return carry

    lax.fori_loop(0, k_ref.shape[1] // (2 * LANES), pair, 0)


def feature_call(queries, keys_in, values_in, short_taps):
    rows, width = keys_in.shape
    heights = (rows, OPENING, rows - 128)
    blocks = [pl.BlockSpec((height, WIDE), lambda p: (0, p)) for height in heights]
    scratch = pltpu.VMEM((2, rows + 8, LANES), F32)
    return pl.pallas_call(
        feature_kernel,
        grid=(width // WIDE,),
        in_specs=[blocks[0]] * 3 + [pl.BlockSpec((3, 7, WIDE), lambda p: (0, 0, p))],
        out_specs=blocks,
        out_shape=[
            jax.ShapeDtypeStruct((height, width), kind) for height, kind in zip(heights, (BF16, F32, F32))
        ],
        scratch_shapes=[scratch] * 3,
        compiler_params=params(),
        cost_estimate=cost(rows * width * 45, rows * width * 13),
        name="features",
    )(queries, keys_in, values_in, short_taps)


def route_kernel(pred_ref, in_ref, out_ref):
    for j in range(in_ref.shape[0]):
        out_ref[j] = in_ref[jnp.maximum(pred_ref[j], 0)]


def route_call(predecessor, received):
    return pl.pallas_call(
        route_kernel,
        in_specs=[pl.BlockSpec(memory_space=pltpu.SMEM), pl.BlockSpec(memory_space=pltpu.VMEM)],
        out_specs=pl.BlockSpec(memory_space=pltpu.VMEM),
        out_shape=jax.ShapeDtypeStruct(received.shape, BF16),
        compiler_params=params(),
        cost_estimate=cost(0, received.size * 4),
        name="route",
    )(predecessor, received)


def all_taps(filt_ref):
    if len(filt_ref.shape) == 2:
        return filt_ref[...]
    rows = []
    for j in range(filt_ref.shape[0]):
        last = filt_ref[j].astype(F32)[8:]
        rows += [last[:, :LANES], last[:, LANES:]]
    return jnp.concatenate(rows).astype(BF16)


def spread_taps(filter_rows):
    shape = (filter_rows.shape[0], WINDOW)
    tap = lax.broadcasted_iota(jnp.int32, shape, 0)
    place = lax.broadcasted_iota(jnp.int32, shape, 1)
    onehot = (place == WINDOW - BLOCK - tap).astype(BF16)
    return lax.dot_general(filter_rows, onehot, (((0,), (0,)), ((), ())), preferred_element_type=F32)


def toeplitz(lines):
    blocks = []
    for g in range(lines.shape[0]):
        line = jnp.broadcast_to(lines[g : g + 1], (BLOCK, WINDOW))
        blocks.append(pltpu.roll(line, 0, 1, stride=1, stride_axis=0).astype(BF16))
    return jnp.concatenate(blocks)


def pick_groups(result, group_size, rows=BLOCK):
    shape = (rows, result.shape[1])
    group = (lax.broadcasted_iota(jnp.int32, shape, 1) & (LANES - 1)) // group_size
    picked = result[:rows]
    for g in range(1, LANES // group_size):
        picked = jnp.where(group == g, result[g * rows : (g + 1) * rows], picked)
    return picked


def main_kernel(group_size, len_ref, query_ref, u_ref, res_ref, filt_ref, mixed_ref, sum_ref, lines_ref, acc):
    step = pl.program_id(0)
    rows = u_ref.shape[0]
    per_lane = LANES // group_size
    length = len_ref[lax.axis_index("seq")]

    @pl.when(step == 0)
    def _():
        lines_ref[...] = spread_taps(all_taps(filt_ref))
        acc[...] = jnp.zeros_like(acc)

    def tiles():
        for number in range(WIDE // LANES):
            cols = slice(number * LANES, (number + 1) * LANES)
            base = pl.multiple_of((step * (WIDE // LANES) + number) * per_lane, per_lane)
            matrix = toeplitz(lines_ref[pl.ds(base, per_lane), :])
            for start in range(128, rows, SIDE * BLOCK):
                windows = []
                for first in range(start, start + SIDE * BLOCK, BLOCK):
                    low = first + BLOCK - WINDOW
                    if low < 0:
                        windows.append(
                            jnp.concatenate([jnp.zeros((-low, LANES), BF16), u_ref[0 : first + BLOCK, cols]])
                        )
                    else:
                        windows.append(u_ref[low : first + BLOCK, cols])
                result = jnp.dot(matrix, jnp.concatenate(windows, axis=1), preferred_element_type=F32)
                picked = pick_groups(result, group_size)
                filtered = unfold(picked)
                here = slice(start - 128, start - 128 + SIDE * BLOCK)
                row = lax.broadcasted_iota(jnp.int32, filtered.shape, 0) + start
                mixed = jnp.where(row < length, query_ref[here, cols] * filtered, 0.0).astype(BF16)
                mixed_ref[here, cols] = mixed
                summed = res_ref[here, cols].astype(F32) + mixed.astype(F32)
                acc[here, :] += summed * summed

    tiles()

    @pl.when(step == pl.num_programs(0) - 1)
    def _():
        sum_ref[...] = jnp.sum(acc[...].T, axis=0, keepdims=True)


def main_call(group_size, stretch_lengths, query_later, mixed_in, residual, filter_rows):
    rows, width = residual.shape
    groups = width // group_size
    if len(filter_rows.shape) == 2:
        filter_spec = pl.BlockSpec(filter_rows.shape, lambda p, *_: (0, 0))
    else:
        filter_spec = pl.BlockSpec((filter_rows.shape[0], 16, STEP), lambda p, *_: (0, PACKED // 16 - 1, 0))
    block = pl.BlockSpec((rows, WIDE), lambda p, *_: (0, p))
    later = pl.BlockSpec((pl.Element(rows - 128), pl.Element(WIDE)), lambda p, *_: (128, p * WIDE))
    return pl.pallas_call(
        functools.partial(main_kernel, group_size),
        grid_spec=pltpu.PrefetchScalarGridSpec(
            num_scalar_prefetch=1,
            grid=(width // WIDE,),
            in_specs=[
                pl.BlockSpec((rows - 128, WIDE), lambda p, *_: (0, p)),
                block,
                later,
                filter_spec,
            ],
            out_specs=[
                later,
                pl.BlockSpec((1, rows - 128), lambda p, *_: (0, 0)),
                pl.BlockSpec((groups, WINDOW), lambda p, *_: (0, 0)),
            ],
            scratch_shapes=[
                pltpu.VMEM((rows - 128, LANES), F32),
            ],
        ),
        out_shape=[
            jax.ShapeDtypeStruct((rows, width), BF16),
            jax.ShapeDtypeStruct((1, rows - 128), F32),
            jax.ShapeDtypeStruct((groups, WINDOW), F32),
        ],
        compiler_params=params(),
        cost_estimate=cost(rows * width * 2 * WINDOW * 8, rows * width * 12),
        name="conv",
    )(stretch_lengths, query_later, mixed_in, residual, filter_rows)


def head_kernel(group_size, pred_ref, len_ref, held, query_ref, q_ref, k_ref, v_ref, u_ref, res_ref, taps_ref, lines_ref, kept_ref, mixed_ref, sum_ref, qs, ks, vs, acc):
    del kept_ref
    step = pl.program_id(0)
    per_lane = LANES // group_size
    device = lax.axis_index("seq")
    length = len_ref[device]
    follows = pred_ref[device] >= 0

    @pl.when(step == 0)
    def _():
        acc[...] = jnp.zeros_like(acc)

    def tiles():
        for number in range(HEAD_WIDE // LANES):
            index, tile = divmod(number, STEP // LANES)
            cols = slice(number * LANES, (number + 1) * LANES)
            here = slice(tile * LANES, (tile + 1) * LANES)
            qt, kt, vt = qs.at[number], ks.at[number], vs.at[number]
            prev = jnp.where(follows, held[index, 128:PACKED, here].astype(F32), 0.0)
            qt[0:8, :] = prev[0:8]
            kt[0:8, :] = prev[8:16]
            vt[0:8, :] = prev[16:24]
            qt[8:24, :] = q_ref[:, cols].astype(F32)
            kt[8:24, :] = k_ref[:, cols].astype(F32)
            vt[8:24, :] = v_ref[:, cols].astype(F32)
            first_query = short_conv(qt, taps_ref[0, :, cols].astype(F32), 0, 16)
            key = short_conv(kt, taps_ref[1, :, cols].astype(F32), 0, 16)
            value = short_conv(vt, taps_ref[2, :, cols].astype(F32), 0, 16)
            opening = (key * value).astype(BF16)
            state = held[index, 0:128, here]
            state = jnp.where(follows, state, jnp.zeros_like(state))
            pad = jnp.zeros((WINDOW - BLOCK - 128, LANES), BF16)
            extended = jnp.concatenate([pad, state, opening, u_ref[16:192, cols]])
            base = number * per_lane
            matrix = toeplitz(lines_ref[pl.ds(base, per_lane), :])
            parts = []
            for first in range(0, 128, SIDE * BLOCK):
                lows = range(first, first + SIDE * BLOCK, BLOCK)
                windows = [extended[low : low + WINDOW] for low in lows]
                result = jnp.dot(matrix, jnp.concatenate(windows, axis=1), preferred_element_type=F32)
                picked = pick_groups(result, group_size)
                parts.append((first, SIDE * BLOCK, unfold(picked)))
            edge = OPENING - 128
            edge_matrix = jnp.concatenate([matrix[g * BLOCK : g * BLOCK + edge] for g in range(per_lane)])
            edge_result = jnp.dot(edge_matrix, extended[128 : 128 + WINDOW], preferred_element_type=F32)
            parts.append((128, edge, pick_groups(edge_result, group_size, edge)))
            for first, rows, filtered in parts:
                query = query_ref[first : first + rows, cols]
                if first == 0:
                    query = jnp.concatenate([first_query, query[16:]])
                row = lax.broadcasted_iota(jnp.int32, (rows, LANES), 0) + first
                mixed = jnp.where(row < length, query * filtered, 0.0).astype(BF16)
                mixed_ref[first : first + rows, cols] = mixed
                summed = res_ref[first : first + rows, cols].astype(F32) + mixed.astype(F32)
                acc[first : first + rows, :] += summed * summed

    tiles()

    @pl.when(step == pl.num_programs(0) - 1)
    def _():
        sum_ref[...] = jnp.sum(acc[...].T, axis=0, keepdims=True)


def head_call(group_size, predecessor, stretch_lengths, previous, query_opening, queries, keys_in, values_in, mixed_in, residual, short_taps, lines, mixed):
    rows, width = queries.shape
    per_step = HEAD_WIDE // group_size
    block = pl.BlockSpec((OPENING, HEAD_WIDE), lambda p, *_: (0, p))
    small = pl.BlockSpec((16, HEAD_WIDE), lambda p, *_: (0, p))
    return pl.pallas_call(
        functools.partial(head_kernel, group_size),
        grid_spec=pltpu.PrefetchScalarGridSpec(
            num_scalar_prefetch=2,
            grid=(width // HEAD_WIDE,),
            in_specs=[
                pl.BlockSpec((HEAD_WIDE // STEP, PACKED, STEP), lambda p, *_: (p, 0, 0)),
                block,
                small,
                small,
                small,
                pl.BlockSpec((192, HEAD_WIDE), lambda p, *_: (0, p)),
                block,
                pl.BlockSpec((3, 7, HEAD_WIDE), lambda p, *_: (0, 0, p)),
                pl.BlockSpec((per_step, WINDOW), lambda p, *_: (p, 0)),
                pl.BlockSpec(memory_space=pl.ANY),
            ],
            out_specs=[block, pl.BlockSpec((1, 256), lambda p, *_: (0, 0))],
            scratch_shapes=[
                pltpu.VMEM((HEAD_WIDE // LANES, 24, LANES), F32),
                pltpu.VMEM((HEAD_WIDE // LANES, 24, LANES), F32),
                pltpu.VMEM((HEAD_WIDE // LANES, 24, LANES), F32),
                pltpu.VMEM((256, LANES), F32),
            ],
        ),
        out_shape=[
            jax.ShapeDtypeStruct((rows, width), BF16),
            jax.ShapeDtypeStruct((1, 256), F32),
        ],
        input_output_aliases={11: 0},
        compiler_params=params(),
        cost_estimate=cost(128 * width * 2 * WINDOW * 8, 128 * width * 12),
        name="head",
    )(predecessor, stretch_lengths, previous, query_opening, queries, keys_in, values_in, mixed_in, residual, short_taps, lines, mixed)


def norm_kernel(channels, first_block, sums, len_ref, *refs):
    sum_refs, (mixed_ref, res_ref, gain_ref), out_ref = refs[:sums], refs[sums : sums + 3], refs[-1]
    rows = mixed_ref.shape[0]
    first = (pl.program_id(0) + first_block) * rows
    length = len_ref[lax.axis_index("seq")]
    total = sum_refs[0][...]
    for ref in sum_refs[1:]:
        total = total + ref[...]
    scale = jnp.broadcast_to(lax.rsqrt(total / channels + EPSILON), (LANES, total.shape[1])).T[:rows]
    scale = jnp.where(lax.broadcasted_iota(jnp.int32, (rows, LANES), 0) + first < length, scale, 0.0)
    for lane in range(0, mixed_ref.shape[1], LANES):
        cols = slice(lane, lane + LANES)
        gain = gain_ref[:, cols].astype(F32)
        summed = res_ref[:, cols].astype(F32) + mixed_ref[:, cols].astype(F32)
        out_ref[:, cols] = (summed * scale * gain).astype(BF16)


def norm_call(channels, steps, first_block, stretch_lengths, totals, mixed, residual, gain, normed=None):
    rows, width = mixed.shape
    opening = first_block == 0
    size, lanes, skip = (OPENING, 256, 0) if opening else (128, 128, first_block - 1)
    block = pl.BlockSpec((size, width), lambda p, *_: (p + first_block, 0))
    operands = [*totals, mixed, residual, gain]
    in_specs = [pl.BlockSpec((1, lanes), lambda p, *_: (0, p + skip))] * len(totals)
    in_specs += [block, block, pl.BlockSpec((1, width), lambda p, *_: (0, 0))]
    aliases = {}
    if normed is not None:
        aliases = {len(operands) + 1: 0}
        operands.append(normed)
        in_specs.append(pl.BlockSpec(memory_space=pl.ANY))
    return pl.pallas_call(
        functools.partial(norm_kernel, channels, first_block, len(totals)),
        grid_spec=pltpu.PrefetchScalarGridSpec(
            num_scalar_prefetch=1, grid=(steps,), in_specs=in_specs, out_specs=block
        ),
        out_shape=jax.ShapeDtypeStruct((rows, width), BF16),
        input_output_aliases=aliases,
        compiler_params=params(),
        cost_estimate=cost(steps * size * width * 6, steps * size * width * 6),
        name="norm%d" % first_block,
    )(stretch_lengths, *operands)


def swap(array, axis, distance):
    size = lax.axis_size(axis)
    return lax.ppermute(array, axis, [(i, i ^ distance) for i in range(size)])


def exchange(pieces):
    return lax.all_to_all(pieces, "seq", split_axis=0, concat_axis=0, tiled=True)


def shares(squares):
    parts = lax.axis_size("mp")
    if parts != 4:
        return [lax.psum(squares, "mp")]
    return [squares] + [swap(squares, "mp", k) for k in range(1, parts)]


def body(queries, keys_in, values_in, residual, short_taps, mr_filter, norm_gain, predecessor, stretch_lengths):
    rows, width = queries.shape
    count = lax.axis_size("seq")
    channels = width * lax.axis_size("mp")
    group_size = width // mr_filter.shape[1]
    two_phase = width // STEP == count == 8 and mr_filter.shape == (16, LANES)
    gain = norm_gain.reshape(1, width)
    packed = tail_call(two_phase, queries, keys_in, values_in, short_taps, mr_filter)
    mixed_in, query_opening, query_later = feature_call(queries, keys_in, values_in, short_taps)
    if two_phase:
        received = exchange(packed)
        received, mixed_in, gain = lax.optimization_barrier((received, mixed_in, gain))
        routed, filter_rows = lax.optimization_barrier((route_call(predecessor, received), received))
        previous = exchange(routed)
    else:
        gathered = lax.all_gather(packed[None], "seq", axis=0, tiled=True)
        source = jnp.clip(predecessor[lax.axis_index("seq")], 0, count - 1)
        previous = lax.dynamic_index_in_dim(gathered, source, 0, keepdims=False)
        filter_rows = lax.all_gather(mr_filter, "seq", axis=0, tiled=True)
    mixed, squares, lines = main_call(
        group_size, stretch_lengths, query_later, mixed_in, residual, filter_rows
    )
    totals = shares(squares)
    early = rows // 128 - 2
    normed = norm_call(channels, early, 1, stretch_lengths, totals, mixed, residual, gain)
    previous, normed = lax.optimization_barrier((previous, normed))
    mixed, squares = head_call(
        group_size, predecessor, stretch_lengths, previous, query_opening, queries, keys_in, values_in,
        mixed_in, residual, short_taps, lines, mixed,
    )
    opening_totals = shares(squares)
    normed = norm_call(channels, 1, early + 1, stretch_lengths, totals, mixed, residual, gain, normed)
    normed = norm_call(channels, 1, 0, stretch_lengths, opening_totals, mixed, residual, gain, normed)
    return (mixed, normed)


def solution(mesh):
    in_specs = (
        P("seq", "mp"),
        P("seq", "mp"),
        P("seq", "mp"),
        P("seq", "mp"),
        P(None, None, "mp"),
        P("seq", "mp"),
        P("mp"),
        P(),
        P(),
    )
    out_specs = (P("seq", "mp"), P("seq", "mp"))
    return jax.shard_map(body, mesh=mesh, in_specs=in_specs, out_specs=out_specs, check_vma=False)
```

```python
import functools

import jax
import jax.numpy as jnp
from jax import lax
from jax.experimental import pallas as pl
from jax.experimental.pallas import tpu as pltpu
from jax.sharding import PartitionSpec as P

EPSILON = 1e-06
F32 = jnp.float32
BF16 = jnp.bfloat16
LANES = 128
STEP = 256
WIDE = 512
HEAD_WIDE = 1024
SIDE = 4
BLOCK = 32
WINDOW = 256
PACKED = 160
OPENING = 144
VMEM_LIMIT = 64 * 1024 * 1024


def params():
    return pltpu.CompilerParams(vmem_limit_bytes=VMEM_LIMIT)


def cost(flops, bytes_accessed):
    return pl.CostEstimate(flops=flops, bytes_accessed=bytes_accessed, transcendentals=0)


def short_conv(scratch, taps, start, rows):
    total = None
    for offset in range(taps.shape[0]):
        term = taps[offset : offset + 1] * scratch[pl.ds(start + 8 - offset, rows), :]
        total = term if total is None else total + term
    return total


def tail_kernel(packed, q_ref, k_ref, v_ref, kb_ref, vb_ref, taps_ref, filt_ref, out_ref, ks, vs):
    for slot in range(out_ref.shape[0]):
        lasts = []
        for tile in range(STEP // LANES):
            number = slot * (STEP // LANES) + tile
            cols = slice(number * LANES, (number + 1) * LANES)
            here = slice(tile * LANES, (tile + 1) * LANES)
            kt, vt = ks.at[number], vs.at[number]
            kt[0:16, :] = kb_ref[:, cols].astype(F32)
            vt[0:16, :] = vb_ref[:, cols].astype(F32)
            kt[16:144, :] = k_ref[:, cols].astype(F32)
            vt[16:144, :] = v_ref[:, cols].astype(F32)
            key_taps = taps_ref[1, :, cols].astype(F32)
            value_taps = taps_ref[2, :, cols].astype(F32)
            for row in range(0, 128, 64):
                key = short_conv(kt, key_taps, row + 8, 64)
                value = short_conv(vt, value_taps, row + 8, 64)
                out_ref[slot, row : row + 64, here] = (key * value).astype(BF16)
            last = [q_ref[:, cols].astype(F32)[8:], kt[136:144, :], vt[136:144, :]]
            if packed:
                last.append(filt_ref[...].astype(F32)[8 * tile : 8 * tile + 8])
            else:
                last.append(jnp.zeros((8, LANES), F32))
            lasts.append(jnp.concatenate(last))
        out_ref[slot, 128:PACKED, :] = jnp.concatenate(lasts, axis=1).astype(BF16)


def tail_call(packed, queries, keys_in, values_in, short_taps, mr_filter):
    rows, width = queries.shape
    slots = width // STEP
    part = width // 2
    count = part // LANES
    return pl.pallas_call(
        functools.partial(tail_kernel, packed),
        grid=(2,),
        in_specs=[
            pl.BlockSpec((16, part), lambda p: (rows // 16 - 1, p)),
            pl.BlockSpec((128, part), lambda p: (rows // 128 - 1, p)),
            pl.BlockSpec((128, part), lambda p: (rows // 128 - 1, p)),
            pl.BlockSpec((16, part), lambda p: (rows // 16 - 9, p)),
            pl.BlockSpec((16, part), lambda p: (rows // 16 - 9, p)),
            pl.BlockSpec((3, 7, part), lambda p: (0, 0, p)),
            pl.BlockSpec(mr_filter.shape, lambda p: (0, 0)),
        ],
        out_specs=pl.BlockSpec((slots // 2, PACKED, STEP), lambda p: (p, 0, 0)),
        out_shape=jax.ShapeDtypeStruct((slots, PACKED, STEP), BF16),
        scratch_shapes=[pltpu.VMEM((count, 144, LANES), F32)] * 2,
        compiler_params=params(),
        cost_estimate=cost(128 * width * 30, 128 * width * 6),
        name="tail",
    )(queries, keys_in, values_in, keys_in, values_in, short_taps, mr_filter)


def feature_kernel(q_ref, k_ref, v_ref, taps_ref, out_ref, opening_ref, later_ref, qs, ks, vs):
    rows = k_ref.shape[0]

    def pair(index, carry):
        for tile in range(2):
            cols = pl.ds(pl.multiple_of(index * 2 * LANES + tile * LANES, LANES), LANES)
            scratches = (qs.at[tile], ks.at[tile], vs.at[tile])
            taps = [taps_ref[i, :, cols].astype(F32) for i in range(3)]
            for scratch, ref in zip(scratches, (q_ref, k_ref, v_ref)):
                scratch[0:8, :] = jnp.zeros((8, LANES), F32)
                scratch[8 : rows + 8, :] = ref[:, cols].astype(F32)
            for row in range(0, rows, 64):
                query, key, value = [short_conv(x, t, row, 64) for x, t in zip(scratches, taps)]
                out_ref[row : row + 64, cols] = (key * value).astype(BF16)
                if row < OPENING:
                    count = min(64, OPENING - row)
                    opening_ref[row : row + count, cols] = query[:count]
                if row >= 128:
                    later_ref[row - 128 : row - 64, cols] = query
        return carry

    lax.fori_loop(0, k_ref.shape[1] // (2 * LANES), pair, 0)


def feature_call(queries, keys_in, values_in, short_taps):
    rows, width = keys_in.shape
    heights = (rows, OPENING, rows - 128)
    blocks = [pl.BlockSpec((height, WIDE), lambda p: (0, p)) for height in heights]
    scratch = pltpu.VMEM((2, rows + 8, LANES), F32)
    return pl.pallas_call(
        feature_kernel,
        grid=(width // WIDE,),
        in_specs=[blocks[0]] * 3 + [pl.BlockSpec((3, 7, WIDE), lambda p: (0, 0, p))],
        out_specs=blocks,
        out_shape=[
            jax.ShapeDtypeStruct((height, width), kind) for height, kind in zip(heights, (BF16, F32, F32))
        ],
        scratch_shapes=[scratch] * 3,
        compiler_params=params(),
        cost_estimate=cost(rows * width * 45, rows * width * 13),
        name="features",
    )(queries, keys_in, values_in, short_taps)


def route_kernel(pred_ref, in_ref, out_ref):
    for j in range(in_ref.shape[0]):
        out_ref[j] = in_ref[jnp.maximum(pred_ref[j], 0)]


def route_call(predecessor, received):
    return pl.pallas_call(
        route_kernel,
        in_specs=[pl.BlockSpec(memory_space=pltpu.SMEM), pl.BlockSpec(memory_space=pltpu.VMEM)],
        out_specs=pl.BlockSpec(memory_space=pltpu.VMEM),
        out_shape=jax.ShapeDtypeStruct(received.shape, BF16),
        compiler_params=params(),
        cost_estimate=cost(0, received.size * 4),
        name="route",
    )(predecessor, received)


def all_taps(filt_ref):
    if len(filt_ref.shape) == 2:
        return filt_ref[...]
    rows = []
    for j in range(filt_ref.shape[0]):
        last = filt_ref[j].astype(F32)[8:]
        rows += [last[:, :LANES], last[:, LANES:]]
    return jnp.concatenate(rows).astype(BF16)


def spread_taps(filter_rows):
    shape = (filter_rows.shape[0], WINDOW)
    tap = lax.broadcasted_iota(jnp.int32, shape, 0)
    place = lax.broadcasted_iota(jnp.int32, shape, 1)
    onehot = (place == WINDOW - BLOCK - tap).astype(BF16)
    return lax.dot_general(filter_rows, onehot, (((0,), (0,)), ((), ())), preferred_element_type=F32)


def toeplitz(lines):
    blocks = []
    for g in range(lines.shape[0]):
        line = jnp.broadcast_to(lines[g : g + 1], (BLOCK, WINDOW))
        blocks.append(pltpu.roll(line, 0, 1, stride=1, stride_axis=0).astype(BF16))
    return jnp.concatenate(blocks)


def pick_groups(result, group_size, rows=BLOCK):
    lane = lax.broadcasted_iota(jnp.int32, (rows, LANES), 1)
    later = [lane >= g * group_size for g in range(LANES // group_size)]
    blocks = []
    for first in range(0, result.shape[1], LANES):
        part = result[:, first : first + LANES]
        picked = part[:rows]
        for g in range(1, LANES // group_size):
            picked = jnp.where(later[g], part[g * rows : (g + 1) * rows], picked)
        blocks.append(picked)
    return jnp.concatenate(blocks) if len(blocks) > 1 else blocks[0]


def main_kernel(group_size, len_ref, query_ref, u_ref, res_ref, filt_ref, mixed_ref, sum_ref, lines_ref, acc):
    step = pl.program_id(0)
    rows = u_ref.shape[0]
    per_lane = LANES // group_size
    length = len_ref[lax.axis_index("seq")]

    @pl.when(step == 0)
    def _():
        lines_ref[...] = spread_taps(all_taps(filt_ref))
        acc[...] = jnp.zeros_like(acc)

    def tiles():
        for number in range(WIDE // LANES):
            cols = slice(number * LANES, (number + 1) * LANES)
            base = pl.multiple_of((step * (WIDE // LANES) + number) * per_lane, per_lane)
            matrix = toeplitz(lines_ref[pl.ds(base, per_lane), :])
            for start in range(128, rows, SIDE * BLOCK):
                windows = []
                for first in range(start, start + SIDE * BLOCK, BLOCK):
                    low = first + BLOCK - WINDOW
                    if low < 0:
                        windows.append(
                            jnp.concatenate([jnp.zeros((-low, LANES), BF16), u_ref[0 : first + BLOCK, cols]])
                        )
                    else:
                        windows.append(u_ref[low : first + BLOCK, cols])
                result = jnp.dot(matrix, jnp.concatenate(windows, axis=1), preferred_element_type=F32)
                picked = pick_groups(result, group_size)
                filtered = picked
                here = slice(start - 128, start - 128 + SIDE * BLOCK)
                row = lax.broadcasted_iota(jnp.int32, filtered.shape, 0) + start
                mixed = jnp.where(row < length, query_ref[here, cols] * filtered, 0.0).astype(BF16)
                mixed_ref[here, cols] = mixed
                summed = res_ref[here, cols].astype(F32) + mixed.astype(F32)
                acc[here, :] += summed * summed

    tiles()

    @pl.when(step == pl.num_programs(0) - 1)
    def _():
        sum_ref[...] = jnp.sum(acc[...].T, axis=0, keepdims=True)


def main_call(group_size, stretch_lengths, query_later, mixed_in, residual, filter_rows):
    rows, width = residual.shape
    groups = width // group_size
    if len(filter_rows.shape) == 2:
        filter_spec = pl.BlockSpec(filter_rows.shape, lambda p, *_: (0, 0))
    else:
        filter_spec = pl.BlockSpec((filter_rows.shape[0], 16, STEP), lambda p, *_: (0, PACKED // 16 - 1, 0))
    block = pl.BlockSpec((rows, WIDE), lambda p, *_: (0, p))
    later = pl.BlockSpec((pl.Element(rows - 128), pl.Element(WIDE)), lambda p, *_: (128, p * WIDE))
    return pl.pallas_call(
        functools.partial(main_kernel, group_size),
        grid_spec=pltpu.PrefetchScalarGridSpec(
            num_scalar_prefetch=1,
            grid=(width // WIDE,),
            in_specs=[
                pl.BlockSpec((rows - 128, WIDE), lambda p, *_: (0, p)),
                block,
                later,
                filter_spec,
            ],
            out_specs=[
                later,
                pl.BlockSpec((1, rows - 128), lambda p, *_: (0, 0)),
                pl.BlockSpec((groups, WINDOW), lambda p, *_: (0, 0)),
            ],
            scratch_shapes=[
                pltpu.VMEM((rows - 128, LANES), F32),
            ],
        ),
        out_shape=[
            jax.ShapeDtypeStruct((rows, width), BF16),
            jax.ShapeDtypeStruct((1, rows - 128), F32),
            jax.ShapeDtypeStruct((groups, WINDOW), F32),
        ],
        compiler_params=params(),
        cost_estimate=cost(rows * width * 2 * WINDOW * 8, rows * width * 12),
        name="conv",
    )(stretch_lengths, query_later, mixed_in, residual, filter_rows)


def head_kernel(group_size, pred_ref, len_ref, held, query_ref, q_ref, k_ref, v_ref, u_ref, res_ref, taps_ref, lines_ref, kept_ref, mixed_ref, sum_ref, qs, ks, vs, acc):
    del kept_ref
    step = pl.program_id(0)
    per_lane = LANES // group_size
    device = lax.axis_index("seq")
    length = len_ref[device]
    follows = pred_ref[device] >= 0

    @pl.when(step == 0)
    def _():
        acc[...] = jnp.zeros_like(acc)

    def tiles():
        for number in range(HEAD_WIDE // LANES):
            index, tile = divmod(number, STEP // LANES)
            cols = slice(number * LANES, (number + 1) * LANES)
            here = slice(tile * LANES, (tile + 1) * LANES)
            qt, kt, vt = qs.at[number], ks.at[number], vs.at[number]
            prev = jnp.where(follows, held[index, 128:PACKED, here].astype(F32), 0.0)
            qt[0:8, :] = prev[0:8]
            kt[0:8, :] = prev[8:16]
            vt[0:8, :] = prev[16:24]
            qt[8:24, :] = q_ref[:, cols].astype(F32)
            kt[8:24, :] = k_ref[:, cols].astype(F32)
            vt[8:24, :] = v_ref[:, cols].astype(F32)
            first_query = short_conv(qt, taps_ref[0, :, cols].astype(F32), 0, 16)
            key = short_conv(kt, taps_ref[1, :, cols].astype(F32), 0, 16)
            value = short_conv(vt, taps_ref[2, :, cols].astype(F32), 0, 16)
            opening = (key * value).astype(BF16)
            state = held[index, 0:128, here]
            state = jnp.where(follows, state, jnp.zeros_like(state))
            pad = jnp.zeros((WINDOW - BLOCK - 128, LANES), BF16)
            extended = jnp.concatenate([pad, state, opening, u_ref[16:192, cols]])
            base = number * per_lane
            matrix = toeplitz(lines_ref[pl.ds(base, per_lane), :])
            parts = []
            for first in range(0, 128, SIDE * BLOCK):
                lows = range(first, first + SIDE * BLOCK, BLOCK)
                windows = [extended[low : low + WINDOW] for low in lows]
                result = jnp.dot(matrix, jnp.concatenate(windows, axis=1), preferred_element_type=F32)
                picked = pick_groups(result, group_size)
                parts.append((first, SIDE * BLOCK, picked))
            edge = OPENING - 128
            edge_matrix = jnp.concatenate([matrix[g * BLOCK : g * BLOCK + edge] for g in range(per_lane)])
            edge_result = jnp.dot(edge_matrix, extended[128 : 128 + WINDOW], preferred_element_type=F32)
            parts.append((128, edge, pick_groups(edge_result, group_size, edge)))
            for first, rows, filtered in parts:
                query = query_ref[first : first + rows, cols]
                if first == 0:
                    query = jnp.concatenate([first_query, query[16:]])
                row = lax.broadcasted_iota(jnp.int32, (rows, LANES), 0) + first
                mixed = jnp.where(row < length, query * filtered, 0.0).astype(BF16)
                mixed_ref[first : first + rows, cols] = mixed
                summed = res_ref[first : first + rows, cols].astype(F32) + mixed.astype(F32)
                acc[first : first + rows, :] += summed * summed

    tiles()

    @pl.when(step == pl.num_programs(0) - 1)
    def _():
        sum_ref[...] = jnp.sum(acc[...].T, axis=0, keepdims=True)


def head_call(group_size, predecessor, stretch_lengths, previous, query_opening, queries, keys_in, values_in, mixed_in, residual, short_taps, lines, mixed):
    rows, width = queries.shape
    per_step = HEAD_WIDE // group_size
    block = pl.BlockSpec((OPENING, HEAD_WIDE), lambda p, *_: (0, p))
    small = pl.BlockSpec((16, HEAD_WIDE), lambda p, *_: (0, p))
    return pl.pallas_call(
        functools.partial(head_kernel, group_size),
        grid_spec=pltpu.PrefetchScalarGridSpec(
            num_scalar_prefetch=2,
            grid=(width // HEAD_WIDE,),
            in_specs=[
                pl.BlockSpec((HEAD_WIDE // STEP, PACKED, STEP), lambda p, *_: (p, 0, 0)),
                block,
                small,
                small,
                small,
                pl.BlockSpec((192, HEAD_WIDE), lambda p, *_: (0, p)),
                block,
                pl.BlockSpec((3, 7, HEAD_WIDE), lambda p, *_: (0, 0, p)),
                pl.BlockSpec((per_step, WINDOW), lambda p, *_: (p, 0)),
                pl.BlockSpec(memory_space=pl.ANY),
            ],
            out_specs=[block, pl.BlockSpec((1, 256), lambda p, *_: (0, 0))],
            scratch_shapes=[
                pltpu.VMEM((HEAD_WIDE // LANES, 24, LANES), F32),
                pltpu.VMEM((HEAD_WIDE // LANES, 24, LANES), F32),
                pltpu.VMEM((HEAD_WIDE // LANES, 24, LANES), F32),
                pltpu.VMEM((256, LANES), F32),
            ],
        ),
        out_shape=[
            jax.ShapeDtypeStruct((rows, width), BF16),
            jax.ShapeDtypeStruct((1, 256), F32),
        ],
        input_output_aliases={11: 0},
        compiler_params=params(),
        cost_estimate=cost(128 * width * 2 * WINDOW * 8, 128 * width * 12),
        name="head",
    )(predecessor, stretch_lengths, previous, query_opening, queries, keys_in, values_in, mixed_in, residual, short_taps, lines, mixed)


def norm_kernel(channels, first_block, sums, len_ref, *refs):
    sum_refs, (mixed_ref, res_ref, gain_ref), out_ref = refs[:sums], refs[sums : sums + 3], refs[-1]
    rows = mixed_ref.shape[0]
    first = (pl.program_id(0) + first_block) * rows
    length = len_ref[lax.axis_index("seq")]
    total = sum_refs[0][...]
    for ref in sum_refs[1:]:
        total = total + ref[...]
    scale = jnp.broadcast_to(lax.rsqrt(total / channels + EPSILON), (LANES, total.shape[1])).T[:rows]
    scale = jnp.where(lax.broadcasted_iota(jnp.int32, (rows, LANES), 0) + first < length, scale, 0.0)
    for lane in range(0, mixed_ref.shape[1], LANES):
        cols = slice(lane, lane + LANES)
        gain = gain_ref[:, cols].astype(F32)
        summed = res_ref[:, cols].astype(F32) + mixed_ref[:, cols].astype(F32)
        out_ref[:, cols] = (summed * scale * gain).astype(BF16)


def norm_call(channels, steps, first_block, stretch_lengths, totals, mixed, residual, gain, normed=None):
    rows, width = mixed.shape
    opening = first_block == 0
    size, lanes, skip = (OPENING, 256, 0) if opening else (128, 128, first_block - 1)
    block = pl.BlockSpec((size, width), lambda p, *_: (p + first_block, 0))
    operands = [*totals, mixed, residual, gain]
    in_specs = [pl.BlockSpec((1, lanes), lambda p, *_: (0, p + skip))] * len(totals)
    in_specs += [block, block, pl.BlockSpec((1, width), lambda p, *_: (0, 0))]
    aliases = {}
    if normed is not None:
        aliases = {len(operands) + 1: 0}
        operands.append(normed)
        in_specs.append(pl.BlockSpec(memory_space=pl.ANY))
    return pl.pallas_call(
        functools.partial(norm_kernel, channels, first_block, len(totals)),
        grid_spec=pltpu.PrefetchScalarGridSpec(
            num_scalar_prefetch=1, grid=(steps,), in_specs=in_specs, out_specs=block
        ),
        out_shape=jax.ShapeDtypeStruct((rows, width), BF16),
        input_output_aliases=aliases,
        compiler_params=params(),
        cost_estimate=cost(steps * size * width * 6, steps * size * width * 6),
        name="norm%d" % first_block,
    )(stretch_lengths, *operands)


def swap(array, axis, distance):
    size = lax.axis_size(axis)
    return lax.ppermute(array, axis, [(i, i ^ distance) for i in range(size)])


def exchange(pieces):
    return lax.all_to_all(pieces, "seq", split_axis=0, concat_axis=0, tiled=True)


def shares(squares):
    parts = lax.axis_size("mp")
    if parts != 4:
        return [lax.psum(squares, "mp")]
    return [squares] + [swap(squares, "mp", k) for k in range(1, parts)]


def body(queries, keys_in, values_in, residual, short_taps, mr_filter, norm_gain, predecessor, stretch_lengths):
    rows, width = queries.shape
    count = lax.axis_size("seq")
    channels = width * lax.axis_size("mp")
    group_size = width // mr_filter.shape[1]
    two_phase = width // STEP == count == 8 and mr_filter.shape == (16, LANES)
    gain = norm_gain.reshape(1, width)
    packed = tail_call(two_phase, queries, keys_in, values_in, short_taps, mr_filter)
    mixed_in, query_opening, query_later = feature_call(queries, keys_in, values_in, short_taps)
    if two_phase:
        received = exchange(packed)
        received, mixed_in, gain = lax.optimization_barrier((received, mixed_in, gain))
        routed, filter_rows = lax.optimization_barrier((route_call(predecessor, received), received))
        previous = exchange(routed)
    else:
        gathered = lax.all_gather(packed[None], "seq", axis=0, tiled=True)
        source = jnp.clip(predecessor[lax.axis_index("seq")], 0, count - 1)
        previous = lax.dynamic_index_in_dim(gathered, source, 0, keepdims=False)
        filter_rows = lax.all_gather(mr_filter, "seq", axis=0, tiled=True)
    mixed, squares, lines = main_call(
        group_size, stretch_lengths, query_later, mixed_in, residual, filter_rows
    )
    totals = shares(squares)
    early = rows // 128 - 2
    normed = norm_call(channels, early, 1, stretch_lengths, totals, mixed, residual, gain)
    previous, normed = lax.optimization_barrier((previous, normed))
    mixed, squares = head_call(
        group_size, predecessor, stretch_lengths, previous, query_opening, queries, keys_in, values_in,
        mixed_in, residual, short_taps, lines, mixed,
    )
    opening_totals = shares(squares)
    normed = norm_call(channels, 1, early + 1, stretch_lengths, totals, mixed, residual, gain, normed)
    normed = norm_call(channels, 1, 0, stretch_lengths, opening_totals, mixed, residual, gain, normed)
    return (mixed, normed)


def solution(mesh):
    in_specs = (
        P("seq", "mp"),
        P("seq", "mp"),
        P("seq", "mp"),
        P("seq", "mp"),
        P(None, None, "mp"),
        P("seq", "mp"),
        P("mp"),
        P(),
        P(),
    )
    out_specs = (P("seq", "mp"), P("seq", "mp"))
    return jax.shard_map(body, mesh=mesh, in_specs=in_specs, out_specs=out_specs, check_vma=False)
```
